128 devices in a mesh: group: 4 (over y), dev: 32 (over z, x, core).
Axes of the slice: x: 4, y: 4, z: 4, core: 2. Of those that a mesh axis runs over, the one named last changes fastest.
Arguments:
- source_points: bfloat16 [262144, 128], P(('group', 'dev')), may hold values from -20 to 20
- target_points: bfloat16 [262144, 128], P(('group', 'dev')), may hold values from -20 to 20
- source_logw: float32 [262144], P(('group', 'dev')), may hold values from -1 to 1
- target_logw: float32 [262144], P(('group', 'dev')), may hold values from -1 to 1
- pair_targets: int32 [512, 8], replicated, may hold values from 0 to 511, as said below
- pair_count: int32 [512], replicated, may hold values from 2 to 8, as said below
Outputs:
- source_potential: float32 [262144], P(('group', 'dev'))
- target_potential: float32 [262144], P(('group', 'dev'))
- mapped_points: float32 [262144, 128], P(('group', 'dev'))
The draws below stay inside these ranges and needn't reach their ends.
Inputs may be any that keep to these rules, and one draw needn't show every extreme that they name: `pair_targets`: slot 0 of row b names target block b. The names in the slots of one row are distinct. Target block t belongs to device t // 4 in the order of group then dev. Among all slots of the 4 rows of one device, the blocks named that belong to one other device are all the same block. A name outside the row's own group stands only in slot 1 and belongs to the device with the same index along dev. `pair_count`: some row uses all 8 slots.
All inputs are finite; a program needn't handle non-finite values.
Results may differ from the reference program's by a relative error of at most 0.0025.
Values may be sent and summed in bfloat16 or wider, within the bound.
A program may use at most 64 MiB of HBM per device.

```python
import math
import jax
import jax.numpy as jnp
from jax import lax

BLOCK = 512
EMB = 128
BLK_DEV = 4
SLOTS = 8
BLOCKS = 512
POINTS = 262144
N_GROUP = 4
N_DEV = 32


def cloud_values(key):
    key_vals, key_scale = jax.random.split(key)
    scales = jnp.exp(jax.random.uniform(key_scale, (POINTS, 1), jnp.float32, math.log(0.3), math.log(3.0)))
    values = jnp.clip(jax.random.normal(key_vals, (POINTS, EMB), jnp.float32), -4.5, 4.5)
    return values * scales


def draw_source_points(key, part):
    key = jax.random.fold_in(key, 1)
    values = cloud_values(key)
    return values.astype(jnp.bfloat16)


def draw_target_points(key, part):
    key = jax.random.fold_in(key, 2)
    values = cloud_values(key)
    return values.astype(jnp.bfloat16)


def pair_plan(key):
    folded = jax.random.fold_in(key, 577)
    key_choose, key_order, key_cross, key_away, key_heavy, key_level, key_forced = jax.random.split(folded, 7)
    devices = N_GROUP * N_DEV
    choose = jax.random.randint(key_choose, (devices, devices), 0, BLK_DEV)
    blocks = jnp.arange(BLOCKS, dtype=jnp.int32)
    src_dev = blocks // BLK_DEV
    group_id = src_dev // N_DEV
    lane_id = src_dev % N_DEV
    ranking = jax.random.randint(key_order, (BLOCKS, N_DEV - 1), 0, 1 << 20) * N_DEV + jnp.arange(N_DEV - 1, dtype=jnp.int32)[None, :]
    offsets = jnp.argsort(ranking, axis=1).astype(jnp.int32)[:, :SLOTS - 1] + 1
    peer_dev = (lane_id[:, None] + offsets) % N_DEV
    owners = group_id[:, None] * N_DEV + peer_dev
    crosses = jax.random.randint(key_cross, (BLOCKS,), 0, 4) == 0
    far_group = (group_id + 1 + jax.random.randint(key_away, (BLOCKS,), 0, N_GROUP - 1)) % N_GROUP
    owners = owners.at[:, 0].set(jnp.where(crosses, far_group * N_DEV + lane_id, owners[:, 0]))
    remote = owners * BLK_DEV + choose[src_dev[:, None], owners]
    targets = jnp.concatenate([blocks[:, None], remote], axis=1).astype(jnp.int32)
    heavy_dev = jax.random.randint(key_heavy, (devices,), 0, 4) == 0
    levels = jnp.where(heavy_dev, SLOTS, jax.random.randint(key_level, (devices,), 2, 5))
    counts = levels[src_dev]
    forced = jax.random.randint(key_forced, (), 0, BLOCKS)
    counts = counts.at[forced].set(SLOTS).astype(jnp.int32)
    return (targets, counts)


def draw_pair_targets(key, part):
    targets, counts = pair_plan(key)
    return targets


def draw_pair_count(key, part):
    targets, counts = pair_plan(key)
    return counts


def level_of(own_key, shape, cuts, smallest, largest):
    def one(axis_at, shards_of):
        draws = jax.random.uniform(jax.random.fold_in(jax.random.fold_in(own_key, 6), axis_at), (shards_of,), jnp.float32, smallest / len(cuts), largest / len(cuts))
        return jnp.repeat(jnp.exp(draws), shape[axis_at] // shards_of).reshape((-1,) + (1,) * (len(shape) - axis_at - 1))

    loudness = one(*cuts[0])
    for cut in cuts[1:]:
        loudness = loudness * one(*cut)
    return loudness


def setup_inputs(seed: int = 0) -> dict:
    splits = jax.random.split(jax.random.key(seed), 7)
    source_points = draw_source_points(jax.random.fold_in(splits[6], 71), 0)
    target_points = draw_target_points(jax.random.fold_in(splits[6], 71), 0)
    source_logw = jnp.clip(jax.random.uniform(splits[2], (POINTS,), jnp.float32, -1.0, 1.0) * level_of(splits[2], (POINTS,), ((0, 128),), -0.4, 0.0), -1.0, 1.0)
    target_logw = jnp.clip(jax.random.uniform(splits[3], (POINTS,), jnp.float32, -1.0, 1.0) * level_of(splits[3], (POINTS,), ((0, 128),), -0.4, 0.0), -1.0, 1.0)
    pair_targets = draw_pair_targets(jax.random.fold_in(splits[6], 71), 0)
    pair_count = draw_pair_count(jax.random.fold_in(splits[6], 71), 0)
    return {"source_points": source_points, "target_points": target_points, "source_logw": source_logw, "target_logw": target_logw, "pair_targets": pair_targets, "pair_count": pair_count}


NEG_FILL = -1e+30

def pair_scores(left, right, factor):
    return jnp.dot(left, right.T, preferred_element_type=jnp.float32) * factor

def row_pass(src_blocks, tgt_blocks, targets, active, dual_tab, factor):

    def per_block(blk_id):

        def advance(carry_in, slot_id):

            def include(state_in):
                row_high, row_sum = state_in
                target_id = targets[blk_id, slot_id]
                scores = pair_scores(src_blocks[blk_id], tgt_blocks[target_id], factor) + dual_tab[target_id][None, :]
                new_high = jnp.maximum(row_high, lax.optimization_barrier(jnp.max(scores, axis=1)))
                new_sum = row_sum * jnp.exp(row_high - new_high) + lax.optimization_barrier(jnp.sum(jnp.exp(scores - new_high[:, None]), axis=1))
                return (new_high, new_sum)
            return (lax.cond(active[blk_id, slot_id], include, lambda unchanged: unchanged, carry_in), None)
        start_state = (jnp.full((BLOCK,), NEG_FILL, jnp.float32), jnp.zeros((BLOCK,), jnp.float32))
        (row_high, row_sum), _ = lax.scan(advance, start_state, jnp.arange(SLOTS, dtype=jnp.int32))
        return row_high + jnp.log(row_sum)
    return lax.map(per_block, jnp.arange(BLOCKS, dtype=jnp.int32))

def column_pass(src_blocks, tgt_blocks, targets, active, potential, dual_tab, row_lse, factor, mapped):

    def advance(carry_in, pair_id):
        blk_id = pair_id // SLOTS
        slot_id = pair_id % SLOTS

        def include(state_in):
            col_max, col_sum = (state_in[0], state_in[1])
            target_id = targets[blk_id, slot_id]
            scores = pair_scores(src_blocks[blk_id], tgt_blocks[target_id], factor)
            shifted = scores + potential[blk_id][:, None]
            part_max = lax.optimization_barrier(jnp.max(shifted, axis=0))
            part_sum = lax.optimization_barrier(jnp.sum(jnp.exp(shifted - part_max[None, :]), axis=0))
            old_max = col_max[target_id]
            new_max = jnp.maximum(old_max, part_max)
            new_sum = col_sum[target_id] * jnp.exp(old_max - new_max) + part_sum * jnp.exp(part_max - new_max)
            col_max = col_max.at[target_id].set(new_max)
            col_sum = col_sum.at[target_id].set(new_sum)
            if mapped:
                plan = jnp.exp(scores + dual_tab[target_id][None, :] - row_lse[blk_id][:, None])
                numerator = state_in[2].at[blk_id].add(jnp.dot(plan.astype(jnp.bfloat16), tgt_blocks[target_id], preferred_element_type=jnp.float32))
                denominator = state_in[3].at[blk_id].add(lax.optimization_barrier(jnp.sum(plan, axis=1)))
                return (col_max, col_sum, numerator, denominator)
            return (col_max, col_sum)
        return (lax.cond(active[blk_id, slot_id], include, lambda unchanged: unchanged, carry_in), None)
    start_state = (jnp.full((BLOCKS, BLOCK), NEG_FILL, jnp.float32), jnp.zeros((BLOCKS, BLOCK), jnp.float32))
    if mapped:
        start_state = start_state + (jnp.zeros((BLOCKS, BLOCK, EMB), jnp.float32), jnp.zeros((BLOCKS, BLOCK), jnp.float32))
    result, _ = lax.scan(advance, start_state, jnp.arange(BLOCKS * SLOTS, dtype=jnp.int32))
    return result

def reference(source_points, target_points, source_logw, target_logw, pair_targets, pair_count):
    factor = 1.0 / math.sqrt(EMB)
    src_blocks = source_points.reshape(BLOCKS, BLOCK, EMB)
    tgt_blocks = target_points.reshape(BLOCKS, BLOCK, EMB)
    log_src = source_logw.reshape(BLOCKS, BLOCK)
    log_tgt = target_logw.reshape(BLOCKS, BLOCK)
    active = jnp.arange(SLOTS, dtype=jnp.int32)[None, :] < pair_count[:, None]
    zero_duals = jnp.zeros((BLOCKS, BLOCK), jnp.float32)
    row_lse1 = row_pass(src_blocks, tgt_blocks, pair_targets, active, zero_duals, factor)
    first_source = log_src - row_lse1
    col_max, col_sum = column_pass(src_blocks, tgt_blocks, pair_targets, active, first_source, None, None, factor, False)
    first_target = log_tgt - (col_max + jnp.log(col_sum))
    row_lse2 = row_pass(src_blocks, tgt_blocks, pair_targets, active, first_target, factor)
    source_potential = log_src - row_lse2
    col_max, col_sum, numerator, denominator = column_pass(src_blocks, tgt_blocks, pair_targets, active, source_potential, first_target, row_lse2, factor, True)
    target_potential = log_tgt - (col_max + jnp.log(col_sum))
    mapped_points = numerator / denominator[:, :, None]
    return (source_potential.reshape(POINTS), target_potential.reshape(POINTS), mapped_points.reshape(POINTS, EMB))
```

```python
import functools
import math

import jax
import jax.numpy as jnp
from jax import lax
from jax.experimental import pallas as pl
from jax.experimental.pallas import tpu as pltpu
from jax.sharding import PartitionSpec as P

BLOCK = 512
EMB = 128
BLK_DEV = 4
SLOTS = 8
LANES = 128
NEG_FILL = -1e30
LOG2E = math.log2(math.e)
ROW_LOW, ROW_HIGH, COL_LOW = 1e-6, 1e30, 1e-22
MESH = pl.DeviceIdType.MESH
VMEM_LIMIT = 48 * 2**20


def requests(targets, counts, owner_self, skipped, blk_count):
    slot_count = targets.shape[2]
    active = jnp.arange(slot_count, dtype=jnp.int32)[None, None, :] < counts[:, :, None]
    match = active & (targets // blk_count == owner_self) & jnp.logical_not(skipped)[:, None, None]
    return jnp.max(jnp.where(match, targets % blk_count, -1), axis=(1, 2))


def raw_scores(left, right):
    return lax.dot_general(left, right, (((1,), (1,)), ((), ())), preferred_element_type=jnp.float32)


def as_columns(row):
    return jnp.transpose(jnp.broadcast_to(row, (LANES, row.shape[1])))


def as_row(columns):
    return jnp.transpose(columns)[0:1]


def weight_rows(weights):
    high = weights.astype(jnp.bfloat16).astype(jnp.float32)
    rest = weights - high
    middle = rest.astype(jnp.bfloat16).astype(jnp.float32)
    low = rest - middle
    at = lax.broadcasted_iota(jnp.int32, (16, weights.shape[1]), 0)
    zero = jnp.zeros((16, weights.shape[1]), jnp.float32)
    rows = jnp.where(at == 0, high, jnp.where(at == 1, middle, jnp.where(at == 2, low, zero)))
    return rows.astype(jnp.bfloat16)


def fetch_all(pos_ref, cnt_ref, loc_ref, dev_ref, grp_ref, held, sems):
    blocks, slots = BLK_DEV, SLOTS
    dev_count = dev_ref.shape[0]

    @pl.loop(0, blocks * slots)
    def _(at):
        position = pos_ref[at]
        active = lax.rem(at, slots) < cnt_ref[at // slots]

        @pl.when(active & (position < blocks))
        def _():
            pltpu.make_async_copy(loc_ref.at[position], held.at[at], sems.at[at]).start()

        @pl.when(active & (position >= blocks) & (position < blocks + dev_count))
        def _():
            pltpu.make_async_copy(dev_ref.at[position - blocks], held.at[at], sems.at[at]).start()

        @pl.when(active & (position >= blocks + dev_count))
        def _():
            pltpu.make_async_copy(
                grp_ref.at[position - blocks - dev_count], held.at[at], sems.at[at]
            ).start()


def first_kernel(
    pos_ref, cnt_ref, src_ref, logw_ref, loc_ref, dev_ref, grp_ref,
    fs_ref, part_ref,
    held, kept, row_acc, col_max, col_sum, tab_max, tab_sum, col_tmp, sems,
):
    factor = 1.0 / math.sqrt(EMB)
    scale = factor * LOG2E
    rows = src_ref.shape[1]
    fetch_all(pos_ref, cnt_ref, loc_ref, dev_ref, grp_ref, held, sems)
    tab_max[...] = jnp.full_like(tab_max, NEG_FILL)
    tab_sum[...] = jnp.zeros_like(tab_sum)

    @pl.loop(0, BLK_DEV)
    def _(blk):
        count = cnt_ref[blk]
        row_acc[...] = jnp.zeros_like(row_acc)
        col_max[...] = jnp.zeros_like(col_max)
        col_sum[...] = jnp.ones_like(col_sum)

        @pl.loop(0, count)
        def _(slot):
            at = blk * SLOTS + slot
            pltpu.make_async_copy(loc_ref.at[0], held.at[at], sems.at[at]).wait()
            for part in range(rows // LANES):
                span = pl.ds(part * LANES, LANES)
                kern = jnp.exp2(raw_scores(src_ref[blk, span, :], held[at]) * scale)
                total = kern[:, :LANES]
                for lane in range(1, rows // LANES):
                    total = total + kern[:, lane * LANES : (lane + 1) * LANES]
                row_acc[span, :] += total
                kept[slot, span, :] = kern.astype(jnp.bfloat16)

        row_sum = lax.dot_general(
            jnp.ones((8, LANES), jnp.float32),
            row_acc[...],
            (((1,), (1,)), ((), ())),
            precision=lax.Precision.HIGHEST,
            preferred_element_type=jnp.float32,
        )[0:1]
        logw = logw_ref[blk]
        fs_ref[blk] = logw - jnp.log(row_sum)
        weights = weight_rows(jnp.exp(logw) / row_sum)

        @pl.loop(0, count)
        def _(slot):
            col_sum[slot] = jnp.sum(
                jnp.dot(weights, kept[slot], preferred_element_type=jnp.float32),
                axis=0,
                keepdims=True,
            )

        row_fine = (row_sum >= ROW_LOW) & (row_sum <= ROW_HIGH)
        fine = jnp.min(jnp.where(row_fine, 1.0, 0.0))
        col_fine = jnp.where(col_sum[...] >= COL_LOW, 1.0, 0.0)
        fine = jnp.minimum(fine, jnp.min(jnp.min(col_fine, axis=0)))

        @pl.when(fine < 0.5)
        def _():
            row_acc[...] = jnp.full_like(row_acc, NEG_FILL)
            col_tmp[...] = jnp.zeros_like(col_tmp)

            @pl.loop(0, count)
            def _(slot):
                at = blk * SLOTS + slot
                for part in range(rows // LANES):
                    span = pl.ds(part * LANES, LANES)
                    scores = raw_scores(src_ref[blk, span, :], held[at]) * factor
                    old = row_acc[span, :]
                    new = jnp.maximum(old, jnp.max(scores, axis=1, keepdims=True))
                    here = jnp.sum(jnp.exp(scores - new[:, 0:1]), axis=1, keepdims=True)
                    col_tmp[span, :] = col_tmp[span, :] * jnp.exp(old - new) + here
                    row_acc[span, :] = new

            source = as_columns(logw_ref[blk]) - (row_acc[...] + jnp.log(col_tmp[...]))
            row_acc[...] = source
            fs_ref[blk] = as_row(source)

            @pl.loop(0, count)
            def _(slot):
                at = blk * SLOTS + slot
                high = jnp.full((1, rows), NEG_FILL, jnp.float32)
                total = jnp.zeros((1, rows), jnp.float32)
                for part in range(rows // LANES):
                    span = pl.ds(part * LANES, LANES)
                    scores = raw_scores(src_ref[blk, span, :], held[at]) * factor
                    scores = scores + row_acc[span, 0:1]
                    new = jnp.maximum(high, jnp.max(scores, axis=0, keepdims=True))
                    total = total * jnp.exp(high - new) + jnp.sum(
                        jnp.exp(scores - new), axis=0, keepdims=True
                    )
                    high = new
                col_max[slot] = high
                col_sum[slot] = total

        @pl.loop(0, count)
        def _(slot):
            position = pos_ref[blk * SLOTS + slot]
            old = tab_max[position]
            high = col_max[slot]
            new = jnp.maximum(old, high)
            tab_sum[position] = tab_sum[position] * jnp.exp(old - new) + col_sum[slot] * jnp.exp(
                high - new
            )
            tab_max[position] = new

    sums = tab_sum[...]
    used = sums > 0.0
    part_ref[...] = jnp.where(
        used, tab_max[...] + jnp.log(jnp.where(used, sums, 1.0)), NEG_FILL
    )


def second_kernel(
    pos_ref, cnt_ref, src_ref, logw_ref, fs_ref, dual_ref, loc_ref, dev_ref, grp_ref,
    pot_ref, map_ref, sum_ref,
    held, kept, fs_col, acc, sems,
):
    scale = LOG2E / math.sqrt(EMB)
    rows = src_ref.shape[1]
    fetch_all(pos_ref, cnt_ref, loc_ref, dev_ref, grp_ref, held, sems)
    sum_ref[...] = jnp.zeros_like(sum_ref)

    @pl.loop(0, BLK_DEV)
    def _(blk):
        count = cnt_ref[blk]
        first_source = fs_ref[blk]
        fs_col[...] = as_columns(first_source * LOG2E)
        acc[...] = jnp.zeros_like(acc)

        @pl.loop(0, count)
        def _(slot):
            at = blk * SLOTS + slot
            pltpu.make_async_copy(loc_ref.at[0], held.at[at], sems.at[at]).wait()
            dual = dual_ref[pos_ref[at]] * LOG2E
            points = held[at]
            beside = jnp.concatenate([points, jnp.ones((rows, LANES), jnp.bfloat16)], axis=1)
            for part in range(rows // LANES):
                span = pl.ds(part * LANES, LANES)
                col = fs_col[span, :]
                shift = jnp.concatenate([col] * (rows // LANES), axis=1)
                plan = jnp.exp2(raw_scores(src_ref[blk, span, :], points) * scale + (dual + shift))
                plan = plan.astype(jnp.bfloat16)
                kept[slot, span, :] = plan
                acc[span, :] += jnp.dot(plan, beside, preferred_element_type=jnp.float32)

        row_col = acc[:, LANES:]
        map_ref[blk] = acc[:, :LANES] / row_col
        row_sum = as_row(row_col)
        logw = logw_ref[blk]
        pot_ref[blk] = logw + first_source - jnp.log(row_sum)
        weights = weight_rows(jnp.exp(logw) / row_sum)

        @pl.loop(0, count)
        def _(slot):
            position = pos_ref[blk * SLOTS + slot]
            sum_ref[position] += jnp.sum(
                jnp.dot(weights, kept[slot], preferred_element_type=jnp.float32),
                axis=0,
                keepdims=True,
            )


def greet(dev_count, group_count, me_dev, me_group):
    barrier = pltpu.get_barrier_semaphore()

    def to_dev(step, carry):
        peer = lax.rem(me_dev + step, dev_count)
        pl.semaphore_signal(barrier, inc=1, device_id=(me_group, peer), device_id_type=MESH)
        return carry

    def to_group(step, carry):
        peer = lax.rem(me_group + step, group_count)
        pl.semaphore_signal(barrier, inc=1, device_id=(peer, me_dev), device_id_type=MESH)
        return carry

    lax.fori_loop(1, dev_count, to_dev, 0)
    lax.fori_loop(1, group_count, to_group, 0)
    pl.semaphore_wait(barrier, dev_count + group_count - 2)


def exchange(
    out_ref, out_base, in_ref, in_base, send_sem, recv_sem, dev_count, group_count, me_dev, me_group
):
    def to_dev(step):
        peer = lax.rem(me_dev + step, dev_count)
        return pltpu.make_async_remote_copy(
            src_ref=out_ref.at[out_base + peer],
            dst_ref=in_ref.at[in_base + me_dev],
            send_sem=send_sem.at[step],
            recv_sem=recv_sem.at[step],
            device_id=(me_group, peer),
            device_id_type=MESH,
        )

    def to_group(step):
        peer = lax.rem(me_group + step, group_count)
        return pltpu.make_async_remote_copy(
            src_ref=out_ref.at[out_base + dev_count + peer],
            dst_ref=in_ref.at[in_base + dev_count + me_group],
            send_sem=send_sem.at[dev_count + step],
            recv_sem=recv_sem.at[dev_count + step],
            device_id=(peer, me_dev),
            device_id_type=MESH,
        )

    def start(copy_of):
        def body(step, carry):
            copy_of(step).start()
            return carry

        return body

    def wait(copy_of):
        def body(step, carry):
            copy_of(step).wait()
            return carry

        return body

    lax.fori_loop(1, dev_count, start(to_dev), 0)
    lax.fori_loop(1, group_count, start(to_group), 0)
    lax.fori_loop(1, dev_count, wait(to_dev), 0)
    lax.fori_loop(1, group_count, wait(to_group), 0)


def settle_kernel(
    dev_count, group_count, pick_ref, part_ref, logw_ref, dual_ref,
    inbox, outbox, send_a, recv_a, send_b, recv_b,
):
    me_group, me_dev = lax.axis_index("group"), lax.axis_index("dev")
    blocks = BLK_DEV
    peers = dev_count + group_count
    empty = jnp.full(inbox.shape[1:], NEG_FILL, jnp.float32)
    greet(dev_count, group_count, me_dev, me_group)
    inbox[me_dev] = empty
    inbox[dev_count + me_group] = empty
    exchange(
        part_ref, blocks, inbox, 0, send_a, recv_a, dev_count, group_count, me_dev, me_group
    )
    own = [part_ref[q] for q in range(blocks)]

    def highest(e, carry):
        pick, here = pick_ref[e], inbox[e]
        return tuple(
            jnp.maximum(high, jnp.where(pick == q, here, NEG_FILL)) for q, high in enumerate(carry)
        )

    highs = lax.fori_loop(0, peers, highest, tuple(own))

    def summed(e, carry):
        pick, here = pick_ref[e], inbox[e]
        return tuple(
            total + jnp.exp(jnp.where(pick == q, here, NEG_FILL) - highs[q])
            for q, total in enumerate(carry)
        )

    totals = lax.fori_loop(
        0, peers, summed, tuple(jnp.exp(o - h) for o, h in zip(own, highs))
    )
    duals = [
        logw_ref[q] - (highs[q] + jnp.log(totals[q])) for q in range(blocks)
    ]
    for q in range(blocks):
        dual_ref[q] = duals[q]

    def fill(e, carry):
        pick = pick_ref[e]
        chosen = jnp.zeros_like(duals[0])
        for q in range(blocks):
            chosen = jnp.where(pick == q, duals[q], chosen)
        outbox[e] = chosen
        return carry

    lax.fori_loop(0, peers, fill, 0)
    dual_ref[blocks + me_dev] = jnp.zeros_like(duals[0])
    dual_ref[blocks + dev_count + me_group] = jnp.zeros_like(duals[0])
    exchange(
        outbox, 0, dual_ref, blocks, send_b, recv_b, dev_count, group_count, me_dev, me_group
    )


def close_kernel(
    dev_count, group_count, pick_ref, sum_ref, logw_ref, first_ref, pot_ref, inbox, send_a, recv_a
):
    me_group, me_dev = lax.axis_index("group"), lax.axis_index("dev")
    blocks = BLK_DEV
    peers = dev_count + group_count
    greet(dev_count, group_count, me_dev, me_group)
    inbox[me_dev] = jnp.zeros(inbox.shape[1:], jnp.float32)
    inbox[dev_count + me_group] = jnp.zeros(inbox.shape[1:], jnp.float32)
    exchange(
        sum_ref, blocks, inbox, 0, send_a, recv_a, dev_count, group_count, me_dev, me_group
    )

    def summed(e, carry):
        pick, here = pick_ref[e], inbox[e]
        return tuple(
            total + jnp.where(pick == q, here, 0.0) for q, total in enumerate(carry)
        )

    totals = lax.fori_loop(0, peers, summed, tuple(sum_ref[q] for q in range(blocks)))
    for q in range(blocks):
        pot_ref[q] = logw_ref[q] - jnp.log(totals[q]) + first_ref[q]


def shards(source_points, target_points, source_logw, target_logw, pair_targets, pair_count):
    group_count = lax.axis_size("group")
    dev_count = lax.axis_size("dev")
    group_idx = lax.axis_index("group")
    dev_idx = lax.axis_index("dev")
    myself = group_idx * dev_count + dev_idx
    blocks, rows, slots = BLK_DEV, BLOCK, SLOTS
    table = blocks + dev_count + group_count
    peers = dev_count + group_count
    sources = source_points.reshape(blocks, rows, EMB)
    targets = target_points.reshape(blocks, rows, EMB)
    log_src = source_logw.reshape(blocks, 1, rows)
    log_tgt = target_logw.reshape(blocks, rows // LANES, LANES)

    own_targets = lax.dynamic_slice_in_dim(pair_targets, myself * blocks, blocks, 0)
    own_counts = lax.dynamic_slice_in_dim(pair_count, myself * blocks, blocks, 0)
    owners = own_targets // blocks
    position = jnp.where(
        owners == myself,
        own_targets % blocks,
        jnp.where(
            owners // dev_count == group_idx,
            blocks + owners % dev_count,
            blocks + dev_count + owners // dev_count,
        ),
    ).reshape(blocks * slots)
    everything = pair_targets.reshape(group_count, dev_count, blocks, slots)
    counts_all = pair_count.reshape(group_count, dev_count, blocks)
    pick_dev = requests(
        lax.dynamic_index_in_dim(everything, group_idx, 0, keepdims=False),
        lax.dynamic_index_in_dim(counts_all, group_idx, 0, keepdims=False),
        myself,
        jnp.arange(dev_count, dtype=jnp.int32) == dev_idx,
        blocks,
    )
    pick_grp = requests(
        lax.dynamic_index_in_dim(everything, dev_idx, 1, keepdims=False),
        lax.dynamic_index_in_dim(counts_all, dev_idx, 1, keepdims=False),
        myself,
        jnp.arange(group_count, dtype=jnp.int32) == group_idx,
        blocks,
    )
    pick = jnp.concatenate([pick_dev, pick_grp])
    dev_rows = lax.all_to_all(
        jnp.take(targets, jnp.maximum(pick_dev, 0), axis=0), "dev", 0, 0, tiled=True
    )
    grp_rows = lax.all_to_all(
        jnp.take(targets, jnp.maximum(pick_grp, 0), axis=0), "group", 0, 0, tiled=True
    )

    smem = pl.BlockSpec(memory_space=pltpu.SMEM)
    vmem = pl.BlockSpec(memory_space=pltpu.VMEM)
    anywhere = pl.BlockSpec(memory_space=pl.ANY)
    f32 = jnp.float32
    held = pltpu.VMEM((blocks * slots, rows, EMB), jnp.bfloat16)
    kept = pltpu.VMEM((slots, rows, rows), jnp.bfloat16)
    copy_sems = pltpu.SemaphoreType.DMA((blocks * slots,))
    pairs = blocks * slots

    first_source, part = pl.pallas_call(
        first_kernel,
        out_shape=(
            jax.ShapeDtypeStruct((blocks, 1, rows), f32),
            jax.ShapeDtypeStruct((table, 1, rows), f32),
        ),
        in_specs=[smem, smem, vmem, vmem, anywhere, anywhere, anywhere],
        out_specs=(vmem, vmem),
        scratch_shapes=[
            held,
            kept,
            pltpu.VMEM((rows, LANES), f32),
            pltpu.VMEM((slots, 1, rows), f32),
            pltpu.VMEM((slots, 1, rows), f32),
            pltpu.VMEM((table, 1, rows), f32),
            pltpu.VMEM((table, 1, rows), f32),
            pltpu.VMEM((rows, LANES), f32),
            copy_sems,
        ],
        compiler_params=pltpu.CompilerParams(vmem_limit_bytes=VMEM_LIMIT),
        cost_estimate=pl.CostEstimate(
            flops=4 * pairs * rows * rows * EMB, bytes_accessed=6 * 2**20, transcendentals=pairs * rows * rows
        ),
        name="first_pass",
    )(position, own_counts, sources, log_src, targets, dev_rows, grp_rows)

    small = (rows // LANES, LANES)
    sems = pltpu.SemaphoreType.DMA((peers,))
    dual = pl.pallas_call(
        functools.partial(settle_kernel, dev_count, group_count),
        out_shape=jax.ShapeDtypeStruct((table, *small), f32),
        in_specs=[smem, vmem, vmem],
        out_specs=vmem,
        scratch_shapes=[
            pltpu.VMEM((peers, *small), f32),
            pltpu.VMEM((peers, *small), f32),
            sems,
            sems,
            sems,
            sems,
        ],
        compiler_params=pltpu.CompilerParams(collective_id=0, has_side_effects=True),
        name="settle_first",
    )(pick, part.reshape(table, *small), log_tgt)

    potential, mapped, col_sums = pl.pallas_call(
        second_kernel,
        out_shape=(
            jax.ShapeDtypeStruct((blocks, 1, rows), f32),
            jax.ShapeDtypeStruct((blocks, rows, EMB), f32),
            jax.ShapeDtypeStruct((table, 1, rows), f32),
        ),
        in_specs=[smem, smem, vmem, vmem, vmem, vmem, anywhere, anywhere, anywhere],
        out_specs=(vmem, vmem, vmem),
        scratch_shapes=[
            held,
            kept,
            pltpu.VMEM((rows, LANES), f32),
            pltpu.VMEM((rows, 2 * LANES), f32),
            copy_sems,
        ],
        compiler_params=pltpu.CompilerParams(vmem_limit_bytes=VMEM_LIMIT),
        cost_estimate=pl.CostEstimate(
            flops=8 * pairs * rows * rows * EMB, bytes_accessed=7 * 2**20, transcendentals=pairs * rows * rows
        ),
        name="second_pass",
    )(
        position, own_counts, sources, log_src, first_source,
        dual.reshape(table, 1, rows), targets, dev_rows, grp_rows,
    )

    target_potential = pl.pallas_call(
        functools.partial(close_kernel, dev_count, group_count),
        out_shape=jax.ShapeDtypeStruct((blocks, *small), f32),
        in_specs=[smem, vmem, vmem, vmem],
        out_specs=vmem,
        scratch_shapes=[pltpu.VMEM((peers, *small), f32), sems, sems],
        compiler_params=pltpu.CompilerParams(collective_id=1, has_side_effects=True),
        name="settle_second",
    )(pick, col_sums.reshape(table, *small), log_tgt, dual)
    return (
        potential.reshape(blocks * rows),
        target_potential.reshape(blocks * rows),
        mapped.reshape(blocks * rows, EMB),
    )


def solution(mesh):
    return jax.shard_map(
        shards,
        mesh=mesh,
        in_specs=(
            P(("group", "dev"), None),
            P(("group", "dev"), None),
            P(("group", "dev")),
            P(("group", "dev")),
            P(),
            P(),
        ),
        out_specs=(P(("group", "dev")), P(("group", "dev")), P(("group", "dev"), None)),
        check_vma=False,
    )
```

```python
import functools
import math

import jax
import jax.numpy as jnp
from jax import lax
from jax.experimental import pallas as pl
from jax.experimental.pallas import tpu as pltpu
from jax.sharding import PartitionSpec as P

BLOCK = 512
EMB = 128
BLK_DEV = 4
SLOTS = 8
LANES = 128
NEG_FILL = -1e30
LOG2E = math.log2(math.e)
ROW_LOW, ROW_HIGH, COL_LOW = 1e-6, 1e30, 1e-22
MESH = pl.DeviceIdType.MESH
VMEM_LIMIT = 48 * 2**20


RING = 4
TRUNK = (0, 3, 1, 2)
BRANCH = ((2, 0), (2, 1), (1, 0), (1, 1), (3, 0), (3, 1))


def chosen_blocks(targets, counts, first, sources):
    takers, blocks, slots = targets.shape
    active = jnp.arange(slots, dtype=jnp.int32) < counts[:, :, None]
    named = jnp.where(active, targets - first, -1).reshape(takers, blocks * slots, 1)
    match = (named >= 0) & (named // blocks == sources)
    return jnp.max(jnp.where(match, named % blocks, -1), axis=1)


def raw_scores(left, right):
    return lax.dot_general(left, right, (((1,), (1,)), ((), ())), preferred_element_type=jnp.float32)


def as_columns(row):
    return jnp.transpose(jnp.broadcast_to(row, (LANES, row.shape[1])))


def as_row(columns):
    return jnp.transpose(columns)[0:1]


def weight_rows(weights):
    high = weights.astype(jnp.bfloat16).astype(jnp.float32)
    rest = weights - high
    middle = rest.astype(jnp.bfloat16).astype(jnp.float32)
    low = rest - middle
    at = lax.broadcasted_iota(jnp.int32, (16, weights.shape[1]), 0)
    zero = jnp.zeros((16, weights.shape[1]), jnp.float32)
    rows = jnp.where(at == 0, high, jnp.where(at == 1, middle, jnp.where(at == 2, low, zero)))
    return rows.astype(jnp.bfloat16)


def fetch_all(pos_ref, cnt_ref, loc_ref, tab_ref, held, sems, clear):
    @pl.loop(0, BLK_DEV * SLOTS)
    def _(at):
        position = pos_ref[at]
        active = lax.rem(at, SLOTS) < cnt_ref[at // SLOTS]

        @pl.when(active & (position < BLK_DEV))
        def _():
            pltpu.make_async_copy(loc_ref.at[position], held.at[at], sems.at[at]).start()

        @pl.when(active & (position >= BLK_DEV))
        def _():
            pltpu.make_async_copy(tab_ref.at[position], held.at[at], sems.at[at]).start()

        if clear:

            @pl.when(jnp.logical_not(active))
            def _():
                held[at] = jnp.zeros(held.shape[1:], held.dtype)


def await_blocks(blk, count, loc_ref, held, sems):
    @pl.loop(0, count)
    def _(slot):
        at = blk * SLOTS + slot
        pltpu.make_async_copy(loc_ref.at[0], held.at[at], sems.at[at]).wait()


def by_width(count, work):
    @pl.when(count <= SLOTS // 2)
    def _():
        work(SLOTS // 2)

    @pl.when(count > SLOTS // 2)
    def _():
        work(SLOTS)


def column_sums(weights, kept, slot):
    return jnp.sum(
        jnp.dot(weights, kept[slot], preferred_element_type=jnp.float32), axis=0, keepdims=True
    )


def first_kernel(
    pos_ref, cnt_ref, src_ref, logw_ref, loc_ref, tab_ref,
    fs_ref, part_ref,
    held, kept, row_acc, col_max, col_sum, tab_max, tab_sum, col_tmp, sems,
):
    factor = 1.0 / math.sqrt(EMB)
    scale = factor * LOG2E
    rows = src_ref.shape[1]
    fetch_all(pos_ref, cnt_ref, loc_ref, tab_ref, held, sems, False)
    tab_max[...] = jnp.full_like(tab_max, NEG_FILL)
    tab_sum[...] = jnp.zeros_like(tab_sum)

    @pl.loop(0, BLK_DEV)
    def _(blk):
        count = cnt_ref[blk]
        await_blocks(blk, count, loc_ref, held, sems)
        col_max[...] = jnp.zeros_like(col_max)

        def row_work(width):
            totals = jnp.zeros_like(row_acc)
            for slot in range(width):
                kern = jnp.exp2(raw_scores(src_ref[blk], held[blk * SLOTS + slot]) * scale)
                kept[slot] = kern.astype(jnp.bfloat16)
                total = kern[:, :LANES]
                for lane in range(1, rows // LANES):
                    total = total + kern[:, lane * LANES : (lane + 1) * LANES]
                totals = totals + jnp.where(slot < count, total, 0.0)
            row_acc[...] = totals

        by_width(count, row_work)
        row_sum = lax.dot_general(
            jnp.ones((8, LANES), jnp.float32),
            row_acc[...],
            (((1,), (1,)), ((), ())),
            precision=lax.Precision.HIGHEST,
            preferred_element_type=jnp.float32,
        )[0:1]
        logw = logw_ref[blk]
        fs_ref[blk] = logw - jnp.log(row_sum)
        weights = weight_rows(jnp.exp(logw) / row_sum)

        def column_work(width):
            for slot in range(width):
                col_sum[slot] = column_sums(weights, kept, slot)

        by_width(count, column_work)
        row_fine = (row_sum >= ROW_LOW) & (row_sum <= ROW_HIGH)
        slot_at = lax.broadcasted_iota(jnp.int32, col_sum.shape, 0)
        col_fine = (slot_at >= count) | (col_sum[...] >= COL_LOW)
        fine = jnp.min(jnp.where(col_fine, 1.0, 0.0), axis=0)
        fine = jnp.min(jnp.where(row_fine, fine, 0.0))

        @pl.when(fine < 0.5)
        def _():
            row_acc[...] = jnp.full_like(row_acc, NEG_FILL)
            col_tmp[...] = jnp.zeros_like(col_tmp)

            @pl.loop(0, count)
            def _(slot):
                at = blk * SLOTS + slot
                for part in range(rows // LANES):
                    span = pl.ds(part * LANES, LANES)
                    scores = raw_scores(src_ref[blk, span, :], held[at]) * factor
                    old = row_acc[span, :]
                    new = jnp.maximum(old, jnp.max(scores, axis=1, keepdims=True))
                    here = jnp.sum(jnp.exp(scores - new[:, 0:1]), axis=1, keepdims=True)
                    col_tmp[span, :] = col_tmp[span, :] * jnp.exp(old - new) + here
                    row_acc[span, :] = new

            source = as_columns(logw_ref[blk]) - (row_acc[...] + jnp.log(col_tmp[...]))
            row_acc[...] = source
            fs_ref[blk] = as_row(source)

            @pl.loop(0, count)
            def _(slot):
                at = blk * SLOTS + slot
                high = jnp.full((1, rows), NEG_FILL, jnp.float32)
                total = jnp.zeros((1, rows), jnp.float32)
                for part in range(rows // LANES):
                    span = pl.ds(part * LANES, LANES)
                    scores = raw_scores(src_ref[blk, span, :], held[at]) * factor
                    scores = scores + row_acc[span, 0:1]
                    new = jnp.maximum(high, jnp.max(scores, axis=0, keepdims=True))
                    total = total * jnp.exp(high - new) + jnp.sum(
                        jnp.exp(scores - new), axis=0, keepdims=True
                    )
                    high = new
                col_max[slot] = high
                col_sum[slot] = total

        @pl.loop(0, count)
        def _(slot):
            position = pos_ref[blk * SLOTS + slot]
            old = tab_max[position]
            high = col_max[slot]
            new = jnp.maximum(old, high)
            tab_sum[position] = tab_sum[position] * jnp.exp(old - new) + col_sum[slot] * jnp.exp(
                high - new
            )
            tab_max[position] = new

    sums = tab_sum[...]
    used = sums > 0.0
    part_ref[...] = jnp.where(
        used, tab_max[...] + jnp.log(jnp.where(used, sums, 1.0)), NEG_FILL
    )


def second_kernel(
    pos_ref, cnt_ref, src_ref, logw_ref, fs_ref, dual_ref, loc_ref, tab_ref,
    pot_ref, map_ref, sum_ref,
    held, kept, fs_col, acc, sems,
):
    scale = LOG2E / math.sqrt(EMB)
    rows = src_ref.shape[1]
    fetch_all(pos_ref, cnt_ref, loc_ref, tab_ref, held, sems, True)
    sum_ref[...] = jnp.zeros_like(sum_ref)
    ones = jnp.ones((rows, LANES), jnp.bfloat16)

    @pl.loop(0, BLK_DEV)
    def _(blk):
        count = cnt_ref[blk]
        await_blocks(blk, count, loc_ref, held, sems)
        first_source = fs_ref[blk]
        fs_col[...] = as_columns(first_source * LOG2E)
        acc[...] = jnp.zeros_like(acc)

        def row_work(width):
            for slot in range(width):
                at = blk * SLOTS + slot
                dual = jnp.where(slot < count, dual_ref[pos_ref[at]] * LOG2E, NEG_FILL)
                points = held[at]
                beside = jnp.concatenate([points, ones], axis=1)
                for part in range(rows // LANES):
                    span = pl.ds(part * LANES, LANES)
                    shift = jnp.concatenate([fs_col[span, :]] * (rows // LANES), axis=1)
                    plan = jnp.exp2(
                        raw_scores(src_ref[blk, span, :], points) * scale + (dual + shift)
                    ).astype(jnp.bfloat16)
                    kept[slot, span, :] = plan
                    acc[span, :] += jnp.dot(plan, beside, preferred_element_type=jnp.float32)

        by_width(count, row_work)
        row_col = acc[:, LANES:]
        map_ref[blk] = acc[:, :LANES] / row_col
        row_sum = as_row(row_col)
        logw = logw_ref[blk]
        pot_ref[blk] = logw + first_source - jnp.log(row_sum)
        weights = weight_rows(jnp.exp(logw) / row_sum)

        def column_work(width):
            for slot in range(width):
                position = pos_ref[blk * SLOTS + slot]
                here = column_sums(weights, kept, slot)
                sum_ref[position] += jnp.where(slot < count, here, 0.0)

        by_width(count, column_work)


def deliver_kernel(
    dev_count, group_count, pick_ref, grp_ref, tgt_ref, tab_ref,
    prev_buf, next_buf, far_buf, relay_up, relay_down, stage,
    trunk_send, trunk_recv, stage_send, tab_recv, relay_recv, fwd_send, grp_recv,
):
    me_group, me_dev = lax.axis_index("group"), lax.axis_index("dev")
    core = lax.rem(me_dev, 2)
    at_x, at_z = lax.rem(me_dev // 2, RING), me_dev // (2 * RING)
    half = BLK_DEV // 2

    def device(along, across, to_core):
        dz = along + core * (across - along)
        dx = across + core * (along - across)
        return (lax.rem(at_z + dz, RING) * RING + lax.rem(at_x + dx, RING)) * 2 + to_core

    def send(src, dst, send_sem, recv_sem, dev, group=None):
        return pltpu.make_async_remote_copy(
            src_ref=src,
            dst_ref=dst,
            send_sem=send_sem,
            recv_sem=recv_sem,
            device_id=(me_group if group is None else group, dev),
            device_id_type=MESH,
        )

    barrier = pltpu.get_barrier_semaphore()
    near = [
        device(i, j, cc) for i, j in ((1, 0), (3, 0), (0, 1), (0, 3)) for cc in (0, 1)
    ] + [device(0, 0, 1 - core)]
    for dev in near:
        pl.semaphore_signal(barrier, inc=1, device_id=(me_group, dev), device_id_type=MESH)
    for step in range(1, group_count):
        pl.semaphore_signal(
            barrier,
            inc=1,
            device_id=(lax.rem(me_group + step, group_count), me_dev),
            device_id_type=MESH,
        )
    pl.semaphore_wait(barrier, len(near) + group_count - 1)

    low, top = pl.ds(0, half), pl.ds(half, half)
    ahead, behind = device(1, 0, core), device(3, 0, core)

    def trunk(n, src, dst, span, dev):
        return send(src.at[span], dst.at[span], trunk_send.at[n], trunk_recv.at[n], dev)

    trunks = [
        trunk(0, tgt_ref, prev_buf, low, ahead),
        trunk(1, tgt_ref, next_buf, top, behind),
        trunk(2, tgt_ref, prev_buf, top, ahead),
        trunk(3, tgt_ref, next_buf, low, behind),
        trunk(4, prev_buf, far_buf, low, ahead),
        trunk(5, next_buf, far_buf, top, behind),
    ]
    for n in range(4):
        trunks[n].start()
    sent = []

    def branch(k, buf):
        source = device(TRUNK[k], 0, core)
        for n, (across, to_core) in enumerate(BRANCH + ((0, 1 - core),)):
            taker = device(0, across, to_core)
            at = k * (len(BRANCH) + 1) + n
            stage[at] = buf[jnp.maximum(pick_ref[taker, source], 0)]
            if across == 2:
                relay, over = ((relay_up, 1), (relay_down, 3))[to_core]
                which = relay_recv.at[to_core * RING + k]
                copy = send(
                    stage.at[at], relay.at[k], stage_send.at[at], which, device(0, over, core)
                )
            else:
                copy = send(
                    stage.at[at],
                    tab_ref.at[BLK_DEV + source],
                    stage_send.at[at],
                    tab_recv.at[source],
                    taker,
                )
            copy.start()
            sent.append(copy)
        if k > 0:
            at = RING * (len(BRANCH) + 1) + group_count - 1 + k - 1
            stage[at] = buf[jnp.maximum(pick_ref[me_dev, source], 0)]
            pltpu.make_async_copy(
                stage.at[at], tab_ref.at[BLK_DEV + source], tab_recv.at[source]
            ).start()

    def pass_on(k):
        for way, (relay, back, over) in enumerate(((relay_up, 3, 1), (relay_down, 1, 3))):
            source = device(TRUNK[k], back, core)
            at = way * RING + k
            copy = send(
                relay.at[k],
                tab_ref.at[BLK_DEV + source],
                fwd_send.at[at],
                tab_recv.at[source],
                device(0, over, way),
            )
            send(
                relay.at[k], relay.at[k], fwd_send.at[at], relay_recv.at[at], ahead
            ).wait_recv()
            copy.start()
            sent.append(copy)

    branch(0, tgt_ref)
    from_groups = []
    for step in range(1, group_count):
        peer = lax.rem(me_group + step, group_count)
        at = RING * (len(BRANCH) + 1) + step - 1
        stage[at] = tgt_ref[jnp.maximum(grp_ref[peer], 0)]
        copy = send(
            stage.at[at],
            tab_ref.at[BLK_DEV + dev_count + me_group],
            stage_send.at[at],
            grp_recv.at[step],
            me_dev,
            peer,
        )
        copy.start()
        sent.append(copy)
        from_groups.append(copy)
    trunks[0].wait_recv()
    trunks[4].start()
    trunks[1].wait_recv()
    trunks[5].start()
    trunks[2].wait_recv()
    branch(1, prev_buf)
    trunks[3].wait_recv()
    branch(2, next_buf)
    pass_on(0)
    trunks[4].wait_recv()
    trunks[5].wait_recv()
    branch(3, far_buf)
    pass_on(1)
    pass_on(2)
    pass_on(3)
    for copy in sent + trunks:
        copy.wait_send()
    for step in range(1, dev_count):
        source = lax.rem(me_dev + step, dev_count)
        send(
            stage.at[0], tab_ref.at[BLK_DEV + source], stage_send.at[0], tab_recv.at[source], ahead
        ).wait_recv()
    for copy in from_groups:
        copy.wait_recv()


def greet(dev_count, group_count, me_dev, me_group):
    barrier = pltpu.get_barrier_semaphore()

    def to_dev(step, carry):
        peer = lax.rem(me_dev + step, dev_count)
        pl.semaphore_signal(barrier, inc=1, device_id=(me_group, peer), device_id_type=MESH)
        return carry

    def to_group(step, carry):
        peer = lax.rem(me_group + step, group_count)
        pl.semaphore_signal(barrier, inc=1, device_id=(peer, me_dev), device_id_type=MESH)
        return carry

    lax.fori_loop(1, dev_count, to_dev, 0)
    lax.fori_loop(1, group_count, to_group, 0)
    pl.semaphore_wait(barrier, dev_count + group_count - 2)


def exchange(
    out_ref, out_base, in_ref, in_base, send_sem, recv_sem, dev_count, group_count, me_dev, me_group
):
    def to_dev(step):
        peer = lax.rem(me_dev + step, dev_count)
        return pltpu.make_async_remote_copy(
            src_ref=out_ref.at[out_base + peer],
            dst_ref=in_ref.at[in_base + me_dev],
            send_sem=send_sem.at[step],
            recv_sem=recv_sem.at[step],
            device_id=(me_group, peer),
            device_id_type=MESH,
        )

    def to_group(step):
        peer = lax.rem(me_group + step, group_count)
        return pltpu.make_async_remote_copy(
            src_ref=out_ref.at[out_base + dev_count + peer],
            dst_ref=in_ref.at[in_base + dev_count + me_group],
            send_sem=send_sem.at[dev_count + step],
            recv_sem=recv_sem.at[dev_count + step],
            device_id=(peer, me_dev),
            device_id_type=MESH,
        )

    def start(copy_of):
        def body(step, carry):
            copy_of(step).start()
            return carry

        return body

    def wait(copy_of):
        def body(step, carry):
            copy_of(step).wait()
            return carry

        return body

    lax.fori_loop(1, dev_count, start(to_dev), 0)
    lax.fori_loop(1, group_count, start(to_group), 0)
    lax.fori_loop(1, dev_count, wait(to_dev), 0)
    lax.fori_loop(1, group_count, wait(to_group), 0)


def picker(pick_ref, grp_ref, dev_count, me_dev):
    def pick_of(e):
        of_dev = pick_ref[jnp.minimum(e, dev_count - 1), me_dev]
        return jnp.where(e < dev_count, of_dev, grp_ref[jnp.maximum(e - dev_count, 0)])

    return pick_of


def settle_kernel(
    dev_count, group_count, pick_ref, grp_ref, part_ref, logw_ref, dual_ref,
    inbox, outbox, send_a, recv_a, send_b, recv_b,
):
    me_group, me_dev = lax.axis_index("group"), lax.axis_index("dev")
    blocks = BLK_DEV
    peers = dev_count + group_count
    empty = jnp.full(inbox.shape[1:], NEG_FILL, jnp.float32)
    greet(dev_count, group_count, me_dev, me_group)
    inbox[me_dev] = empty
    inbox[dev_count + me_group] = empty
    exchange(
        part_ref, blocks, inbox, 0, send_a, recv_a, dev_count, group_count, me_dev, me_group
    )
    own = [part_ref[q] for q in range(blocks)]

    pick_of = picker(pick_ref, grp_ref, dev_count, me_dev)

    def highest(e, carry):
        pick, here = pick_of(e), inbox[e]
        return tuple(
            jnp.maximum(high, jnp.where(pick == q, here, NEG_FILL)) for q, high in enumerate(carry)
        )

    highs = lax.fori_loop(0, peers, highest, tuple(own))

    def summed(e, carry):
        pick, here = pick_of(e), inbox[e]
        return tuple(
            total + jnp.exp(jnp.where(pick == q, here, NEG_FILL) - highs[q])
            for q, total in enumerate(carry)
        )

    totals = lax.fori_loop(
        0, peers, summed, tuple(jnp.exp(o - h) for o, h in zip(own, highs))
    )
    duals = [
        logw_ref[q] - (highs[q] + jnp.log(totals[q])) for q in range(blocks)
    ]
    for q in range(blocks):
        dual_ref[q] = duals[q]

    def fill(e, carry):
        pick = pick_of(e)
        chosen = jnp.zeros_like(duals[0])
        for q in range(blocks):
            chosen = jnp.where(pick == q, duals[q], chosen)
        outbox[e] = chosen
        return carry

    lax.fori_loop(0, peers, fill, 0)
    dual_ref[blocks + me_dev] = jnp.zeros_like(duals[0])
    dual_ref[blocks + dev_count + me_group] = jnp.zeros_like(duals[0])
    exchange(
        outbox, 0, dual_ref, blocks, send_b, recv_b, dev_count, group_count, me_dev, me_group
    )


def close_kernel(
    dev_count, group_count, pick_ref, grp_ref, sum_ref, logw_ref, first_ref, pot_ref,
    inbox, send_a, recv_a,
):
    me_group, me_dev = lax.axis_index("group"), lax.axis_index("dev")
    blocks = BLK_DEV
    peers = dev_count + group_count
    greet(dev_count, group_count, me_dev, me_group)
    inbox[me_dev] = jnp.zeros(inbox.shape[1:], jnp.float32)
    inbox[dev_count + me_group] = jnp.zeros(inbox.shape[1:], jnp.float32)
    exchange(
        sum_ref, blocks, inbox, 0, send_a, recv_a, dev_count, group_count, me_dev, me_group
    )

    pick_of = picker(pick_ref, grp_ref, dev_count, me_dev)

    def summed(e, carry):
        pick, here = pick_of(e), inbox[e]
        return tuple(
            total + jnp.where(pick == q, here, 0.0) for q, total in enumerate(carry)
        )

    totals = lax.fori_loop(0, peers, summed, tuple(sum_ref[q] for q in range(blocks)))
    for q in range(blocks):
        pot_ref[q] = logw_ref[q] - jnp.log(totals[q]) + first_ref[q]


def shards(source_points, target_points, source_logw, target_logw, pair_targets, pair_count):
    group_count = lax.axis_size("group")
    dev_count = lax.axis_size("dev")
    group_idx = lax.axis_index("group")
    dev_idx = lax.axis_index("dev")
    myself = group_idx * dev_count + dev_idx
    blocks, rows, slots = BLK_DEV, BLOCK, SLOTS
    table = blocks + dev_count + group_count
    peers = dev_count + group_count
    sources = source_points.reshape(blocks, rows, EMB)
    targets = target_points.reshape(blocks, rows, EMB)
    log_src = source_logw.reshape(blocks, 1, rows)
    log_tgt = target_logw.reshape(blocks, rows // LANES, LANES)

    own_targets = lax.dynamic_slice_in_dim(pair_targets, myself * blocks, blocks, 0)
    own_counts = lax.dynamic_slice_in_dim(pair_count, myself * blocks, blocks, 0)
    owners = own_targets // blocks
    position = jnp.where(
        owners == myself,
        own_targets % blocks,
        jnp.where(
            owners // dev_count == group_idx,
            blocks + owners % dev_count,
            blocks + dev_count + owners // dev_count,
        ),
    ).reshape(blocks * slots)
    everything = pair_targets.reshape(group_count, dev_count, blocks, slots)
    counts_all = pair_count.reshape(group_count, dev_count, blocks)
    pick = chosen_blocks(
        lax.dynamic_index_in_dim(everything, group_idx, 0, keepdims=False),
        lax.dynamic_index_in_dim(counts_all, group_idx, 0, keepdims=False),
        group_idx * dev_count * blocks,
        jnp.arange(dev_count, dtype=jnp.int32),
    )
    pick_grp = chosen_blocks(
        lax.dynamic_index_in_dim(everything, dev_idx, 1, keepdims=False),
        lax.dynamic_index_in_dim(counts_all, dev_idx, 1, keepdims=False),
        myself * blocks,
        jnp.zeros((1,), jnp.int32),
    )[:, 0]
    pick = jnp.where(
        jnp.arange(dev_count)[:, None] == jnp.arange(dev_count)[None, :], -1, pick
    )
    pick_grp = jnp.where(jnp.arange(group_count) == group_idx, -1, pick_grp)

    smem = pl.BlockSpec(memory_space=pltpu.SMEM)
    vmem = pl.BlockSpec(memory_space=pltpu.VMEM)
    anywhere = pl.BlockSpec(memory_space=pl.ANY)
    f32 = jnp.float32
    held = pltpu.VMEM((blocks * slots, rows, EMB), jnp.bfloat16)
    kept = pltpu.VMEM((slots, rows, rows), jnp.bfloat16)
    copy_sems = pltpu.SemaphoreType.DMA((blocks * slots,))
    pairs = blocks * slots
    dma = pltpu.SemaphoreType.DMA
    block = (rows, EMB)
    lots = RING * (len(BRANCH) + 1) + group_count - 1 + RING - 1
    delivered = pl.pallas_call(
        functools.partial(deliver_kernel, dev_count, group_count),
        out_shape=jax.ShapeDtypeStruct((table, *block), jnp.bfloat16),
        in_specs=[smem, smem, vmem],
        out_specs=anywhere,
        scratch_shapes=[pltpu.VMEM((blocks, *block), jnp.bfloat16)] * 3
        + [pltpu.VMEM((RING, *block), jnp.bfloat16)] * 2
        + [
            pltpu.VMEM((lots, *block), jnp.bfloat16),
            dma((6,)),
            dma((6,)),
            dma((lots,)),
            dma((dev_count,)),
            dma((2 * RING,)),
            dma((2 * RING,)),
            dma((group_count,)),
        ],
        compiler_params=pltpu.CompilerParams(
            collective_id=2, has_side_effects=True, vmem_limit_bytes=VMEM_LIMIT
        ),
        name="deliver_blocks",
    )(pick, pick_grp, targets)

    first_source, part = pl.pallas_call(
        first_kernel,
        out_shape=(
            jax.ShapeDtypeStruct((blocks, 1, rows), f32),
            jax.ShapeDtypeStruct((table, 1, rows), f32),
        ),
        in_specs=[smem, smem, vmem, vmem, anywhere, anywhere],
        out_specs=(vmem, vmem),
        scratch_shapes=[
            held,
            kept,
            pltpu.VMEM((rows, LANES), f32),
            pltpu.VMEM((slots, 1, rows), f32),
            pltpu.VMEM((slots, 1, rows), f32),
            pltpu.VMEM((table, 1, rows), f32),
            pltpu.VMEM((table, 1, rows), f32),
            pltpu.VMEM((rows, LANES), f32),
            copy_sems,
        ],
        compiler_params=pltpu.CompilerParams(vmem_limit_bytes=VMEM_LIMIT),
        cost_estimate=pl.CostEstimate(
            flops=4 * pairs * rows * rows * EMB, bytes_accessed=6 * 2**20, transcendentals=pairs * rows * rows
        ),
        name="first_pass",
    )(position, own_counts, sources, log_src, targets, delivered)

    small = (rows // LANES, LANES)
    sems = pltpu.SemaphoreType.DMA((peers,))
    dual = pl.pallas_call(
        functools.partial(settle_kernel, dev_count, group_count),
        out_shape=jax.ShapeDtypeStruct((table, *small), f32),
        in_specs=[smem, smem, vmem, vmem],
        out_specs=vmem,
        scratch_shapes=[
            pltpu.VMEM((peers, *small), f32),
            pltpu.VMEM((peers, *small), f32),
            sems,
            sems,
            sems,
            sems,
        ],
        compiler_params=pltpu.CompilerParams(collective_id=0, has_side_effects=True),
        name="settle_first",
    )(pick, pick_grp, part.reshape(table, *small), log_tgt)

    potential, mapped, col_sums = pl.pallas_call(
        second_kernel,
        out_shape=(
            jax.ShapeDtypeStruct((blocks, 1, rows), f32),
            jax.ShapeDtypeStruct((blocks, rows, EMB), f32),
            jax.ShapeDtypeStruct((table, 1, rows), f32),
        ),
        in_specs=[smem, smem, vmem, vmem, vmem, vmem, anywhere, anywhere],
        out_specs=(vmem, vmem, vmem),
        scratch_shapes=[
            held,
            kept,
            pltpu.VMEM((rows, LANES), f32),
            pltpu.VMEM((rows, 2 * LANES), f32),
            copy_sems,
        ],
        compiler_params=pltpu.CompilerParams(vmem_limit_bytes=VMEM_LIMIT),
        cost_estimate=pl.CostEstimate(
            flops=8 * pairs * rows * rows * EMB, bytes_accessed=7 * 2**20, transcendentals=pairs * rows * rows
        ),
        name="second_pass",
    )(
        position, own_counts, sources, log_src, first_source,
        dual.reshape(table, 1, rows), targets, delivered,
    )

    target_potential = pl.pallas_call(
        functools.partial(close_kernel, dev_count, group_count),
        out_shape=jax.ShapeDtypeStruct((blocks, *small), f32),
        in_specs=[smem, smem, vmem, vmem, vmem],
        out_specs=vmem,
        scratch_shapes=[pltpu.VMEM((peers, *small), f32), sems, sems],
        compiler_params=pltpu.CompilerParams(collective_id=1, has_side_effects=True),
        name="settle_second",
    )(pick, pick_grp, col_sums.reshape(table, *small), log_tgt, dual)
    return (
        potential.reshape(blocks * rows),
        target_potential.reshape(blocks * rows),
        mapped.reshape(blocks * rows, EMB),
    )


def solution(mesh):
    return jax.shard_map(
        shards,
        mesh=mesh,
        in_specs=(
            P(("group", "dev"), None),
            P(("group", "dev"), None),
            P(("group", "dev")),
            P(("group", "dev")),
            P(),
            P(),
        ),
        out_specs=(P(("group", "dev")), P(("group", "dev")), P(("group", "dev"), None)),
        check_vma=False,
    )
```

```python
import functools
import math

import jax
import jax.numpy as jnp
from jax import lax
from jax.experimental import pallas as pl
from jax.experimental.pallas import tpu as pltpu
from jax.sharding import PartitionSpec as P

BLOCK = 512
EMB = 128
BLK_DEV = 4
SLOTS = 8
LANES = 128
NEG_FILL = -1e30
LOG2E = math.log2(math.e)
ROW_LOW, ROW_HIGH, COL_LOW = 1e-6, 1e30, 1e-22
MESH = pl.DeviceIdType.MESH
VMEM_LIMIT = 20 * 2**20


RING = 4
TRUNK = (0, 3, 1, 2)
BRANCH = ((2, 0), (2, 1), (1, 0), (1, 1), (3, 0), (3, 1))


def plane_picks(targets, counts, first, sources):
    slots = lax.broadcasted_iota(jnp.int32, targets.shape, 0)
    named = jnp.where(slots < counts[None, :], targets - first, -1)[:, None, :]
    source = lax.broadcasted_iota(jnp.int32, (1, sources, 1), 1)
    return jnp.max(jnp.where((named >> 2) == source, named & 3, -1), axis=0)


def pick_of_dev(pick_ref, taker, source):
    first = pick_ref[source, BLK_DEV * taker]
    for row in range(1, BLK_DEV):
        first = jnp.maximum(first, pick_ref[source, BLK_DEV * taker + row])
    return first


def pick_of_group(pairs_ref, dev_count, peer, me_group, me_dev):
    base = (peer * dev_count + me_dev) * BLK_DEV
    mine = me_group * dev_count + me_dev
    found = jnp.int32(-1)
    for row in range(BLK_DEV):
        name = pairs_ref[1, base + row]
        found = jnp.maximum(found, jnp.where(name // BLK_DEV == mine, name % BLK_DEV, -1))
    return found


def table_position(pairs_ref, dev_count, myself, blk, slot):
    name = pairs_ref[slot, myself * BLK_DEV + blk]
    owner = name // BLK_DEV
    group = owner // dev_count
    away = jnp.where(
        group == myself // dev_count, owner % dev_count, dev_count + group
    )
    return jnp.where(owner == myself, name % BLK_DEV, BLK_DEV + away)


def raw_scores(left, right):
    return lax.dot_general(left, right, (((1,), (1,)), ((), ())), preferred_element_type=jnp.float32)


def as_columns(row):
    return jnp.transpose(jnp.broadcast_to(row, (LANES, row.shape[1])))


def as_row(columns):
    return jnp.transpose(columns)[0:1]


def weight_rows(weights):
    high = weights.astype(jnp.bfloat16).astype(jnp.float32)
    rest = weights - high
    middle = rest.astype(jnp.bfloat16).astype(jnp.float32)
    low = rest - middle
    at = lax.broadcasted_iota(jnp.int32, (16, weights.shape[1]), 0)
    zero = jnp.zeros((16, weights.shape[1]), jnp.float32)
    rows = jnp.where(at == 0, high, jnp.where(at == 1, middle, jnp.where(at == 2, low, zero)))
    return rows.astype(jnp.bfloat16)


def by_width(count, work):
    @pl.when(count <= SLOTS // 2)
    def _():
        work(SLOTS // 2)

    @pl.when(count > SLOTS // 2)
    def _():
        work(SLOTS)


def column_sums(weights, kept, slot):
    return jnp.sum(
        jnp.dot(weights, kept[slot], preferred_element_type=jnp.float32), axis=0, keepdims=True
    )


def first_kernel(
    dev_count, pairs_ref, count_ref, src_ref, logw_ref, tab_ref,
    fs_ref, part_ref,
    kept, row_acc, col_sum, slow_max, slow_sum, col_tmp, slow_ref,
):
    factor = 1.0 / math.sqrt(EMB)
    scale = factor * LOG2E
    rows = src_ref.shape[1]
    myself = lax.axis_index("group") * dev_count + lax.axis_index("dev")
    position_of = functools.partial(table_position, pairs_ref, dev_count, myself)
    part_ref[...] = jnp.zeros_like(part_ref)
    slow_ref[0] = jnp.int32(0)

    @pl.loop(0, BLK_DEV)
    def _(blk):
        count = count_ref[myself * BLK_DEV + blk]

        def row_work(width):
            totals = jnp.zeros_like(row_acc)
            for slot in range(width):
                points = tab_ref[position_of(blk, slot)]
                kern = jnp.exp2(raw_scores(src_ref[blk], points) * scale)
                kept[slot] = kern.astype(jnp.bfloat16)
                total = kern[:, :LANES]
                for lane in range(1, rows // LANES):
                    total = total + kern[:, lane * LANES : (lane + 1) * LANES]
                totals = totals + jnp.where(slot < count, total, 0.0)
            row_acc[...] = totals

        by_width(count, row_work)
        row_sum = lax.dot_general(
            jnp.ones((8, LANES), jnp.float32),
            row_acc[...],
            (((1,), (1,)), ((), ())),
            precision=lax.Precision.HIGHEST,
            preferred_element_type=jnp.float32,
        )[0:1]
        logw = logw_ref[blk]
        fs_ref[blk] = logw - jnp.log(row_sum)
        weights = weight_rows(jnp.exp(logw) / row_sum)

        def column_work(width):
            for slot in range(width):
                col_sum[slot] = column_sums(weights, kept, slot)

        by_width(count, column_work)
        row_fine = (row_sum >= ROW_LOW) & (row_sum <= ROW_HIGH)
        slot_at = lax.broadcasted_iota(jnp.int32, col_sum.shape, 0)
        col_fine = (slot_at >= count) | (col_sum[...] >= COL_LOW)
        fine = jnp.min(jnp.where(col_fine, 1.0, 0.0), axis=0)
        fine = jnp.min(jnp.where(row_fine, fine, 0.0))

        @pl.when(fine >= 0.5)
        def _():
            def add(width):
                for slot in range(width):
                    part_ref[position_of(blk, slot)] += jnp.where(slot < count, col_sum[slot], 0.0)

            by_width(count, add)

        @pl.when(fine < 0.5)
        def _():
            @pl.when(slow_ref[0] == 0)
            def _():
                slow_ref[0] = jnp.int32(1)
                slow_max[...] = jnp.full_like(slow_max, NEG_FILL)
                slow_sum[...] = jnp.zeros_like(slow_sum)

            row_acc[...] = jnp.full_like(row_acc, NEG_FILL)
            col_tmp[...] = jnp.zeros_like(col_tmp)

            @pl.loop(0, count)
            def _(slot):
                points = tab_ref[position_of(blk, slot)]
                for part in range(rows // LANES):
                    span = pl.ds(part * LANES, LANES)
                    scores = raw_scores(src_ref[blk, span, :], points) * factor
                    old = row_acc[span, :]
                    new = jnp.maximum(old, jnp.max(scores, axis=1, keepdims=True))
                    here = jnp.sum(jnp.exp(scores - new[:, 0:1]), axis=1, keepdims=True)
                    col_tmp[span, :] = col_tmp[span, :] * jnp.exp(old - new) + here
                    row_acc[span, :] = new

            source = as_columns(logw_ref[blk]) - (row_acc[...] + jnp.log(col_tmp[...]))
            row_acc[...] = source
            fs_ref[blk] = as_row(source)

            @pl.loop(0, count)
            def _(slot):
                position = position_of(blk, slot)
                points = tab_ref[position]
                high = jnp.full((1, rows), NEG_FILL, jnp.float32)
                total = jnp.zeros((1, rows), jnp.float32)
                for part in range(rows // LANES):
                    span = pl.ds(part * LANES, LANES)
                    scores = raw_scores(src_ref[blk, span, :], points) * factor
                    scores = scores + row_acc[span, 0:1]
                    new = jnp.maximum(high, jnp.max(scores, axis=0, keepdims=True))
                    total = total * jnp.exp(high - new) + jnp.sum(
                        jnp.exp(scores - new), axis=0, keepdims=True
                    )
                    high = new
                old = slow_max[position]
                new = jnp.maximum(old, high)
                slow_sum[position] = slow_sum[position] * jnp.exp(old - new) + total * jnp.exp(
                    high - new
                )
                slow_max[position] = new

    sums = part_ref[...]
    lse = jnp.where(sums > 0.0, jnp.log(jnp.where(sums > 0.0, sums, 1.0)), NEG_FILL)
    part_ref[...] = lse

    @pl.when(slow_ref[0] == 1)
    def _():
        fast, sums = part_ref[...], slow_sum[...]
        slow = slow_max[...] + jnp.log(jnp.where(sums > 0.0, sums, 1.0))
        slow = jnp.where(sums > 0.0, slow, NEG_FILL)
        high = jnp.maximum(fast, slow)
        part_ref[...] = high + jnp.log(jnp.exp(fast - high) + jnp.exp(slow - high))


def second_kernel(
    dev_count, pairs_ref, count_ref, src_ref, logw_ref, fs_ref, dual_ref, tab_ref,
    pot_ref, map_ref, sum_ref,
    kept, fs_col, acc,
):
    scale = LOG2E / math.sqrt(EMB)
    rows = src_ref.shape[1]
    myself = lax.axis_index("group") * dev_count + lax.axis_index("dev")
    position_of = functools.partial(table_position, pairs_ref, dev_count, myself)
    sum_ref[...] = jnp.zeros_like(sum_ref)
    ones = jnp.ones((rows, LANES), jnp.bfloat16)

    @pl.loop(0, BLK_DEV)
    def _(blk):
        count = count_ref[myself * BLK_DEV + blk]
        first_source = fs_ref[blk]
        fs_col[...] = as_columns(first_source * LOG2E)
        acc[...] = jnp.zeros_like(acc)

        def row_work(width):
            for slot in range(width):
                position = position_of(blk, slot)
                dual = jnp.where(slot < count, dual_ref[position] * LOG2E, NEG_FILL)
                points = tab_ref[position]
                beside = jnp.concatenate([points, ones], axis=1)
                for part in range(rows // LANES):
                    span = pl.ds(part * LANES, LANES)
                    shift = jnp.concatenate([fs_col[span, :]] * (rows // LANES), axis=1)
                    plan = jnp.exp2(
                        raw_scores(src_ref[blk, span, :], points) * scale + (dual + shift)
                    ).astype(jnp.bfloat16)
                    kept[slot, span, :] = plan
                    acc[span, :] += jnp.dot(plan, beside, preferred_element_type=jnp.float32)

        by_width(count, row_work)
        row_col = acc[:, LANES:]
        map_ref[blk] = acc[:, :LANES] / row_col
        row_sum = as_row(row_col)
        logw = logw_ref[blk]
        pot_ref[blk] = logw + first_source - jnp.log(row_sum)
        weights = weight_rows(jnp.exp(logw) / row_sum)

        def column_work(width):
            for slot in range(width):
                here = column_sums(weights, kept, slot)
                sum_ref[position_of(blk, slot)] += jnp.where(slot < count, here, 0.0)

        by_width(count, column_work)


def deliver_kernel(
    dev_count, group_count, pick_ref, pairs_ref, tgt_ref, tab_ref,
    prev_buf, next_buf, far_buf, relay_up, relay_down, stage,
    trunk_send, trunk_recv, stage_send, tab_recv, relay_recv, fwd_send, grp_recv, own_sem,
):
    me_group, me_dev = lax.axis_index("group"), lax.axis_index("dev")
    core = lax.rem(me_dev, 2)
    at_x, at_z = lax.rem(me_dev // 2, RING), me_dev // (2 * RING)
    half = BLK_DEV // 2

    def device(along, across, to_core):
        dz = along + core * (across - along)
        dx = across + core * (along - across)
        return (lax.rem(at_z + dz, RING) * RING + lax.rem(at_x + dx, RING)) * 2 + to_core

    def send(src, dst, send_sem, recv_sem, dev, group=None):
        return pltpu.make_async_remote_copy(
            src_ref=src,
            dst_ref=dst,
            send_sem=send_sem,
            recv_sem=recv_sem,
            device_id=(me_group if group is None else group, dev),
            device_id_type=MESH,
        )

    barrier = pltpu.get_barrier_semaphore()
    near = [
        device(i, j, cc) for i, j in ((1, 0), (3, 0), (0, 1), (0, 3)) for cc in (0, 1)
    ] + [device(0, 0, 1 - core)]
    for dev in near:
        pl.semaphore_signal(barrier, inc=1, device_id=(me_group, dev), device_id_type=MESH)
    for step in range(1, group_count):
        pl.semaphore_signal(
            barrier,
            inc=1,
            device_id=(lax.rem(me_group + step, group_count), me_dev),
            device_id_type=MESH,
        )
    pl.semaphore_wait(barrier, len(near) + group_count - 1)

    low, top = pl.ds(0, half), pl.ds(half, half)
    ahead, behind = device(1, 0, core), device(3, 0, core)

    def trunk(n, src, dst, span, dev):
        return send(src.at[span], dst.at[span], trunk_send.at[n], trunk_recv.at[n], dev)

    trunks = [
        trunk(0, tgt_ref, prev_buf, low, ahead),
        trunk(1, tgt_ref, next_buf, top, behind),
        trunk(2, tgt_ref, prev_buf, top, ahead),
        trunk(3, tgt_ref, next_buf, low, behind),
        trunk(4, prev_buf, far_buf, low, ahead),
        trunk(5, next_buf, far_buf, top, behind),
    ]
    for n in range(4):
        trunks[n].start()
    sent = []

    def branch(k, buf):
        source = device(TRUNK[k], 0, core)
        for n, (across, to_core) in enumerate(BRANCH + ((0, 1 - core),)):
            taker = device(0, across, to_core)
            at = k * (len(BRANCH) + 1) + n
            stage[at] = buf[jnp.maximum(pick_of_dev(pick_ref, taker, source), 0)]
            if across == 2:
                relay, over = ((relay_up, 1), (relay_down, 3))[to_core]
                which = relay_recv.at[to_core * RING + k]
                copy = send(
                    stage.at[at], relay.at[k], stage_send.at[at], which, device(0, over, core)
                )
            else:
                copy = send(
                    stage.at[at],
                    tab_ref.at[BLK_DEV + source],
                    stage_send.at[at],
                    tab_recv.at[source],
                    taker,
                )
            copy.start()
            sent.append(copy)
        if k > 0:
            at = RING * (len(BRANCH) + 1) + group_count - 1 + k - 1
            stage[at] = buf[jnp.maximum(pick_of_dev(pick_ref, me_dev, source), 0)]
            pltpu.make_async_copy(
                stage.at[at], tab_ref.at[BLK_DEV + source], tab_recv.at[source]
            ).start()

    def pass_on(k):
        for way, (relay, back, over) in enumerate(((relay_up, 3, 1), (relay_down, 1, 3))):
            source = device(TRUNK[k], back, core)
            at = way * RING + k
            copy = send(
                relay.at[k],
                tab_ref.at[BLK_DEV + source],
                fwd_send.at[at],
                tab_recv.at[source],
                device(0, over, way),
            )
            send(
                relay.at[k], relay.at[k], fwd_send.at[at], relay_recv.at[at], ahead
            ).wait_recv()
            copy.start()
            sent.append(copy)

    branch(0, tgt_ref)
    own = pltpu.make_async_copy(tgt_ref, tab_ref.at[pl.ds(0, BLK_DEV)], own_sem.at[0])
    own.start()
    from_groups = []
    for step in range(1, group_count):
        peer = lax.rem(me_group + step, group_count)
        at = RING * (len(BRANCH) + 1) + step - 1
        pick = pick_of_group(pairs_ref, dev_count, peer, me_group, me_dev)
        stage[at] = tgt_ref[jnp.maximum(pick, 0)]
        copy = send(
            stage.at[at],
            tab_ref.at[BLK_DEV + dev_count + me_group],
            stage_send.at[at],
            grp_recv.at[step],
            me_dev,
            peer,
        )
        copy.start()
        sent.append(copy)
        from_groups.append(copy)
    trunks[0].wait_recv()
    trunks[4].start()
    trunks[1].wait_recv()
    trunks[5].start()
    trunks[2].wait_recv()
    branch(1, prev_buf)
    trunks[3].wait_recv()
    branch(2, next_buf)
    pass_on(0)
    trunks[4].wait_recv()
    trunks[5].wait_recv()
    branch(3, far_buf)
    pass_on(1)
    pass_on(2)
    pass_on(3)
    for copy in sent + trunks:
        copy.wait_send()
    for step in range(1, dev_count):
        source = lax.rem(me_dev + step, dev_count)
        send(
            stage.at[0], tab_ref.at[BLK_DEV + source], stage_send.at[0], tab_recv.at[source], ahead
        ).wait_recv()
    for copy in from_groups:
        copy.wait_recv()
    own.wait()


def greet(dev_count, group_count, me_dev, me_group):
    barrier = pltpu.get_barrier_semaphore()

    def to_dev(step, carry):
        peer = lax.rem(me_dev + step, dev_count)
        pl.semaphore_signal(barrier, inc=1, device_id=(me_group, peer), device_id_type=MESH)
        return carry

    def to_group(step, carry):
        peer = lax.rem(me_group + step, group_count)
        pl.semaphore_signal(barrier, inc=1, device_id=(peer, me_dev), device_id_type=MESH)
        return carry

    lax.fori_loop(1, dev_count, to_dev, 0)
    lax.fori_loop(1, group_count, to_group, 0)
    pl.semaphore_wait(barrier, dev_count + group_count - 2)


def exchange(
    out_ref, out_base, in_ref, in_base, send_sem, recv_sem, dev_count, group_count, me_dev, me_group
):
    def to_dev(step):
        peer = lax.rem(me_dev + step, dev_count)
        return pltpu.make_async_remote_copy(
            src_ref=out_ref.at[out_base + peer],
            dst_ref=in_ref.at[in_base + me_dev],
            send_sem=send_sem.at[step],
            recv_sem=recv_sem.at[step],
            device_id=(me_group, peer),
            device_id_type=MESH,
        )

    def to_group(step):
        peer = lax.rem(me_group + step, group_count)
        return pltpu.make_async_remote_copy(
            src_ref=out_ref.at[out_base + dev_count + peer],
            dst_ref=in_ref.at[in_base + dev_count + me_group],
            send_sem=send_sem.at[dev_count + step],
            recv_sem=recv_sem.at[dev_count + step],
            device_id=(peer, me_dev),
            device_id_type=MESH,
        )

    def start(copy_of):
        def body(step, carry):
            copy_of(step).start()
            return carry

        return body

    def wait(copy_of):
        def body(step, carry):
            copy_of(step).wait()
            return carry

        return body

    lax.fori_loop(1, dev_count, start(to_dev), 0)
    lax.fori_loop(1, group_count, start(to_group), 0)
    lax.fori_loop(1, dev_count, wait(to_dev), 0)
    lax.fori_loop(1, group_count, wait(to_group), 0)


def picks_of_peers(pick_ref, pairs_ref, dev_count, group_count, me_group, me_dev):
    return [
        jnp.where(me_dev == e, -1, pick_of_dev(pick_ref, e, me_dev)) for e in range(dev_count)
    ] + [
        jnp.where(me_group == e, -1, pick_of_group(pairs_ref, dev_count, e, me_group, me_dev))
        for e in range(group_count)
    ]


def settle_kernel(
    dev_count, group_count, pick_ref, pairs_ref, part_ref, logw_ref, dual_ref,
    inbox, outbox, send_a, recv_a, send_b, recv_b,
):
    me_group, me_dev = lax.axis_index("group"), lax.axis_index("dev")
    blocks = BLK_DEV
    empty = jnp.full(inbox.shape[1:], NEG_FILL, jnp.float32)
    greet(dev_count, group_count, me_dev, me_group)
    inbox[me_dev] = empty
    inbox[dev_count + me_group] = empty
    picks = picks_of_peers(pick_ref, pairs_ref, dev_count, group_count, me_group, me_dev)
    exchange(
        part_ref, blocks, inbox, 0, send_a, recv_a, dev_count, group_count, me_dev, me_group
    )
    duals = []
    for q in range(blocks):
        terms = [part_ref[q]] + [
            jnp.where(pick == q, inbox[e], NEG_FILL) for e, pick in enumerate(picks)
        ]
        high = functools.reduce(jnp.maximum, terms)
        total = sum(jnp.exp(term - high) for term in terms)
        duals.append(logw_ref[q] - (high + jnp.log(total)))
        dual_ref[q] = duals[q]
    for e, pick in enumerate(picks):
        chosen = duals[0]
        for q in range(1, blocks):
            chosen = jnp.where(pick == q, duals[q], chosen)
        outbox[e] = chosen
    dual_ref[blocks + me_dev] = jnp.zeros_like(empty)
    dual_ref[blocks + dev_count + me_group] = jnp.zeros_like(empty)
    exchange(
        outbox, 0, dual_ref, blocks, send_b, recv_b, dev_count, group_count, me_dev, me_group
    )


def close_kernel(
    dev_count, group_count, pick_ref, pairs_ref, sum_ref, logw_ref, first_ref, pot_ref,
    inbox, send_a, recv_a,
):
    me_group, me_dev = lax.axis_index("group"), lax.axis_index("dev")
    blocks = BLK_DEV
    greet(dev_count, group_count, me_dev, me_group)
    inbox[me_dev] = jnp.zeros(inbox.shape[1:], jnp.float32)
    inbox[dev_count + me_group] = jnp.zeros(inbox.shape[1:], jnp.float32)
    picks = picks_of_peers(pick_ref, pairs_ref, dev_count, group_count, me_group, me_dev)
    exchange(
        sum_ref, blocks, inbox, 0, send_a, recv_a, dev_count, group_count, me_dev, me_group
    )
    for q in range(blocks):
        total = sum_ref[q]
        for e, pick in enumerate(picks):
            total = total + jnp.where(pick == q, inbox[e], 0.0)
        pot_ref[q] = logw_ref[q] - jnp.log(total) + first_ref[q]


def shards(source_points, target_points, source_logw, target_logw, pair_targets, pair_count):
    group_count = lax.axis_size("group")
    dev_count = lax.axis_size("dev")
    group_idx = lax.axis_index("group")
    blocks, rows, slots = BLK_DEV, BLOCK, SLOTS
    table = blocks + dev_count + group_count
    peers = dev_count + group_count
    sources = source_points.reshape(blocks, rows, EMB)
    targets = target_points.reshape(blocks, rows, EMB)
    log_src = source_logw.reshape(blocks, 1, rows)
    log_tgt = target_logw.reshape(blocks, rows // LANES, LANES)

    plane = dev_count * blocks
    named = pair_targets.T
    pick = plane_picks(
        lax.dynamic_slice_in_dim(named, group_idx * plane, plane, 1),
        lax.dynamic_slice_in_dim(pair_count, group_idx * plane, plane, 0),
        group_idx * plane,
        dev_count,
    )

    smem = pl.BlockSpec(memory_space=pltpu.SMEM)
    vmem = pl.BlockSpec(memory_space=pltpu.VMEM)
    anywhere = pl.BlockSpec(memory_space=pl.ANY)
    f32 = jnp.float32
    kept = pltpu.VMEM((slots, rows, rows), jnp.bfloat16)
    pairs = blocks * slots
    dma = pltpu.SemaphoreType.DMA
    block = (rows, EMB)
    lots = RING * (len(BRANCH) + 1) + group_count - 1 + RING - 1
    delivered = pl.pallas_call(
        functools.partial(deliver_kernel, dev_count, group_count),
        out_shape=jax.ShapeDtypeStruct((table, *block), jnp.bfloat16),
        in_specs=[smem, smem, vmem],
        out_specs=anywhere,
        scratch_shapes=[pltpu.VMEM((blocks, *block), jnp.bfloat16)] * 3
        + [pltpu.VMEM((RING, *block), jnp.bfloat16)] * 2
        + [
            pltpu.VMEM((lots, *block), jnp.bfloat16),
            dma((6,)),
            dma((6,)),
            dma((lots,)),
            dma((dev_count,)),
            dma((2 * RING,)),
            dma((2 * RING,)),
            dma((group_count,)),
            dma((1,)),
        ],
        compiler_params=pltpu.CompilerParams(
            collective_id=2, has_side_effects=True, vmem_limit_bytes=VMEM_LIMIT
        ),
        name="deliver_blocks",
    )(pick, named, targets)

    first_source, part = pl.pallas_call(
        functools.partial(first_kernel, dev_count),
        out_shape=(
            jax.ShapeDtypeStruct((blocks, 1, rows), f32),
            jax.ShapeDtypeStruct((table, 1, rows), f32),
        ),
        in_specs=[smem, smem, vmem, vmem, vmem],
        out_specs=(vmem, vmem),
        scratch_shapes=[
            kept,
            pltpu.VMEM((rows, LANES), f32),
            pltpu.VMEM((slots, 1, rows), f32),
            pltpu.VMEM((table, 1, rows), f32),
            pltpu.VMEM((table, 1, rows), f32),
            pltpu.VMEM((rows, LANES), f32),
            pltpu.SMEM((1,), jnp.int32),
        ],
        compiler_params=pltpu.CompilerParams(vmem_limit_bytes=VMEM_LIMIT),
        cost_estimate=pl.CostEstimate(
            flops=4 * pairs * rows * rows * EMB, bytes_accessed=6 * 2**20, transcendentals=pairs * rows * rows
        ),
        name="first_pass",
    )(named, pair_count, sources, log_src, delivered)

    small = (rows // LANES, LANES)
    sems = pltpu.SemaphoreType.DMA((peers,))
    dual = pl.pallas_call(
        functools.partial(settle_kernel, dev_count, group_count),
        out_shape=jax.ShapeDtypeStruct((table, *small), f32),
        in_specs=[smem, smem, vmem, vmem],
        out_specs=vmem,
        scratch_shapes=[
            pltpu.VMEM((peers, *small), f32),
            pltpu.VMEM((peers, *small), f32),
            sems,
            sems,
            sems,
            sems,
        ],
        compiler_params=pltpu.CompilerParams(
            collective_id=0, has_side_effects=True, vmem_limit_bytes=4 * 2**20
        ),
        name="settle_first",
    )(pick, named, part.reshape(table, *small), log_tgt)

    potential, mapped, col_sums = pl.pallas_call(
        functools.partial(second_kernel, dev_count),
        out_shape=(
            jax.ShapeDtypeStruct((blocks, 1, rows), f32),
            jax.ShapeDtypeStruct((blocks, rows, EMB), f32),
            jax.ShapeDtypeStruct((table, 1, rows), f32),
        ),
        in_specs=[smem, smem, vmem, vmem, vmem, vmem, vmem],
        out_specs=(vmem, vmem, vmem),
        scratch_shapes=[
            kept,
            pltpu.VMEM((rows, LANES), f32),
            pltpu.VMEM((rows, 2 * LANES), f32),
        ],
        compiler_params=pltpu.CompilerParams(vmem_limit_bytes=VMEM_LIMIT),
        cost_estimate=pl.CostEstimate(
            flops=8 * pairs * rows * rows * EMB, bytes_accessed=7 * 2**20, transcendentals=pairs * rows * rows
        ),
        name="second_pass",
    )(
        named, pair_count, sources, log_src, first_source,
        dual.reshape(table, 1, rows), delivered,
    )

    target_potential = pl.pallas_call(
        functools.partial(close_kernel, dev_count, group_count),
        out_shape=jax.ShapeDtypeStruct((blocks, *small), f32),
        in_specs=[smem, smem, vmem, vmem, vmem],
        out_specs=vmem,
        scratch_shapes=[pltpu.VMEM((peers, *small), f32), sems, sems],
        compiler_params=pltpu.CompilerParams(
            collective_id=1, has_side_effects=True, vmem_limit_bytes=4 * 2**20
        ),
        name="settle_second",
    )(pick, named, col_sums.reshape(table, *small), log_tgt, dual)
    return (
        potential.reshape(blocks * rows),
        target_potential.reshape(blocks * rows),
        mapped.reshape(blocks * rows, EMB),
    )


def solution(mesh):
    return jax.shard_map(
        shards,
        mesh=mesh,
        in_specs=(
            P(("group", "dev"), None),
            P(("group", "dev"), None),
            P(("group", "dev")),
            P(("group", "dev")),
            P(),
            P(),
        ),
        out_specs=(P(("group", "dev")), P(("group", "dev")), P(("group", "dev"), None)),
        check_vma=False,
    )
```

```python
import functools
import math

import jax
import jax.numpy as jnp
from jax import lax
from jax.experimental import pallas as pl
from jax.experimental.pallas import tpu as pltpu
from jax.sharding import PartitionSpec as P

BLOCK = 512
EMB = 128
BLK_DEV = 4
SLOTS = 8
LANES = 128
NEG_FILL = -1e30
LOG2E = math.log2(math.e)
ROW_LOW, ROW_HIGH, COL_LOW = 1e-6, 1e30, 1e-22
MESH = pl.DeviceIdType.MESH
VMEM_LIMIT = 20 * 2**20
PAIR_LIMIT = 36 * 2**20


RING = 4
TRUNK = (0, 3, 1, 2)
BRANCH = ((2, 0), (2, 1), (1, 0), (1, 1), (3, 0), (3, 1))


def plane_picks(targets, counts, first, sources):
    slots = lax.broadcasted_iota(jnp.int32, targets.shape, 0)
    named = jnp.where(slots < counts[None, :], targets - first, -1)[:, None, :]
    source = lax.broadcasted_iota(jnp.int32, (1, sources, 1), 1)
    return jnp.max(jnp.where((named >> 2) == source, named & 3, -1), axis=0)


def pick_of_dev(pick_ref, taker, source):
    first = pick_ref[source, BLK_DEV * taker]
    for row in range(1, BLK_DEV):
        first = jnp.maximum(first, pick_ref[source, BLK_DEV * taker + row])
    return first


def pick_of_group(pairs_ref, dev_count, peer, me_group, me_dev):
    base = (peer * dev_count + me_dev) * BLK_DEV
    mine = me_group * dev_count + me_dev
    found = jnp.int32(-1)
    for row in range(BLK_DEV):
        name = pairs_ref[1, base + row]
        found = jnp.maximum(found, jnp.where(name // BLK_DEV == mine, name % BLK_DEV, -1))
    return found


def table_position(pairs_ref, dev_count, myself, blk, slot):
    name = pairs_ref[slot, myself * BLK_DEV + blk]
    owner = name // BLK_DEV
    group = owner // dev_count
    away = jnp.where(
        group == myself // dev_count, owner % dev_count, dev_count + group
    )
    return jnp.where(owner == myself, name % BLK_DEV, BLK_DEV + away)


def raw_scores(left, right):
    return lax.dot_general(left, right, (((1,), (1,)), ((), ())), preferred_element_type=jnp.float32)


def as_columns(row):
    return jnp.transpose(jnp.broadcast_to(row, (LANES, row.shape[1])))


def as_row(columns):
    return jnp.transpose(columns)[0:1]


def weight_rows(weights):
    high = weights.astype(jnp.bfloat16).astype(jnp.float32)
    rest = weights - high
    middle = rest.astype(jnp.bfloat16).astype(jnp.float32)
    low = rest - middle
    at = lax.broadcasted_iota(jnp.int32, (16, weights.shape[1]), 0)
    zero = jnp.zeros((16, weights.shape[1]), jnp.float32)
    rows = jnp.where(at == 0, high, jnp.where(at == 1, middle, jnp.where(at == 2, low, zero)))
    return rows.astype(jnp.bfloat16)


def by_width(count, work):
    @pl.when(count <= SLOTS // 2)
    def _():
        work(SLOTS // 2)

    @pl.when(count > SLOTS // 2)
    def _():
        work(SLOTS)


def column_sums(weights, kernel):
    return jnp.sum(
        jnp.dot(weights, kernel, preferred_element_type=jnp.float32), axis=0, keepdims=True
    )


def first_kernel(
    dev_count, pairs_ref, count_ref, src_ref, logw_ref, tab_ref,
    fs_ref, part_ref,
    kept, row_acc, wts, fine_ref, col_max, col_total,
):
    factor = 1.0 / math.sqrt(EMB)
    scale = factor * LOG2E
    rows = src_ref.shape[1]
    myself = lax.axis_index("group") * dev_count + lax.axis_index("dev")
    position_of = functools.partial(table_position, pairs_ref, dev_count, myself)

    @pl.loop(0, BLK_DEV)
    def _(blk):
        count = count_ref[myself * BLK_DEV + blk]

        def row_work(width):
            totals = jnp.zeros((rows, LANES), jnp.float32)
            for slot in range(width):
                points = tab_ref[position_of(blk, slot)]
                kern = jnp.exp2(raw_scores(src_ref[blk], points) * scale)
                kept[blk * SLOTS + slot] = kern.astype(jnp.bfloat16)
                total = kern[:, :LANES]
                for lane in range(1, rows // LANES):
                    total = total + kern[:, lane * LANES : (lane + 1) * LANES]
                totals = totals + jnp.where(slot < count, total, 0.0)
            row_acc[pl.ds(blk * rows, rows), :] = totals

        by_width(count, row_work)

    row_sum = lax.dot_general(
        jnp.ones((8, LANES), jnp.float32),
        row_acc[...],
        (((1,), (1,)), ((), ())),
        precision=lax.Precision.HIGHEST,
        preferred_element_type=jnp.float32,
    )[0:1]
    logw = logw_ref[...]
    fs_ref[...] = logw - jnp.log(row_sum)
    weights = weight_rows(jnp.exp(logw) / row_sum)
    row_fine = jnp.where((row_sum >= ROW_LOW) & (row_sum <= ROW_HIGH), 1.0, 0.0)
    fine = jnp.ones((1, rows), jnp.float32)
    for blk in range(BLK_DEV):
        span = slice(blk * rows, (blk + 1) * rows)
        wts[blk] = weights[:, span]
        fine = jnp.minimum(fine, row_fine[:, span])
    fine_ref[...] = fine
    part_ref[...] = jnp.zeros_like(part_ref)

    @pl.loop(0, BLK_DEV)
    def _(blk):
        count = count_ref[myself * BLK_DEV + blk]

        def column_work(width):
            fine = fine_ref[...]
            for slot in range(width):
                here = column_sums(wts[blk], kept[blk * SLOTS + slot])
                part_ref[position_of(blk, slot)] += jnp.where(slot < count, here, 0.0)
                fine = jnp.minimum(
                    fine, jnp.where((here >= COL_LOW) | (slot >= count), 1.0, 0.0)
                )
            fine_ref[...] = fine

        by_width(count, column_work)

    sums = part_ref[...]
    part_ref[...] = jnp.where(sums > 0.0, jnp.log(jnp.where(sums > 0.0, sums, 1.0)), NEG_FILL)

    @pl.when(jnp.min(fine_ref[...]) < 0.5)
    def _():
        part_ref[...] = jnp.full_like(part_ref, NEG_FILL)

        @pl.loop(0, BLK_DEV)
        def _(blk):
            count = count_ref[myself * BLK_DEV + blk]
            col_max[...] = jnp.full_like(col_max, NEG_FILL)
            col_total[...] = jnp.zeros_like(col_total)

            @pl.loop(0, count)
            def _(slot):
                points = tab_ref[position_of(blk, slot)]
                for part in range(rows // LANES):
                    span = pl.ds(part * LANES, LANES)
                    scores = raw_scores(src_ref[blk, span, :], points) * factor
                    old = col_max[span, :]
                    new = jnp.maximum(old, jnp.max(scores, axis=1, keepdims=True))
                    here = jnp.sum(jnp.exp(scores - new[:, 0:1]), axis=1, keepdims=True)
                    col_total[span, :] = col_total[span, :] * jnp.exp(old - new) + here
                    col_max[span, :] = new

            lse = col_max[...] + jnp.log(col_total[...])
            row_acc[pl.ds(blk * rows, rows), :] = lse

            @pl.loop(0, count)
            def _(slot):
                position = position_of(blk, slot)
                points = tab_ref[position]
                logw_col = as_columns(logw_ref[:, pl.ds(pl.multiple_of(blk * rows, rows), rows)])
                source = logw_col - row_acc[pl.ds(blk * rows, rows), :]
                col_max[...] = source
                high = jnp.full((1, rows), NEG_FILL, jnp.float32)
                total = jnp.zeros((1, rows), jnp.float32)
                for part in range(rows // LANES):
                    span = pl.ds(part * LANES, LANES)
                    scores = raw_scores(src_ref[blk, span, :], points) * factor
                    scores = scores + col_max[span, 0:1]
                    new = jnp.maximum(high, jnp.max(scores, axis=0, keepdims=True))
                    total = total * jnp.exp(high - new) + jnp.sum(
                        jnp.exp(scores - new), axis=0, keepdims=True
                    )
                    high = new
                here = high + jnp.log(total)
                old = part_ref[position]
                new = jnp.maximum(old, here)
                part_ref[position] = new + jnp.log(jnp.exp(old - new) + jnp.exp(here - new))

        fs_ref[...] = logw_ref[...] - as_row(row_acc[...])


def deliver_kernel(
    dev_count, group_count, pick_ref, pairs_ref, tgt_ref, tab_ref,
    prev_buf, next_buf, far_buf, relay_up, relay_down, stage,
    trunk_send, trunk_recv, stage_send, tab_recv, relay_recv, fwd_send, grp_recv, own_sem,
):
    me_group, me_dev = lax.axis_index("group"), lax.axis_index("dev")
    core = lax.rem(me_dev, 2)
    at_x, at_z = lax.rem(me_dev // 2, RING), me_dev // (2 * RING)
    half = BLK_DEV // 2

    def device(along, across, to_core):
        dz = along + core * (across - along)
        dx = across + core * (along - across)
        return (lax.rem(at_z + dz, RING) * RING + lax.rem(at_x + dx, RING)) * 2 + to_core

    def send(src, dst, send_sem, recv_sem, dev, group=None):
        return pltpu.make_async_remote_copy(
            src_ref=src,
            dst_ref=dst,
            send_sem=send_sem,
            recv_sem=recv_sem,
            device_id=(me_group if group is None else group, dev),
            device_id_type=MESH,
        )

    barrier = pltpu.get_barrier_semaphore()
    near = [
        device(i, j, cc) for i, j in ((1, 0), (3, 0), (0, 1), (0, 3)) for cc in (0, 1)
    ] + [device(0, 0, 1 - core)]
    for dev in near:
        pl.semaphore_signal(barrier, inc=1, device_id=(me_group, dev), device_id_type=MESH)
    for step in range(1, group_count):
        pl.semaphore_signal(
            barrier,
            inc=1,
            device_id=(lax.rem(me_group + step, group_count), me_dev),
            device_id_type=MESH,
        )
    pl.semaphore_wait(barrier, len(near) + group_count - 1)

    low, top = pl.ds(0, half), pl.ds(half, half)
    ahead, behind = device(1, 0, core), device(3, 0, core)

    def trunk(n, src, dst, span, dev):
        return send(src.at[span], dst.at[span], trunk_send.at[n], trunk_recv.at[n], dev)

    trunks = [
        trunk(0, tgt_ref, prev_buf, low, ahead),
        trunk(1, tgt_ref, next_buf, top, behind),
        trunk(2, tgt_ref, prev_buf, top, ahead),
        trunk(3, tgt_ref, next_buf, low, behind),
        trunk(4, prev_buf, far_buf, low, ahead),
        trunk(5, next_buf, far_buf, top, behind),
    ]
    for n in range(4):
        trunks[n].start()
    sent = []

    def branch(k, buf):
        source = device(TRUNK[k], 0, core)
        for n, (across, to_core) in enumerate(BRANCH + ((0, 1 - core),)):
            taker = device(0, across, to_core)
            at = k * (len(BRANCH) + 1) + n
            stage[at] = buf[jnp.maximum(pick_of_dev(pick_ref, taker, source), 0)]
            if across == 2:
                relay, over = ((relay_up, 1), (relay_down, 3))[to_core]
                which = relay_recv.at[to_core * RING + k]
                copy = send(
                    stage.at[at], relay.at[k], stage_send.at[at], which, device(0, over, core)
                )
            else:
                copy = send(
                    stage.at[at],
                    tab_ref.at[BLK_DEV + source],
                    stage_send.at[at],
                    tab_recv.at[source],
                    taker,
                )
            copy.start()
            sent.append(copy)
        if k > 0:
            at = RING * (len(BRANCH) + 1) + group_count - 1 + k - 1
            stage[at] = buf[jnp.maximum(pick_of_dev(pick_ref, me_dev, source), 0)]
            pltpu.make_async_copy(
                stage.at[at], tab_ref.at[BLK_DEV + source], tab_recv.at[source]
            ).start()

    def pass_on(k):
        for way, (relay, back, over) in enumerate(((relay_up, 3, 1), (relay_down, 1, 3))):
            source = device(TRUNK[k], back, core)
            at = way * RING + k
            copy = send(
                relay.at[k],
                tab_ref.at[BLK_DEV + source],
                fwd_send.at[at],
                tab_recv.at[source],
                device(0, over, way),
            )
            send(
                relay.at[k], relay.at[k], fwd_send.at[at], relay_recv.at[at], ahead
            ).wait_recv()
            copy.start()
            sent.append(copy)

    branch(0, tgt_ref)
    own = pltpu.make_async_copy(tgt_ref, tab_ref.at[pl.ds(0, BLK_DEV)], own_sem.at[0])
    own.start()
    from_groups = []
    for step in range(1, group_count):
        peer = lax.rem(me_group + step, group_count)
        at = RING * (len(BRANCH) + 1) + step - 1
        pick = pick_of_group(pairs_ref, dev_count, peer, me_group, me_dev)
        stage[at] = tgt_ref[jnp.maximum(pick, 0)]
        copy = send(
            stage.at[at],
            tab_ref.at[BLK_DEV + dev_count + me_group],
            stage_send.at[at],
            grp_recv.at[step],
            me_dev,
            peer,
        )
        copy.start()
        sent.append(copy)
        from_groups.append(copy)
    trunks[0].wait_recv()
    trunks[4].start()
    trunks[1].wait_recv()
    trunks[5].start()
    trunks[2].wait_recv()
    branch(1, prev_buf)
    trunks[3].wait_recv()
    branch(2, next_buf)
    pass_on(0)
    trunks[4].wait_recv()
    trunks[5].wait_recv()
    branch(3, far_buf)
    pass_on(1)
    pass_on(2)
    pass_on(3)
    for copy in sent + trunks:
        copy.wait_send()
    for step in range(1, dev_count):
        source = lax.rem(me_dev + step, dev_count)
        send(
            stage.at[0], tab_ref.at[BLK_DEV + source], stage_send.at[0], tab_recv.at[source], ahead
        ).wait_recv()
    for copy in from_groups:
        copy.wait_recv()
    own.wait()


def greet(dev_count, group_count, me_dev, me_group):
    barrier = pltpu.get_barrier_semaphore()

    def to_dev(step, carry):
        peer = lax.rem(me_dev + step, dev_count)
        pl.semaphore_signal(barrier, inc=1, device_id=(me_group, peer), device_id_type=MESH)
        return carry

    def to_group(step, carry):
        peer = lax.rem(me_group + step, group_count)
        pl.semaphore_signal(barrier, inc=1, device_id=(peer, me_dev), device_id_type=MESH)
        return carry

    lax.fori_loop(1, dev_count, to_dev, 0)
    lax.fori_loop(1, group_count, to_group, 0)
    pl.semaphore_wait(barrier, dev_count + group_count - 2)


def exchange(
    out_ref, out_base, in_ref, in_base, send_sem, recv_sem, dev_count, group_count, me_dev, me_group
):
    def to_dev(step):
        peer = lax.rem(me_dev + step, dev_count)
        return pltpu.make_async_remote_copy(
            src_ref=out_ref.at[out_base + peer],
            dst_ref=in_ref.at[in_base + me_dev],
            send_sem=send_sem.at[step],
            recv_sem=recv_sem.at[step],
            device_id=(me_group, peer),
            device_id_type=MESH,
        )

    def to_group(step):
        peer = lax.rem(me_group + step, group_count)
        return pltpu.make_async_remote_copy(
            src_ref=out_ref.at[out_base + dev_count + peer],
            dst_ref=in_ref.at[in_base + dev_count + me_group],
            send_sem=send_sem.at[dev_count + step],
            recv_sem=recv_sem.at[dev_count + step],
            device_id=(peer, me_dev),
            device_id_type=MESH,
        )

    def start(copy_of):
        def body(step, carry):
            copy_of(step).start()
            return carry

        return body

    def wait(copy_of):
        def body(step, carry):
            copy_of(step).wait()
            return carry

        return body

    lax.fori_loop(1, dev_count, start(to_dev), 0)
    lax.fori_loop(1, group_count, start(to_group), 0)

    def finish():
        lax.fori_loop(1, dev_count, wait(to_dev), 0)
        lax.fori_loop(1, group_count, wait(to_group), 0)

    return finish


def picks_of_peers(pick_ref, pairs_ref, dev_count, group_count, me_group, me_dev):
    return [
        jnp.where(me_dev == e, -1, pick_of_dev(pick_ref, e, me_dev)) for e in range(dev_count)
    ] + [
        jnp.where(me_group == e, -1, pick_of_group(pairs_ref, dev_count, e, me_group, me_dev))
        for e in range(group_count)
    ]


def finish_kernel(
    dev_count, group_count, pick_ref, pairs_ref, count_ref, part_ref, tgt_logw_ref, src_ref,
    src_logw_ref, fs_ref, tab_ref,
    pot_ref, map_ref, tgt_pot_ref,
    inbox, outbox, dual_ref, inbox2, outbox2, kept, fs_col, acc, wts, col_sum,
    send_a, recv_a, send_b, recv_b, send_c, recv_c,
):
    me_group, me_dev = lax.axis_index("group"), lax.axis_index("dev")
    myself = me_group * dev_count + me_dev
    blocks, rows = BLK_DEV, src_ref.shape[1]
    scale = LOG2E / math.sqrt(EMB)
    position_of = functools.partial(table_position, pairs_ref, dev_count, myself)
    place = (dev_count, group_count, me_dev, me_group)
    greet(*place)
    arrived = exchange(part_ref, blocks, inbox, 0, send_a, recv_a, *place)
    empty = jnp.full(inbox.shape[1:], NEG_FILL, jnp.float32)
    for at in (me_dev, dev_count + me_group):
        inbox[at] = empty
        inbox2[at] = jnp.zeros_like(empty)
        dual_ref[blocks + at] = jnp.zeros_like(empty)
    picks = picks_of_peers(pick_ref, pairs_ref, dev_count, group_count, me_group, me_dev)
    fs_col[...] = as_columns(fs_ref[...] * LOG2E)
    arrived()
    for q in range(blocks):
        terms = [part_ref[q]] + [
            jnp.where(pick == q, inbox[e], NEG_FILL) for e, pick in enumerate(picks)
        ]
        high = functools.reduce(jnp.maximum, terms)
        total = sum(jnp.exp(term - high) for term in terms)
        dual_ref[q] = tgt_logw_ref[q] - (high + jnp.log(total))
    duals = [dual_ref[q] for q in range(blocks)]
    for e, pick in enumerate(picks):
        chosen = duals[0]
        for q in range(1, blocks):
            chosen = jnp.where(pick == q, duals[q], chosen)
        outbox[e] = chosen
    exchange(outbox, 0, dual_ref, blocks, send_b, recv_b, *place)()

    ones = jnp.ones((rows, LANES), jnp.bfloat16)

    @pl.loop(0, blocks)
    def _(blk):
        count = count_ref[myself * blocks + blk]
        for slot in range(SLOTS):
            position = position_of(blk, slot)
            dual = jnp.where(slot < count, dual_ref[position] * LOG2E, NEG_FILL)
            points = tab_ref[position]
            beside = jnp.concatenate([points, ones], axis=1)
            for part in range(rows // LANES):
                span = pl.ds(part * LANES, LANES)
                here = pl.ds(blk * rows + part * LANES, LANES)
                shift = jnp.concatenate([fs_col[here, :]] * (rows // LANES), axis=1)
                plan = jnp.exp2(
                    raw_scores(src_ref[blk, span, :], points) * scale + (dual + shift)
                ).astype(jnp.bfloat16)
                kept[blk * SLOTS + slot, span, :] = plan
                product = jnp.dot(plan, beside, preferred_element_type=jnp.float32)
                acc[here, :] = product if slot == 0 else acc[here, :] + product

    row_sum = as_row(acc[:, LANES:])
    logw = src_logw_ref[...]
    weights = weight_rows(jnp.exp(logw) / row_sum)
    for blk in range(blocks):
        wts[blk] = weights[:, blk * rows : (blk + 1) * rows]

    @pl.loop(0, blocks)
    def _(blk):
        for slot in range(SLOTS):
            col_sum[pl.ds(blk * SLOTS + slot, 1), :] = column_sums(
                wts[blk], kept[blk * SLOTS + slot]
            )

    table, pairs = part_ref.shape[0], blocks * SLOTS
    row_at = lax.broadcasted_iota(jnp.int32, (table, pairs), 0)
    col_at = lax.broadcasted_iota(jnp.int32, (table, pairs), 1)
    into = jnp.full((table, pairs), -1, jnp.int32)
    for blk in range(blocks):
        count = count_ref[myself * blocks + blk]
        for slot in range(SLOTS):
            position = jnp.where(slot < count, position_of(blk, slot), -1)
            into = jnp.where(col_at == blk * SLOTS + slot, position, into)
    gathered = lax.dot_general(
        jnp.where(into == row_at, 1.0, 0.0),
        col_sum[...],
        (((1,), (0,)), ((), ())),
        precision=lax.Precision.HIGHEST,
        preferred_element_type=jnp.float32,
    )
    for e in range(table):
        outbox2[e] = gathered[e : e + 1]
    arrived = exchange(outbox2, blocks, inbox2, 0, send_c, recv_c, *place)
    pot_ref[...] = logw + fs_ref[...] - jnp.log(row_sum)
    for blk in range(blocks):
        span = pl.ds(blk * rows, rows)
        map_ref[blk] = acc[span, :LANES] / acc[span, LANES:]
    arrived()
    for q in range(blocks):
        total = outbox2[q]
        for e, pick in enumerate(picks):
            total = total + jnp.where(pick == q, inbox2[e], 0.0)
        tgt_pot_ref[q] = tgt_logw_ref[q] - jnp.log(total) + dual_ref[q]


def shards(source_points, target_points, source_logw, target_logw, pair_targets, pair_count):
    group_count = lax.axis_size("group")
    dev_count = lax.axis_size("dev")
    group_idx = lax.axis_index("group")
    blocks, rows, slots = BLK_DEV, BLOCK, SLOTS
    table = blocks + dev_count + group_count
    peers = dev_count + group_count
    sources = source_points.reshape(blocks, rows, EMB)
    targets = target_points.reshape(blocks, rows, EMB)
    log_src = source_logw.reshape(1, blocks * rows)
    log_tgt = target_logw.reshape(blocks, 1, rows)

    plane = dev_count * blocks
    named = pair_targets.T
    pick = plane_picks(
        lax.dynamic_slice_in_dim(named, group_idx * plane, plane, 1),
        lax.dynamic_slice_in_dim(pair_count, group_idx * plane, plane, 0),
        group_idx * plane,
        dev_count,
    )

    smem = pl.BlockSpec(memory_space=pltpu.SMEM)
    vmem = pl.BlockSpec(memory_space=pltpu.VMEM)
    anywhere = pl.BlockSpec(memory_space=pl.ANY)
    f32 = jnp.float32
    kept = pltpu.VMEM((blocks * slots, rows, rows), jnp.bfloat16)
    pairs = blocks * slots
    dma = pltpu.SemaphoreType.DMA
    block = (rows, EMB)
    lots = RING * (len(BRANCH) + 1) + group_count - 1 + RING - 1
    delivered = pl.pallas_call(
        functools.partial(deliver_kernel, dev_count, group_count),
        out_shape=jax.ShapeDtypeStruct((table, *block), jnp.bfloat16),
        in_specs=[smem, smem, vmem],
        out_specs=anywhere,
        scratch_shapes=[pltpu.VMEM((blocks, *block), jnp.bfloat16)] * 3
        + [pltpu.VMEM((RING, *block), jnp.bfloat16)] * 2
        + [
            pltpu.VMEM((lots, *block), jnp.bfloat16),
            dma((6,)),
            dma((6,)),
            dma((lots,)),
            dma((dev_count,)),
            dma((2 * RING,)),
            dma((2 * RING,)),
            dma((group_count,)),
            dma((1,)),
        ],
        compiler_params=pltpu.CompilerParams(
            collective_id=2, has_side_effects=True, vmem_limit_bytes=VMEM_LIMIT
        ),
        name="deliver_blocks",
    )(pick, named, targets)

    first_source, part = pl.pallas_call(
        functools.partial(first_kernel, dev_count),
        out_shape=(
            jax.ShapeDtypeStruct((1, blocks * rows), f32),
            jax.ShapeDtypeStruct((table, 1, rows), f32),
        ),
        in_specs=[smem, smem, vmem, vmem, vmem],
        out_specs=(vmem, vmem),
        scratch_shapes=[
            kept,
            pltpu.VMEM((blocks * rows, LANES), f32),
            pltpu.VMEM((blocks, 16, rows), jnp.bfloat16),
            pltpu.VMEM((1, rows), f32),
            pltpu.VMEM((rows, LANES), f32),
            pltpu.VMEM((rows, LANES), f32),
        ],
        compiler_params=pltpu.CompilerParams(vmem_limit_bytes=PAIR_LIMIT),
        cost_estimate=pl.CostEstimate(
            flops=4 * pairs * rows * rows * EMB, bytes_accessed=6 * 2**20, transcendentals=pairs * rows * rows
        ),
        name="first_pass",
    )(named, pair_count, sources, log_src, delivered)

    row = pltpu.VMEM((peers, 1, rows), f32)
    full = pltpu.VMEM((table, 1, rows), f32)
    potential, mapped, target_potential = pl.pallas_call(
        functools.partial(finish_kernel, dev_count, group_count),
        out_shape=(
            jax.ShapeDtypeStruct((1, blocks * rows), f32),
            jax.ShapeDtypeStruct((blocks, rows, EMB), f32),
            jax.ShapeDtypeStruct((blocks, 1, rows), f32),
        ),
        in_specs=[smem, smem, smem, vmem, vmem, vmem, vmem, vmem, vmem],
        out_specs=(vmem, vmem, vmem),
        scratch_shapes=[
            row,
            row,
            full,
            row,
            full,
            kept,
            pltpu.VMEM((blocks * rows, LANES), f32),
            pltpu.VMEM((blocks * rows, 2 * LANES), f32),
            pltpu.VMEM((blocks, 16, rows), jnp.bfloat16),
            pltpu.VMEM((pairs, rows), f32),
        ]
        + [dma((peers,))] * 6,
        compiler_params=pltpu.CompilerParams(
            collective_id=0, has_side_effects=True, vmem_limit_bytes=PAIR_LIMIT
        ),
        cost_estimate=pl.CostEstimate(
            flops=8 * pairs * rows * rows * EMB, bytes_accessed=7 * 2**20, transcendentals=pairs * rows * rows
        ),
        name="finish",
    )(
        pick, named, pair_count, part, log_tgt, sources, log_src, first_source, delivered
    )
    return (
        potential.reshape(blocks * rows),
        target_potential.reshape(blocks * rows),
        mapped.reshape(blocks * rows, EMB),
    )


def solution(mesh):
    return jax.shard_map(
        shards,
        mesh=mesh,
        in_specs=(
            P(("group", "dev"), None),
            P(("group", "dev"), None),
            P(("group", "dev")),
            P(("group", "dev")),
            P(),
            P(),
        ),
        out_specs=(P(("group", "dev")), P(("group", "dev")), P(("group", "dev"), None)),
        check_vma=False,
    )
```

```python
import functools
import math

import jax
import jax.numpy as jnp
from jax import lax
from jax.experimental import pallas as pl
from jax.experimental.pallas import tpu as pltpu
from jax.sharding import PartitionSpec as P

BLOCK = 512
EMB = 128
BLK_DEV = 4
SLOTS = 8
LANES = 128
NEG_FILL = -1e30
LOG2E = math.log2(math.e)
ROW_LOW, ROW_HIGH, COL_LOW = 1e-6, 1e30, 1e-22
MESH = pl.DeviceIdType.MESH
VMEM_LIMIT = 20 * 2**20
PAIR_LIMIT = 28 * 2**20
FINISH_LIMIT = 52 * 2**20
PREPARED = 3


RING = 4
TRUNK = (0, 3, 1, 2)
BRANCH = ((2, 0), (2, 1), (1, 0), (1, 1), (3, 0), (3, 1))


def plane_picks(targets, counts, first, sources):
    slots = lax.broadcasted_iota(jnp.int32, targets.shape, 0)
    named = jnp.where(slots < counts[None, :], targets - first, -1)[:, None, :]
    source = lax.broadcasted_iota(jnp.int32, (1, sources, 1), 1)
    return jnp.max(jnp.where((named >> 2) == source, named & 3, -1), axis=0)


def pick_of_dev(pick_ref, taker, source):
    first = pick_ref[source, BLK_DEV * taker]
    for row in range(1, BLK_DEV):
        first = jnp.maximum(first, pick_ref[source, BLK_DEV * taker + row])
    return first


def pick_of_group(pairs_ref, dev_count, peer, me_group, me_dev):
    base = (peer * dev_count + me_dev) * BLK_DEV
    mine = me_group * dev_count + me_dev
    found = jnp.int32(-1)
    for row in range(BLK_DEV):
        name = pairs_ref[1, base + row]
        found = jnp.maximum(found, jnp.where(name // BLK_DEV == mine, name % BLK_DEV, -1))
    return found


def table_position(pairs_ref, dev_count, myself, blk, slot):
    name = pairs_ref[slot, myself * BLK_DEV + blk]
    owner = name // BLK_DEV
    group = owner // dev_count
    away = jnp.where(
        group == myself // dev_count, owner % dev_count, dev_count + group
    )
    return jnp.where(owner == myself, name % BLK_DEV, BLK_DEV + away)


def raw_scores(left, right):
    return lax.dot_general(left, right, (((1,), (1,)), ((), ())), preferred_element_type=jnp.float32)


def as_columns(row):
    return jnp.transpose(jnp.broadcast_to(row, (LANES, row.shape[1])))


def as_row(columns):
    return jnp.transpose(columns)[0:1]


def lane_sums(columns):
    high = columns.astype(jnp.bfloat16)
    low = (columns - high.astype(jnp.float32)).astype(jnp.bfloat16)
    parts = jnp.concatenate([high, low], axis=1)
    return raw_scores(jnp.ones((16, parts.shape[1]), jnp.bfloat16), parts)[0:1]


def weight_rows(weights):
    high = weights.astype(jnp.bfloat16).astype(jnp.float32)
    rest = weights - high
    middle = rest.astype(jnp.bfloat16).astype(jnp.float32)
    low = rest - middle
    at = lax.broadcasted_iota(jnp.int32, (16, weights.shape[1]), 0)
    zero = jnp.zeros((16, weights.shape[1]), jnp.float32)
    rows = jnp.where(at == 0, high, jnp.where(at == 1, middle, jnp.where(at == 2, low, zero)))
    return rows.astype(jnp.bfloat16)


def by_width(count, work):
    @pl.when(count <= SLOTS // 2)
    def _():
        work(SLOTS // 2)

    @pl.when(count > SLOTS // 2)
    def _():
        work(SLOTS)


def column_sums(weights, kernel):
    return jnp.sum(
        jnp.dot(weights, kernel, preferred_element_type=jnp.float32), axis=0, keepdims=True
    )


def first_kernel(
    dev_count, pairs_ref, count_ref, src_ref, logw_ref, tab_ref,
    fs_ref, part_ref,
    kept, row_acc, wts, fine_ref, col_max, col_total,
):
    factor = 1.0 / math.sqrt(EMB)
    scale = factor * LOG2E
    rows = src_ref.shape[1]
    myself = lax.axis_index("group") * dev_count + lax.axis_index("dev")
    position_of = functools.partial(table_position, pairs_ref, dev_count, myself)

    @pl.loop(0, BLK_DEV)
    def _(blk):
        count = count_ref[myself * BLK_DEV + blk]

        def row_work(width):
            totals = jnp.zeros((rows, LANES), jnp.float32)
            for slot in range(width):
                points = tab_ref[position_of(blk, slot)]
                kern = jnp.exp2(raw_scores(src_ref[blk], points) * scale)
                kept[blk * SLOTS + slot] = kern.astype(jnp.bfloat16)
                total = kern[:, :LANES]
                for lane in range(1, rows // LANES):
                    total = total + kern[:, lane * LANES : (lane + 1) * LANES]
                totals = totals + jnp.where(slot < count, total, 0.0)
            row_acc[pl.ds(blk * rows, rows), :] = totals

        by_width(count, row_work)

    row_sum = lane_sums(row_acc[...])
    logw = logw_ref[...]
    fs_ref[...] = logw - jnp.log(row_sum)
    weights = weight_rows(jnp.exp(logw) / row_sum)
    row_fine = jnp.where((row_sum >= ROW_LOW) & (row_sum <= ROW_HIGH), 1.0, 0.0)
    fine = jnp.ones((1, rows), jnp.float32)
    for blk in range(BLK_DEV):
        span = slice(blk * rows, (blk + 1) * rows)
        wts[blk] = weights[:, span]
        fine = jnp.minimum(fine, row_fine[:, span])
    fine_ref[...] = fine
    part_ref[...] = jnp.zeros_like(part_ref)

    @pl.loop(0, BLK_DEV)
    def _(blk):
        count = count_ref[myself * BLK_DEV + blk]

        def column_work(width):
            fine = fine_ref[...]
            for slot in range(width):
                here = column_sums(wts[blk], kept[blk * SLOTS + slot])
                part_ref[position_of(blk, slot)] += jnp.where(slot < count, here, 0.0)
                fine = jnp.minimum(
                    fine, jnp.where((here >= COL_LOW) | (slot >= count), 1.0, 0.0)
                )
            fine_ref[...] = fine

        by_width(count, column_work)

    sums = part_ref[...]
    part_ref[...] = jnp.where(sums > 0.0, jnp.log(jnp.where(sums > 0.0, sums, 1.0)), NEG_FILL)

    @pl.when(jnp.min(fine_ref[...]) < 0.5)
    def _():
        part_ref[...] = jnp.full_like(part_ref, NEG_FILL)

        @pl.loop(0, BLK_DEV)
        def _(blk):
            count = count_ref[myself * BLK_DEV + blk]
            col_max[...] = jnp.full_like(col_max, NEG_FILL)
            col_total[...] = jnp.zeros_like(col_total)

            @pl.loop(0, count)
            def _(slot):
                points = tab_ref[position_of(blk, slot)]
                for part in range(rows // LANES):
                    span = pl.ds(part * LANES, LANES)
                    scores = raw_scores(src_ref[blk, span, :], points) * factor
                    old = col_max[span, :]
                    new = jnp.maximum(old, jnp.max(scores, axis=1, keepdims=True))
                    here = jnp.sum(jnp.exp(scores - new[:, 0:1]), axis=1, keepdims=True)
                    col_total[span, :] = col_total[span, :] * jnp.exp(old - new) + here
                    col_max[span, :] = new

            lse = col_max[...] + jnp.log(col_total[...])
            row_acc[pl.ds(blk * rows, rows), :] = lse

            @pl.loop(0, count)
            def _(slot):
                position = position_of(blk, slot)
                points = tab_ref[position]
                logw_col = as_columns(logw_ref[:, pl.ds(pl.multiple_of(blk * rows, rows), rows)])
                source = logw_col - row_acc[pl.ds(blk * rows, rows), :]
                col_max[...] = source
                high = jnp.full((1, rows), NEG_FILL, jnp.float32)
                total = jnp.zeros((1, rows), jnp.float32)
                for part in range(rows // LANES):
                    span = pl.ds(part * LANES, LANES)
                    scores = raw_scores(src_ref[blk, span, :], points) * factor
                    scores = scores + col_max[span, 0:1]
                    new = jnp.maximum(high, jnp.max(scores, axis=0, keepdims=True))
                    total = total * jnp.exp(high - new) + jnp.sum(
                        jnp.exp(scores - new), axis=0, keepdims=True
                    )
                    high = new
                here = high + jnp.log(total)
                old = part_ref[position]
                new = jnp.maximum(old, here)
                part_ref[position] = new + jnp.log(jnp.exp(old - new) + jnp.exp(here - new))

        fs_ref[...] = logw_ref[...] - as_row(row_acc[...])


def deliver_kernel(
    dev_count, group_count, pick_ref, pairs_ref, tgt_ref, tab_ref,
    prev_buf, next_buf, far_buf, relay_up, relay_down, stage,
    trunk_send, trunk_recv, stage_send, tab_recv, relay_recv, fwd_send, grp_recv, own_sem,
):
    me_group, me_dev = lax.axis_index("group"), lax.axis_index("dev")
    core = lax.rem(me_dev, 2)
    at_x, at_z = lax.rem(me_dev // 2, RING), me_dev // (2 * RING)
    half = BLK_DEV // 2

    def device(along, across, to_core):
        dz = along + core * (across - along)
        dx = across + core * (along - across)
        return (lax.rem(at_z + dz, RING) * RING + lax.rem(at_x + dx, RING)) * 2 + to_core

    def send(src, dst, send_sem, recv_sem, dev, group=None):
        return pltpu.make_async_remote_copy(
            src_ref=src,
            dst_ref=dst,
            send_sem=send_sem,
            recv_sem=recv_sem,
            device_id=(me_group if group is None else group, dev),
            device_id_type=MESH,
        )

    barrier = pltpu.get_barrier_semaphore()
    near = [
        device(i, j, cc) for i, j in ((1, 0), (3, 0), (0, 1), (0, 3)) for cc in (0, 1)
    ] + [device(0, 0, 1 - core)]
    for dev in near:
        pl.semaphore_signal(barrier, inc=1, device_id=(me_group, dev), device_id_type=MESH)
    for step in range(1, group_count):
        pl.semaphore_signal(
            barrier,
            inc=1,
            device_id=(lax.rem(me_group + step, group_count), me_dev),
            device_id_type=MESH,
        )
    pl.semaphore_wait(barrier, len(near) + group_count - 1)

    low, top = pl.ds(0, half), pl.ds(half, half)
    ahead, behind = device(1, 0, core), device(3, 0, core)

    def trunk(n, src, dst, span, dev):
        return send(src.at[span], dst.at[span], trunk_send.at[n], trunk_recv.at[n], dev)

    trunks = [
        trunk(0, tgt_ref, prev_buf, low, ahead),
        trunk(1, tgt_ref, next_buf, top, behind),
        trunk(2, tgt_ref, prev_buf, top, ahead),
        trunk(3, tgt_ref, next_buf, low, behind),
        trunk(4, prev_buf, far_buf, low, ahead),
        trunk(5, next_buf, far_buf, top, behind),
    ]
    for n in range(4):
        trunks[n].start()
    sent = []

    def branch(k, buf):
        source = device(TRUNK[k], 0, core)
        for n, (across, to_core) in enumerate(BRANCH + ((0, 1 - core),)):
            taker = device(0, across, to_core)
            at = k * (len(BRANCH) + 1) + n
            stage[at] = buf[jnp.maximum(pick_of_dev(pick_ref, taker, source), 0)]
            if across == 2:
                relay, over = ((relay_up, 1), (relay_down, 3))[to_core]
                which = relay_recv.at[to_core * RING + k]
                copy = send(
                    stage.at[at], relay.at[k], stage_send.at[at], which, device(0, over, core)
                )
            else:
                copy = send(
                    stage.at[at],
                    tab_ref.at[BLK_DEV + source],
                    stage_send.at[at],
                    tab_recv.at[source],
                    taker,
                )
            copy.start()
            sent.append(copy)
        if k > 0:
            at = RING * (len(BRANCH) + 1) + group_count - 1 + k - 1
            stage[at] = buf[jnp.maximum(pick_of_dev(pick_ref, me_dev, source), 0)]
            pltpu.make_async_copy(
                stage.at[at], tab_ref.at[BLK_DEV + source], tab_recv.at[source]
            ).start()

    def pass_on(k):
        for way, (relay, back, over) in enumerate(((relay_up, 3, 1), (relay_down, 1, 3))):
            source = device(TRUNK[k], back, core)
            at = way * RING + k
            copy = send(
                relay.at[k],
                tab_ref.at[BLK_DEV + source],
                fwd_send.at[at],
                tab_recv.at[source],
                device(0, over, way),
            )
            send(
                relay.at[k], relay.at[k], fwd_send.at[at], relay_recv.at[at], ahead
            ).wait_recv()
            copy.start()
            sent.append(copy)

    branch(0, tgt_ref)
    own = pltpu.make_async_copy(tgt_ref, tab_ref.at[pl.ds(0, BLK_DEV)], own_sem.at[0])
    own.start()
    from_groups = []
    for step in range(1, group_count):
        peer = lax.rem(me_group + step, group_count)
        at = RING * (len(BRANCH) + 1) + step - 1
        pick = pick_of_group(pairs_ref, dev_count, peer, me_group, me_dev)
        stage[at] = tgt_ref[jnp.maximum(pick, 0)]
        copy = send(
            stage.at[at],
            tab_ref.at[BLK_DEV + dev_count + me_group],
            stage_send.at[at],
            grp_recv.at[step],
            me_dev,
            peer,
        )
        copy.start()
        sent.append(copy)
        from_groups.append(copy)
    trunks[0].wait_recv()
    trunks[4].start()
    trunks[1].wait_recv()
    trunks[5].start()
    trunks[2].wait_recv()
    branch(1, prev_buf)
    trunks[3].wait_recv()
    branch(2, next_buf)
    pass_on(0)
    trunks[4].wait_recv()
    trunks[5].wait_recv()
    branch(3, far_buf)
    pass_on(1)
    pass_on(2)
    pass_on(3)
    for copy in sent + trunks:
        copy.wait_send()
    for step in range(1, dev_count):
        source = lax.rem(me_dev + step, dev_count)
        send(
            stage.at[0], tab_ref.at[BLK_DEV + source], stage_send.at[0], tab_recv.at[source], ahead
        ).wait_recv()
    for copy in from_groups:
        copy.wait_recv()
    own.wait()


def greet(dev_count, group_count, me_dev, me_group):
    barrier = pltpu.get_barrier_semaphore()

    def to_dev(step, carry):
        peer = lax.rem(me_dev + step, dev_count)
        pl.semaphore_signal(barrier, inc=1, device_id=(me_group, peer), device_id_type=MESH)
        return carry

    def to_group(step, carry):
        peer = lax.rem(me_group + step, group_count)
        pl.semaphore_signal(barrier, inc=1, device_id=(peer, me_dev), device_id_type=MESH)
        return carry

    lax.fori_loop(1, dev_count, to_dev, 0)
    lax.fori_loop(1, group_count, to_group, 0)
    pl.semaphore_wait(barrier, dev_count + group_count - 2)


def exchange(
    out_ref, out_base, in_ref, in_base, send_sem, recv_sem, dev_count, group_count, me_dev, me_group
):
    def to_dev(step):
        peer = lax.rem(me_dev + step, dev_count)
        return pltpu.make_async_remote_copy(
            src_ref=out_ref.at[out_base + peer],
            dst_ref=in_ref.at[in_base + me_dev],
            send_sem=send_sem.at[step],
            recv_sem=recv_sem.at[step],
            device_id=(me_group, peer),
            device_id_type=MESH,
        )

    def to_group(step):
        peer = lax.rem(me_group + step, group_count)
        return pltpu.make_async_remote_copy(
            src_ref=out_ref.at[out_base + dev_count + peer],
            dst_ref=in_ref.at[in_base + dev_count + me_group],
            send_sem=send_sem.at[dev_count + step],
            recv_sem=recv_sem.at[dev_count + step],
            device_id=(peer, me_dev),
            device_id_type=MESH,
        )

    def start(copy_of):
        def body(step, carry):
            copy_of(step).start()
            return carry

        return body

    def wait(copy_of):
        def body(step, carry):
            copy_of(step).wait()
            return carry

        return body

    lax.fori_loop(1, dev_count, start(to_dev), 0)
    lax.fori_loop(1, group_count, start(to_group), 0)

    def finish():
        lax.fori_loop(1, dev_count, wait(to_dev), 0)
        lax.fori_loop(1, group_count, wait(to_group), 0)

    return finish


def picks_of_peers(pick_ref, pairs_ref, dev_count, group_count, me_group, me_dev):
    return [
        jnp.where(me_dev == e, -1, pick_of_dev(pick_ref, e, me_dev)) for e in range(dev_count)
    ] + [
        jnp.where(me_group == e, -1, pick_of_group(pairs_ref, dev_count, e, me_group, me_dev))
        for e in range(group_count)
    ]


def finish_kernel(
    dev_count, group_count, pick_ref, pairs_ref, count_ref, part_ref, tgt_logw_ref, src_ref,
    src_logw_ref, fs_ref, tab_ref,
    pot_ref, map_ref, tgt_pot_ref,
    inbox, outbox, dual_ref, inbox2, outbox2, kept, ready, fs_col, acc, wts, col_sum,
    send_a, recv_a, send_b, recv_b, send_c, recv_c,
):
    me_group, me_dev = lax.axis_index("group"), lax.axis_index("dev")
    myself = me_group * dev_count + me_dev
    blocks, rows = BLK_DEV, src_ref.shape[1]
    scale = LOG2E / math.sqrt(EMB)
    position_of = functools.partial(table_position, pairs_ref, dev_count, myself)
    place = (dev_count, group_count, me_dev, me_group)
    greet(*place)
    arrived = exchange(part_ref, blocks, inbox, 0, send_a, recv_a, *place)
    empty = jnp.full(inbox.shape[1:], NEG_FILL, jnp.float32)
    for at in (me_dev, dev_count + me_group):
        inbox[at] = empty
        inbox2[at] = jnp.zeros_like(empty)
        dual_ref[blocks + at] = jnp.zeros_like(empty)
    picks = picks_of_peers(pick_ref, pairs_ref, dev_count, group_count, me_group, me_dev)
    fs_col[...] = as_columns(fs_ref[...] * LOG2E)

    def exponent(blk, part, points):
        span = pl.ds(part * LANES, LANES)
        shift = fs_col[pl.ds(blk * rows + part * LANES, LANES), :]
        shift = jnp.concatenate([shift] * (rows // LANES), axis=1)
        return raw_scores(src_ref[blk, span, :], points) * scale + shift

    def prepare(first, last):
        @pl.loop(first, last)
        def _(blk):
            for slot in range(SLOTS):
                points = tab_ref[position_of(blk, slot)]
                for part in range(rows // LANES):
                    span = pl.ds(part * LANES, LANES)
                    ready[blk * SLOTS + slot, span, :] = exponent(blk, part, points)

    prepare(0, (PREPARED + 1) // 2)
    arrived()
    for q in range(blocks):
        terms = [part_ref[q]] + [
            jnp.where(pick == q, inbox[e], NEG_FILL) for e, pick in enumerate(picks)
        ]
        high = functools.reduce(jnp.maximum, terms)
        total = sum(jnp.exp(term - high) for term in terms)
        dual_ref[q] = tgt_logw_ref[q] - (high + jnp.log(total))
    duals = [dual_ref[q] for q in range(blocks)]
    for e, pick in enumerate(picks):
        chosen = duals[0]
        for q in range(1, blocks):
            chosen = jnp.where(pick == q, duals[q], chosen)
        outbox[e] = chosen
    arrived = exchange(outbox, 0, dual_ref, blocks, send_b, recv_b, *place)
    prepare((PREPARED + 1) // 2, PREPARED)
    arrived()
    ones = jnp.ones((rows, LANES), jnp.bfloat16)

    def plans(blk, exponent_of):
        count = count_ref[myself * blocks + blk]
        for slot in range(SLOTS):
            position = position_of(blk, slot)
            dual = jnp.where(slot < count, dual_ref[position] * LOG2E, NEG_FILL)
            points = tab_ref[position]
            beside = jnp.concatenate([points, ones], axis=1)
            for part in range(rows // LANES):
                span = pl.ds(part * LANES, LANES)
                here = pl.ds(blk * rows + part * LANES, LANES)
                plan = jnp.exp2(exponent_of(slot, part, points) + dual).astype(jnp.bfloat16)
                kept[blk * SLOTS + slot, span, :] = plan
                product = jnp.dot(plan, beside, preferred_element_type=jnp.float32)
                acc[here, :] = product if slot == 0 else acc[here, :] + product

    @pl.loop(0, PREPARED)
    def _(blk):
        plans(
            blk,
            lambda slot, part, points: ready[
                blk * SLOTS + slot, pl.ds(part * LANES, LANES), :
            ],
        )

    for blk in range(PREPARED, blocks):
        plans(blk, lambda slot, part, points: exponent(blk, part, points))

    row_sum = lane_sums(acc[:, LANES:]) * (1.0 / LANES)
    logw = src_logw_ref[...]
    weights = weight_rows(jnp.exp(logw) / row_sum)
    for blk in range(blocks):
        wts[blk] = weights[:, blk * rows : (blk + 1) * rows]

    @pl.loop(0, blocks)
    def _(blk):
        for slot in range(SLOTS):
            col_sum[pl.ds(blk * SLOTS + slot, 1), :] = column_sums(
                wts[blk], kept[blk * SLOTS + slot]
            )

    table, pairs = part_ref.shape[0], blocks * SLOTS
    row_at = lax.broadcasted_iota(jnp.int32, (table, pairs), 0)
    col_at = lax.broadcasted_iota(jnp.int32, (table, pairs), 1)
    into = jnp.full((table, pairs), -1, jnp.int32)
    for blk in range(blocks):
        count = count_ref[myself * blocks + blk]
        for slot in range(SLOTS):
            position = jnp.where(slot < count, position_of(blk, slot), -1)
            into = jnp.where(col_at == blk * SLOTS + slot, position, into)
    gathered = lax.dot_general(
        jnp.where(into == row_at, 1.0, 0.0),
        col_sum[...],
        (((1,), (0,)), ((), ())),
        precision=lax.Precision.HIGHEST,
        preferred_element_type=jnp.float32,
    )
    for e in range(table):
        outbox2[e] = gathered[e : e + 1]
    arrived = exchange(outbox2, blocks, inbox2, 0, send_c, recv_c, *place)
    pot_ref[...] = logw + fs_ref[...] - jnp.log(row_sum)
    for blk in range(blocks):
        span = pl.ds(blk * rows, rows)
        map_ref[blk] = acc[span, :LANES] / acc[span, LANES:]
    arrived()
    for q in range(blocks):
        total = outbox2[q]
        for e, pick in enumerate(picks):
            total = total + jnp.where(pick == q, inbox2[e], 0.0)
        tgt_pot_ref[q] = tgt_logw_ref[q] - jnp.log(total) + dual_ref[q]


def shards(source_points, target_points, source_logw, target_logw, pair_targets, pair_count):
    group_count = lax.axis_size("group")
    dev_count = lax.axis_size("dev")
    group_idx = lax.axis_index("group")
    blocks, rows, slots = BLK_DEV, BLOCK, SLOTS
    table = blocks + dev_count + group_count
    peers = dev_count + group_count
    sources = source_points.reshape(blocks, rows, EMB)
    targets = target_points.reshape(blocks, rows, EMB)
    log_src = source_logw.reshape(1, blocks * rows)
    log_tgt = target_logw.reshape(blocks, 1, rows)

    plane = dev_count * blocks
    named = pair_targets.T
    pick = plane_picks(
        lax.dynamic_slice_in_dim(named, group_idx * plane, plane, 1),
        lax.dynamic_slice_in_dim(pair_count, group_idx * plane, plane, 0),
        group_idx * plane,
        dev_count,
    )

    smem = pl.BlockSpec(memory_space=pltpu.SMEM)
    vmem = pl.BlockSpec(memory_space=pltpu.VMEM)
    anywhere = pl.BlockSpec(memory_space=pl.ANY)
    f32 = jnp.float32
    kept = pltpu.VMEM((blocks * slots, rows, rows), jnp.bfloat16)
    pairs = blocks * slots
    dma = pltpu.SemaphoreType.DMA
    block = (rows, EMB)
    lots = RING * (len(BRANCH) + 1) + group_count - 1 + RING - 1
    delivered = pl.pallas_call(
        functools.partial(deliver_kernel, dev_count, group_count),
        out_shape=jax.ShapeDtypeStruct((table, *block), jnp.bfloat16),
        in_specs=[smem, smem, vmem],
        out_specs=anywhere,
        scratch_shapes=[pltpu.VMEM((blocks, *block), jnp.bfloat16)] * 3
        + [pltpu.VMEM((RING, *block), jnp.bfloat16)] * 2
        + [
            pltpu.VMEM((lots, *block), jnp.bfloat16),
            dma((6,)),
            dma((6,)),
            dma((lots,)),
            dma((dev_count,)),
            dma((2 * RING,)),
            dma((2 * RING,)),
            dma((group_count,)),
            dma((1,)),
        ],
        compiler_params=pltpu.CompilerParams(
            collective_id=2, has_side_effects=True, vmem_limit_bytes=VMEM_LIMIT
        ),
        name="deliver_blocks",
    )(pick, named, targets)

    first_source, part = pl.pallas_call(
        functools.partial(first_kernel, dev_count),
        out_shape=(
            jax.ShapeDtypeStruct((1, blocks * rows), f32),
            jax.ShapeDtypeStruct((table, 1, rows), f32),
        ),
        in_specs=[smem, smem, vmem, vmem, vmem],
        out_specs=(vmem, vmem),
        scratch_shapes=[
            kept,
            pltpu.VMEM((blocks * rows, LANES), f32),
            pltpu.VMEM((blocks, 16, rows), jnp.bfloat16),
            pltpu.VMEM((1, rows), f32),
            pltpu.VMEM((rows, LANES), f32),
            pltpu.VMEM((rows, LANES), f32),
        ],
        compiler_params=pltpu.CompilerParams(vmem_limit_bytes=PAIR_LIMIT),
        cost_estimate=pl.CostEstimate(
            flops=4 * pairs * rows * rows * EMB, bytes_accessed=6 * 2**20, transcendentals=pairs * rows * rows
        ),
        name="first_pass",
    )(named, pair_count, sources, log_src, delivered)

    row = pltpu.VMEM((peers, 1, rows), f32)
    full = pltpu.VMEM((table, 1, rows), f32)
    potential, mapped, target_potential = pl.pallas_call(
        functools.partial(finish_kernel, dev_count, group_count),
        out_shape=(
            jax.ShapeDtypeStruct((1, blocks * rows), f32),
            jax.ShapeDtypeStruct((blocks, rows, EMB), f32),
            jax.ShapeDtypeStruct((blocks, 1, rows), f32),
        ),
        in_specs=[smem, smem, smem, vmem, vmem, vmem, vmem, vmem, vmem],
        out_specs=(vmem, vmem, vmem),
        scratch_shapes=[
            row,
            row,
            full,
            row,
            full,
            kept,
            pltpu.VMEM((PREPARED * slots, rows, rows), f32),
            pltpu.VMEM((blocks * rows, LANES), f32),
            pltpu.VMEM((blocks * rows, 2 * LANES), f32),
            pltpu.VMEM((blocks, 16, rows), jnp.bfloat16),
            pltpu.VMEM((pairs, rows), f32),
        ]
        + [dma((peers,))] * 6,
        compiler_params=pltpu.CompilerParams(
            collective_id=0, has_side_effects=True, vmem_limit_bytes=FINISH_LIMIT
        ),
        cost_estimate=pl.CostEstimate(
            flops=8 * pairs * rows * rows * EMB, bytes_accessed=7 * 2**20, transcendentals=pairs * rows * rows
        ),
        name="finish",
    )(
        pick, named, pair_count, part, log_tgt, sources, log_src, first_source, delivered
    )
    return (
        potential.reshape(blocks * rows),
        target_potential.reshape(blocks * rows),
        mapped.reshape(blocks * rows, EMB),
    )


def solution(mesh):
    return jax.shard_map(
        shards,
        mesh=mesh,
        in_specs=(
            P(("group", "dev"), None),
            P(("group", "dev"), None),
            P(("group", "dev")),
            P(("group", "dev")),
            P(),
            P(),
        ),
        out_specs=(P(("group", "dev")), P(("group", "dev")), P(("group", "dev"), None)),
        check_vma=False,
    )
```

```python
import functools
import math

import jax
import jax.numpy as jnp
from jax import lax
from jax.experimental import pallas as pl
from jax.experimental.pallas import tpu as pltpu
from jax.sharding import PartitionSpec as P

BLOCK = 512
EMB = 128
BLK_DEV = 4
SLOTS = 8
LANES = 128
NEG_FILL = -1e30
LOG2E = math.log2(math.e)
ROW_LOW, ROW_HIGH, COL_LOW = 1e-6, 1e30, 1e-22
MESH = pl.DeviceIdType.MESH
VMEM_LIMIT = 20 * 2**20
PAIR_LIMIT = 28 * 2**20
FINISH_LIMIT = 52 * 2**20
PREPARED = 3


RING = 4
TRUNK = (0, 3, 1, 2)
BRANCH = ((2, 0), (2, 1), (1, 0), (1, 1), (3, 0), (3, 1))


def all_picks(pairs_ref, dev_count, group_count, me_group, me_dev):
    plane = dev_count * BLK_DEV
    first = me_group * plane
    span = pl.ds(pl.multiple_of(first, plane), plane)
    slots = lax.broadcasted_iota(jnp.int32, (SLOTS, plane), 0)
    name, counts = pairs_ref[0:SLOTS, span], pairs_ref[SLOTS : SLOTS + 1, span]
    named = jnp.where(slots < counts, name - first, -1)
    source = lax.broadcasted_iota(jnp.int32, (dev_count, plane), 0)
    picks = jnp.full((dev_count, plane), -1, jnp.int32)
    for slot in range(SLOTS):
        here = named[slot : slot + 1]
        picks = jnp.maximum(picks, jnp.where((here >> 2) == source, here & 3, -1))
    away = pairs_ref[1:2, :]
    away = jnp.where((away >> 2) == me_group * dev_count + me_dev, away & 3, -1)
    away = [away[:, g * plane : (g + 1) * plane] for g in range(group_count)]
    bits = dev_count.bit_length() - 1
    owner = name >> 2
    there = jnp.where(
        (owner >> bits) == me_group, owner & (dev_count - 1), dev_count + (owner >> bits)
    )
    places = jnp.where(owner == me_group * dev_count + me_dev, name & 3, BLK_DEV + there)
    return picks, away, places, counts


def pick_of_dev(pick_ref, taker, source):
    first = pick_ref[source, BLK_DEV * taker]
    for row in range(1, BLK_DEV):
        first = jnp.maximum(first, pick_ref[source, BLK_DEV * taker + row])
    return first


def pick_of_group(pick_ref, dev_count, peer, me_dev):
    return pick_of_dev(pick_ref, me_dev, dev_count + peer)


def slot_reader(place_ref, me_dev):
    def position_of(blk, slot):
        return place_ref[slot, me_dev * BLK_DEV + blk]

    def count_of(blk):
        return place_ref[SLOTS, me_dev * BLK_DEV + blk]

    return position_of, count_of


def raw_scores(left, right):
    return lax.dot_general(left, right, (((1,), (1,)), ((), ())), preferred_element_type=jnp.float32)


def as_columns(row):
    return jnp.transpose(jnp.broadcast_to(row, (LANES, row.shape[1])))


def as_row(columns):
    return jnp.transpose(columns)[0:1]


def lane_sums(columns):
    high = columns.astype(jnp.bfloat16)
    low = (columns - high.astype(jnp.float32)).astype(jnp.bfloat16)
    parts = jnp.concatenate([high, low], axis=1)
    return raw_scores(jnp.ones((16, parts.shape[1]), jnp.bfloat16), parts)[0:1]


def weight_rows(weights):
    high = weights.astype(jnp.bfloat16).astype(jnp.float32)
    rest = weights - high
    middle = rest.astype(jnp.bfloat16).astype(jnp.float32)
    low = rest - middle
    at = lax.broadcasted_iota(jnp.int32, (16, weights.shape[1]), 0)
    zero = jnp.zeros((16, weights.shape[1]), jnp.float32)
    rows = jnp.where(at == 0, high, jnp.where(at == 1, middle, jnp.where(at == 2, low, zero)))
    return rows.astype(jnp.bfloat16)


def by_width(count, work):
    @pl.when(count <= SLOTS // 2)
    def _():
        work(SLOTS // 2)

    @pl.when(count > SLOTS // 2)
    def _():
        work(SLOTS)


def column_sums(weights, kernel):
    return jnp.sum(
        jnp.dot(weights, kernel, preferred_element_type=jnp.float32), axis=0, keepdims=True
    )


def first_kernel(
    place_ref, src_ref, logw_ref, tab_ref,
    fs_ref, part_ref,
    kept, row_acc, wts, fine_ref, col_max, col_total,
):
    factor = 1.0 / math.sqrt(EMB)
    scale = factor * LOG2E
    rows = src_ref.shape[1]
    position_of, count_of = slot_reader(place_ref, lax.axis_index("dev"))

    @pl.loop(0, BLK_DEV)
    def _(blk):
        count = count_of(blk)

        def row_work(width):
            totals = jnp.zeros((rows, LANES), jnp.float32)
            for slot in range(width):
                points = tab_ref[position_of(blk, slot)]
                kern = jnp.exp2(raw_scores(src_ref[blk], points) * scale)
                kept[blk * SLOTS + slot] = kern.astype(jnp.bfloat16)
                total = kern[:, :LANES]
                for lane in range(1, rows // LANES):
                    total = total + kern[:, lane * LANES : (lane + 1) * LANES]
                totals = totals + jnp.where(slot < count, total, 0.0)
            row_acc[pl.ds(blk * rows, rows), :] = totals

        by_width(count, row_work)

    row_sum = lane_sums(row_acc[...])
    logw = logw_ref[...]
    fs_ref[...] = logw - jnp.log(row_sum)
    weights = weight_rows(jnp.exp(logw) / row_sum)
    row_fine = jnp.where((row_sum >= ROW_LOW) & (row_sum <= ROW_HIGH), 1.0, 0.0)
    fine = jnp.ones((1, rows), jnp.float32)
    for blk in range(BLK_DEV):
        span = slice(blk * rows, (blk + 1) * rows)
        wts[blk] = weights[:, span]
        fine = jnp.minimum(fine, row_fine[:, span])
    fine_ref[...] = fine
    part_ref[...] = jnp.zeros_like(part_ref)

    @pl.loop(0, BLK_DEV)
    def _(blk):
        count = count_of(blk)

        def column_work(width):
            fine = fine_ref[...]
            for slot in range(width):
                here = column_sums(wts[blk], kept[blk * SLOTS + slot])
                part_ref[position_of(blk, slot)] += jnp.where(slot < count, here, 0.0)
                fine = jnp.minimum(
                    fine, jnp.where((here >= COL_LOW) | (slot >= count), 1.0, 0.0)
                )
            fine_ref[...] = fine

        by_width(count, column_work)

    sums = part_ref[...]
    part_ref[...] = jnp.where(sums > 0.0, jnp.log(jnp.where(sums > 0.0, sums, 1.0)), NEG_FILL)

    @pl.when(jnp.min(fine_ref[...]) < 0.5)
    def _():
        part_ref[...] = jnp.full_like(part_ref, NEG_FILL)

        @pl.loop(0, BLK_DEV)
        def _(blk):
            count = count_of(blk)
            col_max[...] = jnp.full_like(col_max, NEG_FILL)
            col_total[...] = jnp.zeros_like(col_total)

            @pl.loop(0, count)
            def _(slot):
                points = tab_ref[position_of(blk, slot)]
                for part in range(rows // LANES):
                    span = pl.ds(part * LANES, LANES)
                    scores = raw_scores(src_ref[blk, span, :], points) * factor
                    old = col_max[span, :]
                    new = jnp.maximum(old, jnp.max(scores, axis=1, keepdims=True))
                    here = jnp.sum(jnp.exp(scores - new[:, 0:1]), axis=1, keepdims=True)
                    col_total[span, :] = col_total[span, :] * jnp.exp(old - new) + here
                    col_max[span, :] = new

            lse = col_max[...] + jnp.log(col_total[...])
            row_acc[pl.ds(blk * rows, rows), :] = lse

            @pl.loop(0, count)
            def _(slot):
                position = position_of(blk, slot)
                points = tab_ref[position]
                logw_col = as_columns(logw_ref[:, pl.ds(pl.multiple_of(blk * rows, rows), rows)])
                source = logw_col - row_acc[pl.ds(blk * rows, rows), :]
                col_max[...] = source
                high = jnp.full((1, rows), NEG_FILL, jnp.float32)
                total = jnp.zeros((1, rows), jnp.float32)
                for part in range(rows // LANES):
                    span = pl.ds(part * LANES, LANES)
                    scores = raw_scores(src_ref[blk, span, :], points) * factor
                    scores = scores + col_max[span, 0:1]
                    new = jnp.maximum(high, jnp.max(scores, axis=0, keepdims=True))
                    total = total * jnp.exp(high - new) + jnp.sum(
                        jnp.exp(scores - new), axis=0, keepdims=True
                    )
                    high = new
                here = high + jnp.log(total)
                old = part_ref[position]
                new = jnp.maximum(old, here)
                part_ref[position] = new + jnp.log(jnp.exp(old - new) + jnp.exp(here - new))

        fs_ref[...] = logw_ref[...] - as_row(row_acc[...])


def deliver_kernel(
    dev_count, group_count, pairs_ref, tgt_hbm, src_hbm, src_logw_hbm,
    tab_ref, pick_out, place_out, src_out, src_logw_out,
    pick_ref, tgt_ref, prev_buf, next_buf, far_buf, relay_up, relay_down, stage,
    trunk_send, trunk_recv, stage_send, tab_recv, relay_recv, fwd_send, grp_recv, own_sem,
):
    me_group, me_dev = lax.axis_index("group"), lax.axis_index("dev")
    core = lax.rem(me_dev, 2)
    at_x, at_z = lax.rem(me_dev // 2, RING), me_dev // (2 * RING)
    half = BLK_DEV // 2

    def device(along, across, to_core):
        dz = along + core * (across - along)
        dx = across + core * (along - across)
        return (lax.rem(at_z + dz, RING) * RING + lax.rem(at_x + dx, RING)) * 2 + to_core

    def send(src, dst, send_sem, recv_sem, dev, group=None):
        return pltpu.make_async_remote_copy(
            src_ref=src,
            dst_ref=dst,
            send_sem=send_sem,
            recv_sem=recv_sem,
            device_id=(me_group if group is None else group, dev),
            device_id_type=MESH,
        )

    needs = [
        pltpu.make_async_copy(src, dst, own_sem.at[n])
        for n, (src, dst) in enumerate(
            (
                (tgt_hbm, tgt_ref),
                (src_logw_hbm, src_logw_out),
                (src_hbm, src_out),
                (tgt_hbm, tab_ref.at[pl.ds(0, BLK_DEV)]),
            )
        )
    ]
    for copy in needs:
        copy.start()
    barrier = pltpu.get_barrier_semaphore()
    near = [
        device(i, j, cc) for i, j in ((1, 0), (3, 0), (0, 1), (0, 3)) for cc in (0, 1)
    ] + [device(0, 0, 1 - core)]
    for dev in near:
        pl.semaphore_signal(barrier, inc=1, device_id=(me_group, dev), device_id_type=MESH)
    for step in range(1, group_count):
        pl.semaphore_signal(
            barrier,
            inc=1,
            device_id=(lax.rem(me_group + step, group_count), me_dev),
            device_id_type=MESH,
        )
    by_dev, by_group, places, counts = all_picks(
        pairs_ref, dev_count, group_count, me_group, me_dev
    )
    place_out[0:SLOTS, :] = places
    place_out[SLOTS : SLOTS + 1, :] = counts
    pick_out[0:dev_count, :] = by_dev
    for g, here in enumerate(by_group):
        pick_out[dev_count + g : dev_count + g + 1, :] = here
    known = pltpu.make_async_copy(pick_out, pick_ref, own_sem.at[len(needs)])
    known.start()
    pl.semaphore_wait(barrier, len(near) + group_count - 1)

    low, top = pl.ds(0, half), pl.ds(half, half)
    ahead, behind = device(1, 0, core), device(3, 0, core)

    def trunk(n, src, dst, span, dev):
        return send(src.at[span], dst.at[span], trunk_send.at[n], trunk_recv.at[n], dev)

    trunks = [
        trunk(0, tgt_hbm, prev_buf, low, ahead),
        trunk(1, tgt_hbm, next_buf, top, behind),
        trunk(2, tgt_hbm, prev_buf, top, ahead),
        trunk(3, tgt_hbm, next_buf, low, behind),
        trunk(4, prev_buf, far_buf, low, ahead),
        trunk(5, next_buf, far_buf, top, behind),
    ]
    for n in range(4):
        trunks[n].start()
    sent = []

    def branch(k, buf):
        source = device(TRUNK[k], 0, core)
        for n, (across, to_core) in enumerate(BRANCH + ((0, 1 - core),)):
            taker = device(0, across, to_core)
            at = k * (len(BRANCH) + 1) + n
            stage[at] = buf[jnp.maximum(pick_of_dev(pick_ref, taker, source), 0)]
            if across == 2:
                relay, over = ((relay_up, 1), (relay_down, 3))[to_core]
                which = relay_recv.at[to_core * RING + k]
                copy = send(
                    stage.at[at], relay.at[k], stage_send.at[at], which, device(0, over, core)
                )
            else:
                copy = send(
                    stage.at[at],
                    tab_ref.at[BLK_DEV + source],
                    stage_send.at[at],
                    tab_recv.at[source],
                    taker,
                )
            copy.start()
            sent.append(copy)
        if k > 0:
            at = RING * (len(BRANCH) + 1) + group_count - 1 + k - 1
            stage[at] = buf[jnp.maximum(pick_of_dev(pick_ref, me_dev, source), 0)]
            pltpu.make_async_copy(
                stage.at[at], tab_ref.at[BLK_DEV + source], tab_recv.at[source]
            ).start()

    def pass_on(k):
        for way, (relay, back, over) in enumerate(((relay_up, 3, 1), (relay_down, 1, 3))):
            source = device(TRUNK[k], back, core)
            at = way * RING + k
            copy = send(
                relay.at[k],
                tab_ref.at[BLK_DEV + source],
                fwd_send.at[at],
                tab_recv.at[source],
                device(0, over, way),
            )
            send(
                relay.at[k], relay.at[k], fwd_send.at[at], relay_recv.at[at], ahead
            ).wait_recv()
            copy.start()
            sent.append(copy)

    known.wait()
    needs[0].wait()
    branch(0, tgt_ref)
    from_groups = []
    for step in range(1, group_count):
        peer = lax.rem(me_group + step, group_count)
        at = RING * (len(BRANCH) + 1) + step - 1
        pick = pick_of_group(pick_ref, dev_count, peer, me_dev)
        stage[at] = tgt_ref[jnp.maximum(pick, 0)]
        copy = send(
            stage.at[at],
            tab_ref.at[BLK_DEV + dev_count + me_group],
            stage_send.at[at],
            grp_recv.at[step],
            me_dev,
            peer,
        )
        copy.start()
        sent.append(copy)
        from_groups.append(copy)
    trunks[0].wait_recv()
    trunks[4].start()
    trunks[1].wait_recv()
    trunks[5].start()
    trunks[2].wait_recv()
    branch(1, prev_buf)
    trunks[3].wait_recv()
    branch(2, next_buf)
    pass_on(0)
    trunks[4].wait_recv()
    trunks[5].wait_recv()
    branch(3, far_buf)
    pass_on(1)
    pass_on(2)
    pass_on(3)
    for copy in sent + trunks:
        copy.wait_send()
    for step in range(1, dev_count):
        source = lax.rem(me_dev + step, dev_count)
        send(
            stage.at[0], tab_ref.at[BLK_DEV + source], stage_send.at[0], tab_recv.at[source], ahead
        ).wait_recv()
    for copy in from_groups:
        copy.wait_recv()
    for copy in needs[1:]:
        copy.wait()


def greet(dev_count, group_count, me_dev, me_group):
    barrier = pltpu.get_barrier_semaphore()

    def to_dev(step, carry):
        peer = lax.rem(me_dev + step, dev_count)
        pl.semaphore_signal(barrier, inc=1, device_id=(me_group, peer), device_id_type=MESH)
        return carry

    def to_group(step, carry):
        peer = lax.rem(me_group + step, group_count)
        pl.semaphore_signal(barrier, inc=1, device_id=(peer, me_dev), device_id_type=MESH)
        return carry

    lax.fori_loop(1, dev_count, to_dev, 0)
    lax.fori_loop(1, group_count, to_group, 0)
    pl.semaphore_wait(barrier, dev_count + group_count - 2)


def exchange(
    out_ref, out_base, in_ref, in_base, send_sem, recv_sem, dev_count, group_count, me_dev, me_group
):
    def to_dev(step):
        peer = lax.rem(me_dev + step, dev_count)
        return pltpu.make_async_remote_copy(
            src_ref=out_ref.at[out_base + peer],
            dst_ref=in_ref.at[in_base + me_dev],
            send_sem=send_sem.at[step],
            recv_sem=recv_sem.at[step],
            device_id=(me_group, peer),
            device_id_type=MESH,
        )

    def to_group(step):
        peer = lax.rem(me_group + step, group_count)
        return pltpu.make_async_remote_copy(
            src_ref=out_ref.at[out_base + dev_count + peer],
            dst_ref=in_ref.at[in_base + dev_count + me_group],
            send_sem=send_sem.at[dev_count + step],
            recv_sem=recv_sem.at[dev_count + step],
            device_id=(peer, me_dev),
            device_id_type=MESH,
        )

    def start(copy_of):
        def body(step, carry):
            copy_of(step).start()
            return carry

        return body

    def wait(copy_of):
        def body(step, carry):
            copy_of(step).wait()
            return carry

        return body

    lax.fori_loop(1, dev_count, start(to_dev), 0)
    lax.fori_loop(1, group_count, start(to_group), 0)

    def finish():
        lax.fori_loop(1, dev_count, wait(to_dev), 0)
        lax.fori_loop(1, group_count, wait(to_group), 0)

    return finish


def picks_of_peers(pick_ref, dev_count, group_count, me_group, me_dev):
    return [
        jnp.where(me_dev == e, -1, pick_of_dev(pick_ref, e, me_dev)) for e in range(dev_count)
    ] + [
        jnp.where(me_group == e, -1, pick_of_group(pick_ref, dev_count, e, me_dev))
        for e in range(group_count)
    ]


def finish_kernel(
    dev_count, group_count, pick_ref, place_ref, part_ref, tgt_logw_ref, src_hbm,
    src_logw_ref, fs_ref, tab_hbm,
    pot_ref, map_ref, tgt_pot_ref,
    src_ref, tab_ref, own_sem, inbox, outbox, dual_ref, inbox2, outbox2, kept, ready, fs_col, acc, wts, col_sum,
    send_a, recv_a, send_b, recv_b, send_c, recv_c,
):
    me_group, me_dev = lax.axis_index("group"), lax.axis_index("dev")
    blocks, rows = BLK_DEV, src_ref.shape[1]
    needs = [
        pltpu.make_async_copy(src_hbm, src_ref, own_sem.at[0]),
        pltpu.make_async_copy(tab_hbm, tab_ref, own_sem.at[1]),
    ]
    for copy in needs:
        copy.start()
    scale = LOG2E / math.sqrt(EMB)
    position_of, count_of = slot_reader(place_ref, me_dev)
    place = (dev_count, group_count, me_dev, me_group)
    greet(*place)
    arrived = exchange(part_ref, blocks, inbox, 0, send_a, recv_a, *place)
    empty = jnp.full(inbox.shape[1:], NEG_FILL, jnp.float32)
    for at in (me_dev, dev_count + me_group):
        inbox[at] = empty
        inbox2[at] = jnp.zeros_like(empty)
        dual_ref[blocks + at] = jnp.zeros_like(empty)
    picks = picks_of_peers(pick_ref, dev_count, group_count, me_group, me_dev)
    fs_col[...] = as_columns(fs_ref[...] * LOG2E)

    def exponent(blk, part, points):
        span = pl.ds(part * LANES, LANES)
        shift = fs_col[pl.ds(blk * rows + part * LANES, LANES), :]
        shift = jnp.concatenate([shift] * (rows // LANES), axis=1)
        return raw_scores(src_ref[blk, span, :], points) * scale + shift

    def prepare(first, last):
        @pl.loop(first, last)
        def _(blk):
            for slot in range(SLOTS):
                points = tab_ref[position_of(blk, slot)]
                for part in range(rows // LANES):
                    span = pl.ds(part * LANES, LANES)
                    ready[blk * SLOTS + slot, span, :] = exponent(blk, part, points)

    for copy in needs:
        copy.wait()
    prepare(0, (PREPARED + 1) // 2)
    arrived()
    for q in range(blocks):
        terms = [part_ref[q]] + [
            jnp.where(pick == q, inbox[e], NEG_FILL) for e, pick in enumerate(picks)
        ]
        high = functools.reduce(jnp.maximum, terms)
        total = sum(jnp.exp(term - high) for term in terms)
        dual_ref[q] = tgt_logw_ref[q] - (high + jnp.log(total))
    duals = [dual_ref[q] for q in range(blocks)]
    for e, pick in enumerate(picks):
        chosen = duals[0]
        for q in range(1, blocks):
            chosen = jnp.where(pick == q, duals[q], chosen)
        outbox[e] = chosen
    arrived = exchange(outbox, 0, dual_ref, blocks, send_b, recv_b, *place)
    prepare((PREPARED + 1) // 2, PREPARED)
    arrived()
    ones = jnp.ones((rows, LANES), jnp.bfloat16)

    def plans(blk, exponent_of):
        count = count_of(blk)
        for slot in range(SLOTS):
            position = position_of(blk, slot)
            dual = jnp.where(slot < count, dual_ref[position] * LOG2E, NEG_FILL)
            points = tab_ref[position]
            beside = jnp.concatenate([points, ones], axis=1)
            for part in range(rows // LANES):
                span = pl.ds(part * LANES, LANES)
                here = pl.ds(blk * rows + part * LANES, LANES)
                plan = jnp.exp2(exponent_of(slot, part, points) + dual).astype(jnp.bfloat16)
                kept[blk * SLOTS + slot, span, :] = plan
                product = jnp.dot(plan, beside, preferred_element_type=jnp.float32)
                acc[here, :] = product if slot == 0 else acc[here, :] + product

    @pl.loop(0, PREPARED)
    def _(blk):
        plans(
            blk,
            lambda slot, part, points: ready[
                blk * SLOTS + slot, pl.ds(part * LANES, LANES), :
            ],
        )

    for blk in range(PREPARED, blocks):
        plans(blk, lambda slot, part, points: exponent(blk, part, points))

    row_sum = lane_sums(acc[:, LANES:]) * (1.0 / LANES)
    logw = src_logw_ref[...]
    weights = weight_rows(jnp.exp(logw) / row_sum)
    for blk in range(blocks):
        wts[blk] = weights[:, blk * rows : (blk + 1) * rows]

    @pl.loop(0, blocks)
    def _(blk):
        for slot in range(SLOTS):
            col_sum[pl.ds(blk * SLOTS + slot, 1), :] = column_sums(
                wts[blk], kept[blk * SLOTS + slot]
            )

    table, pairs = part_ref.shape[0], blocks * SLOTS
    row_at = lax.broadcasted_iota(jnp.int32, (table, pairs), 0)
    col_at = lax.broadcasted_iota(jnp.int32, (table, pairs), 1)
    into = jnp.full((table, pairs), -1, jnp.int32)
    for blk in range(blocks):
        count = count_of(blk)
        for slot in range(SLOTS):
            position = jnp.where(slot < count, position_of(blk, slot), -1)
            into = jnp.where(col_at == blk * SLOTS + slot, position, into)
    gathered = lax.dot_general(
        jnp.where(into == row_at, 1.0, 0.0),
        col_sum[...],
        (((1,), (0,)), ((), ())),
        precision=lax.Precision.HIGHEST,
        preferred_element_type=jnp.float32,
    )
    for e in range(table):
        outbox2[e] = gathered[e : e + 1]
    arrived = exchange(outbox2, blocks, inbox2, 0, send_c, recv_c, *place)
    pot_ref[...] = logw + fs_ref[...] - jnp.log(row_sum)
    for blk in range(blocks):
        span = pl.ds(blk * rows, rows)
        map_ref[blk] = acc[span, :LANES] / acc[span, LANES:]
    arrived()
    for q in range(blocks):
        total = outbox2[q]
        for e, pick in enumerate(picks):
            total = total + jnp.where(pick == q, inbox2[e], 0.0)
        tgt_pot_ref[q] = tgt_logw_ref[q] - jnp.log(total) + dual_ref[q]


def shards(source_points, target_points, source_logw, target_logw, pair_targets, pair_count):
    group_count = lax.axis_size("group")
    dev_count = lax.axis_size("dev")
    blocks, rows, slots = BLK_DEV, BLOCK, SLOTS
    table = blocks + dev_count + group_count
    peers = dev_count + group_count
    sources = source_points.reshape(blocks, rows, EMB)
    targets = target_points.reshape(blocks, rows, EMB)
    log_src = source_logw.reshape(1, blocks * rows)
    log_tgt = target_logw.reshape(blocks, 1, rows)

    named = jnp.concatenate([pair_targets.T, pair_count[None, :]], axis=0)

    smem = pl.BlockSpec(memory_space=pltpu.SMEM)
    vmem = pl.BlockSpec(memory_space=pltpu.VMEM)
    anywhere = pl.BlockSpec(memory_space=pl.ANY)
    f32 = jnp.float32
    kept = pltpu.VMEM((blocks * slots, rows, rows), jnp.bfloat16)
    pairs = blocks * slots
    dma = pltpu.SemaphoreType.DMA
    block = (rows, EMB)
    lots = RING * (len(BRANCH) + 1) + group_count - 1 + RING - 1
    picks = (peers, dev_count * blocks)
    hbm = pl.BlockSpec(memory_space=pltpu.HBM)
    delivered, pick, places, near_src, near_log_src = pl.pallas_call(
        functools.partial(deliver_kernel, dev_count, group_count),
        out_shape=(
            jax.ShapeDtypeStruct((table, *block), jnp.bfloat16),
            jax.ShapeDtypeStruct(picks, jnp.int32),
            jax.ShapeDtypeStruct((2 * slots, dev_count * blocks), jnp.int32),
            jax.ShapeDtypeStruct((blocks, *block), jnp.bfloat16),
            jax.ShapeDtypeStruct((1, blocks * rows), f32),
        ),
        in_specs=[vmem, hbm, hbm, hbm],
        out_specs=(anywhere, vmem, vmem, anywhere, anywhere),
        scratch_shapes=[
            pltpu.SMEM(picks, jnp.int32),
        ]
        + [pltpu.VMEM((blocks, *block), jnp.bfloat16)] * 4
        + [pltpu.VMEM((RING, *block), jnp.bfloat16)] * 2
        + [
            pltpu.VMEM((lots, *block), jnp.bfloat16),
            dma((6,)),
            dma((6,)),
            dma((lots,)),
            dma((dev_count,)),
            dma((2 * RING,)),
            dma((2 * RING,)),
            dma((group_count,)),
            dma((5,)),
        ],
        compiler_params=pltpu.CompilerParams(
            collective_id=2, has_side_effects=True, vmem_limit_bytes=VMEM_LIMIT
        ),
        name="deliver_blocks",
    )(named, targets, sources, log_src)

    first_source, part = pl.pallas_call(
        first_kernel,
        out_shape=(
            jax.ShapeDtypeStruct((1, blocks * rows), f32),
            jax.ShapeDtypeStruct((table, 1, rows), f32),
        ),
        in_specs=[smem, vmem, vmem, vmem],
        out_specs=(vmem, vmem),
        scratch_shapes=[
            kept,
            pltpu.VMEM((blocks * rows, LANES), f32),
            pltpu.VMEM((blocks, 16, rows), jnp.bfloat16),
            pltpu.VMEM((1, rows), f32),
            pltpu.VMEM((rows, LANES), f32),
            pltpu.VMEM((rows, LANES), f32),
        ],
        compiler_params=pltpu.CompilerParams(vmem_limit_bytes=PAIR_LIMIT),
        cost_estimate=pl.CostEstimate(
            flops=4 * pairs * rows * rows * EMB, bytes_accessed=6 * 2**20, transcendentals=pairs * rows * rows
        ),
        name="first_pass",
    )(places, near_src, near_log_src, delivered)

    row = pltpu.VMEM((peers, 1, rows), f32)
    full = pltpu.VMEM((table, 1, rows), f32)
    potential, mapped, target_potential = pl.pallas_call(
        functools.partial(finish_kernel, dev_count, group_count),
        out_shape=(
            jax.ShapeDtypeStruct((1, blocks * rows), f32),
            jax.ShapeDtypeStruct((blocks, rows, EMB), f32),
            jax.ShapeDtypeStruct((blocks, 1, rows), f32),
        ),
        in_specs=[smem, smem, vmem, vmem, hbm, vmem, vmem, hbm],
        out_specs=(vmem, vmem, vmem),
        scratch_shapes=[
            pltpu.VMEM((blocks, *block), jnp.bfloat16),
            pltpu.VMEM((table, *block), jnp.bfloat16),
            dma((2,)),
            row,
            row,
            full,
            row,
            full,
            kept,
            pltpu.VMEM((PREPARED * slots, rows, rows), f32),
            pltpu.VMEM((blocks * rows, LANES), f32),
            pltpu.VMEM((blocks * rows, 2 * LANES), f32),
            pltpu.VMEM((blocks, 16, rows), jnp.bfloat16),
            pltpu.VMEM((pairs, rows), f32),
        ]
        + [dma((peers,))] * 6,
        compiler_params=pltpu.CompilerParams(
            collective_id=0, has_side_effects=True, vmem_limit_bytes=FINISH_LIMIT
        ),
        cost_estimate=pl.CostEstimate(
            flops=8 * pairs * rows * rows * EMB, bytes_accessed=7 * 2**20, transcendentals=pairs * rows * rows
        ),
        name="finish",
    )(
        pick, places, part, log_tgt, sources, near_log_src, first_source, delivered
    )
    return (
        potential.reshape(blocks * rows),
        target_potential.reshape(blocks * rows),
        mapped.reshape(blocks * rows, EMB),
    )


def solution(mesh):
    return jax.shard_map(
        shards,
        mesh=mesh,
        in_specs=(
            P(("group", "dev"), None),
            P(("group", "dev"), None),
            P(("group", "dev")),
            P(("group", "dev")),
            P(),
            P(),
        ),
        out_specs=(P(("group", "dev")), P(("group", "dev")), P(("group", "dev"), None)),
        check_vma=False,
    )
```

```python
import functools
import math

import jax
import jax.numpy as jnp
from jax import lax
from jax.experimental import pallas as pl
from jax.experimental.pallas import tpu as pltpu
from jax.sharding import PartitionSpec as P

BLOCK = 512
EMB = 128
BLK_DEV = 4
SLOTS = 8
LANES = 128
NEG_FILL = -1e30
LOG2E = math.log2(math.e)
ROW_LOW, ROW_HIGH, COL_LOW = 1e-6, 1e30, 1e-22
MESH = pl.DeviceIdType.MESH
VMEM_LIMIT = 20 * 2**20
PAIR_LIMIT = 28 * 2**20
FINISH_LIMIT = 52 * 2**20
PREPARED = 3


RING = 4
TRUNK = (0, 3, 1, 2)
BRANCH = ((2, 0), (2, 1), (1, 0), (1, 1), (3, 0), (3, 1))


def all_picks(pairs_ref, dev_count, group_count, me_group, me_dev):
    plane = dev_count * BLK_DEV
    first = me_group * plane
    span = pl.ds(pl.multiple_of(first, plane), plane)
    slots = lax.broadcasted_iota(jnp.int32, (SLOTS, plane), 0)
    name, counts = pairs_ref[0:SLOTS, span], pairs_ref[SLOTS : SLOTS + 1, span]
    named = jnp.where(slots < counts, name - first, -1)
    source = lax.broadcasted_iota(jnp.int32, (dev_count, plane), 0)
    picks = jnp.full((dev_count, plane), -1, jnp.int32)
    for slot in range(SLOTS):
        here = named[slot : slot + 1]
        picks = jnp.maximum(picks, jnp.where((here >> 2) == source, here & 3, -1))
    away = pairs_ref[1:2, :]
    away = jnp.where((away >> 2) == me_group * dev_count + me_dev, away & 3, -1)
    away = [away[:, g * plane : (g + 1) * plane] for g in range(group_count)]
    bits = dev_count.bit_length() - 1
    owner = name >> 2
    there = jnp.where(
        (owner >> bits) == me_group, owner & (dev_count - 1), dev_count + (owner >> bits)
    )
    places = jnp.where(owner == me_group * dev_count + me_dev, name & 3, BLK_DEV + there)
    return picks, away, places, counts


def pick_of_dev(pick_ref, taker, source):
    first = pick_ref[source, BLK_DEV * taker]
    for row in range(1, BLK_DEV):
        first = jnp.maximum(first, pick_ref[source, BLK_DEV * taker + row])
    return first


def pick_of_group(pick_ref, dev_count, peer, me_dev):
    return pick_of_dev(pick_ref, me_dev, dev_count + peer)


def slot_reader(place_ref, me_dev):
    def position_of(blk, slot):
        return place_ref[slot, me_dev * BLK_DEV + blk]

    def count_of(blk):
        return place_ref[SLOTS, me_dev * BLK_DEV + blk]

    return position_of, count_of


def raw_scores(left, right):
    return lax.dot_general(left, right, (((1,), (1,)), ((), ())), preferred_element_type=jnp.float32)


def as_columns(row):
    return jnp.transpose(jnp.broadcast_to(row, (LANES, row.shape[1])))


def as_row(columns):
    return jnp.transpose(columns)[0:1]


def lane_sums(columns):
    high = columns.astype(jnp.bfloat16)
    low = (columns - high.astype(jnp.float32)).astype(jnp.bfloat16)
    parts = jnp.concatenate([high, low], axis=1)
    return raw_scores(jnp.ones((16, parts.shape[1]), jnp.bfloat16), parts)[0:1]


def weight_rows(weights):
    high = weights.astype(jnp.bfloat16).astype(jnp.float32)
    rest = weights - high
    middle = rest.astype(jnp.bfloat16).astype(jnp.float32)
    low = rest - middle
    at = lax.broadcasted_iota(jnp.int32, (16, weights.shape[1]), 0)
    zero = jnp.zeros((16, weights.shape[1]), jnp.float32)
    rows = jnp.where(at == 0, high, jnp.where(at == 1, middle, jnp.where(at == 2, low, zero)))
    return rows.astype(jnp.bfloat16)


def by_width(count, work):
    @pl.when(count <= SLOTS // 2)
    def _():
        work(SLOTS // 2)

    @pl.when(count > SLOTS // 2)
    def _():
        work(SLOTS)


def column_sums(weights, kernel):
    return jnp.sum(
        jnp.dot(weights, kernel, preferred_element_type=jnp.float32), axis=0, keepdims=True
    )


def first_kernel(
    place_ref, src_ref, logw_ref, tab_ref,
    fs_ref, part_ref,
    kept, row_acc, wts, fine_ref, col_max, col_total,
):
    factor = 1.0 / math.sqrt(EMB)
    scale = factor * LOG2E
    rows = src_ref.shape[1]
    position_of, count_of = slot_reader(place_ref, lax.axis_index("dev"))

    @pl.loop(0, BLK_DEV)
    def _(blk):
        count = count_of(blk)

        def row_work(width):
            totals = jnp.zeros((rows, LANES), jnp.float32)
            for slot in range(width):
                points = tab_ref[position_of(blk, slot)]
                kern = jnp.exp2(raw_scores(src_ref[blk], points) * scale)
                kept[blk * SLOTS + slot] = kern.astype(jnp.bfloat16)
                total = kern[:, :LANES]
                for lane in range(1, rows // LANES):
                    total = total + kern[:, lane * LANES : (lane + 1) * LANES]
                totals = totals + jnp.where(slot < count, total, 0.0)
            row_acc[pl.ds(blk * rows, rows), :] = totals

        by_width(count, row_work)

    row_sum = lane_sums(row_acc[...])
    logw = logw_ref[...]
    fs_ref[...] = logw - jnp.log(row_sum)
    weights = weight_rows(jnp.exp(logw) / row_sum)
    row_fine = jnp.where((row_sum >= ROW_LOW) & (row_sum <= ROW_HIGH), 1.0, 0.0)
    fine = jnp.ones((1, rows), jnp.float32)
    for blk in range(BLK_DEV):
        span = slice(blk * rows, (blk + 1) * rows)
        wts[blk] = weights[:, span]
        fine = jnp.minimum(fine, row_fine[:, span])
    fine_ref[...] = fine
    part_ref[...] = jnp.zeros_like(part_ref)

    @pl.loop(0, BLK_DEV)
    def _(blk):
        count = count_of(blk)

        def column_work(width):
            fine = fine_ref[...]
            for slot in range(width):
                here = column_sums(wts[blk], kept[blk * SLOTS + slot])
                part_ref[position_of(blk, slot)] += jnp.where(slot < count, here, 0.0)
                fine = jnp.minimum(
                    fine, jnp.where((here >= COL_LOW) | (slot >= count), 1.0, 0.0)
                )
            fine_ref[...] = fine

        by_width(count, column_work)

    sums = part_ref[...]
    part_ref[...] = jnp.where(sums > 0.0, jnp.log(jnp.where(sums > 0.0, sums, 1.0)), NEG_FILL)

    @pl.when(jnp.min(fine_ref[...]) < 0.5)
    def _():
        part_ref[...] = jnp.full_like(part_ref, NEG_FILL)

        @pl.loop(0, BLK_DEV)
        def _(blk):
            count = count_of(blk)
            col_max[...] = jnp.full_like(col_max, NEG_FILL)
            col_total[...] = jnp.zeros_like(col_total)

            @pl.loop(0, count)
            def _(slot):
                points = tab_ref[position_of(blk, slot)]
                for part in range(rows // LANES):
                    span = pl.ds(part * LANES, LANES)
                    scores = raw_scores(src_ref[blk, span, :], points) * factor
                    old = col_max[span, :]
                    new = jnp.maximum(old, jnp.max(scores, axis=1, keepdims=True))
                    here = jnp.sum(jnp.exp(scores - new[:, 0:1]), axis=1, keepdims=True)
                    col_total[span, :] = col_total[span, :] * jnp.exp(old - new) + here
                    col_max[span, :] = new

            lse = col_max[...] + jnp.log(col_total[...])
            row_acc[pl.ds(blk * rows, rows), :] = lse

            @pl.loop(0, count)
            def _(slot):
                position = position_of(blk, slot)
                points = tab_ref[position]
                logw_col = as_columns(logw_ref[:, pl.ds(pl.multiple_of(blk * rows, rows), rows)])
                source = logw_col - row_acc[pl.ds(blk * rows, rows), :]
                col_max[...] = source
                high = jnp.full((1, rows), NEG_FILL, jnp.float32)
                total = jnp.zeros((1, rows), jnp.float32)
                for part in range(rows // LANES):
                    span = pl.ds(part * LANES, LANES)
                    scores = raw_scores(src_ref[blk, span, :], points) * factor
                    scores = scores + col_max[span, 0:1]
                    new = jnp.maximum(high, jnp.max(scores, axis=0, keepdims=True))
                    total = total * jnp.exp(high - new) + jnp.sum(
                        jnp.exp(scores - new), axis=0, keepdims=True
                    )
                    high = new
                here = high + jnp.log(total)
                old = part_ref[position]
                new = jnp.maximum(old, here)
                part_ref[position] = new + jnp.log(jnp.exp(old - new) + jnp.exp(here - new))

        fs_ref[...] = logw_ref[...] - as_row(row_acc[...])


def deliver_kernel(
    dev_count, group_count, pairs_ref, points_hbm, src_logw_hbm,
    tab_ref, pick_out, place_out, src_out, src_logw_out,
    pick_ref, tgt_ref, prev_buf, next_buf, far_buf, relay_up, relay_down, stage,
    trunk_send, trunk_recv, stage_send, tab_recv, relay_recv, fwd_send, grp_recv, own_sem,
):
    me_group, me_dev = lax.axis_index("group"), lax.axis_index("dev")
    core = lax.rem(me_dev, 2)
    at_x, at_z = lax.rem(me_dev // 2, RING), me_dev // (2 * RING)
    half = BLK_DEV // 2

    def device(along, across, to_core):
        dz = along + core * (across - along)
        dx = across + core * (along - across)
        return (lax.rem(at_z + dz, RING) * RING + lax.rem(at_x + dx, RING)) * 2 + to_core

    def send(src, dst, send_sem, recv_sem, dev, group=None):
        return pltpu.make_async_remote_copy(
            src_ref=src,
            dst_ref=dst,
            send_sem=send_sem,
            recv_sem=recv_sem,
            device_id=(me_group if group is None else group, dev),
            device_id_type=MESH,
        )

    tgt_hbm, src_hbm = points_hbm.at[0], points_hbm.at[1]
    needs = [
        pltpu.make_async_copy(src, dst, own_sem.at[n])
        for n, (src, dst) in enumerate(
            (
                (tgt_hbm, tgt_ref),
                (src_logw_hbm, src_logw_out),
                (src_hbm, src_out),
                (tgt_hbm, tab_ref.at[pl.ds(0, BLK_DEV)]),
            )
        )
    ]
    for copy in needs:
        copy.start()
    barrier = pltpu.get_barrier_semaphore()
    near = [
        device(i, j, cc) for i, j in ((1, 0), (3, 0), (0, 1), (0, 3)) for cc in (0, 1)
    ] + [device(0, 0, 1 - core)]
    for dev in near:
        pl.semaphore_signal(barrier, inc=1, device_id=(me_group, dev), device_id_type=MESH)
    for step in range(1, group_count):
        pl.semaphore_signal(
            barrier,
            inc=1,
            device_id=(lax.rem(me_group + step, group_count), me_dev),
            device_id_type=MESH,
        )
    by_dev, by_group, places, counts = all_picks(
        pairs_ref, dev_count, group_count, me_group, me_dev
    )
    place_out[0:SLOTS, :] = places
    place_out[SLOTS : SLOTS + 1, :] = counts
    pick_out[0:dev_count, :] = by_dev
    for g, here in enumerate(by_group):
        pick_out[dev_count + g : dev_count + g + 1, :] = here
    known = pltpu.make_async_copy(pick_out, pick_ref, own_sem.at[len(needs)])
    known.start()
    pl.semaphore_wait(barrier, len(near) + group_count - 1)

    low, top = pl.ds(0, half), pl.ds(half, half)
    ahead, behind = device(1, 0, core), device(3, 0, core)

    def trunk(n, src, dst, span, dev):
        return send(src.at[span], dst.at[span], trunk_send.at[n], trunk_recv.at[n], dev)

    trunks = [
        trunk(0, tgt_hbm, prev_buf, low, ahead),
        trunk(1, tgt_hbm, next_buf, top, behind),
        trunk(2, tgt_hbm, prev_buf, top, ahead),
        trunk(3, tgt_hbm, next_buf, low, behind),
        trunk(4, prev_buf, far_buf, low, ahead),
        trunk(5, next_buf, far_buf, top, behind),
    ]
    for n in range(4):
        trunks[n].start()
    sent = []

    def branch(k, buf):
        source = device(TRUNK[k], 0, core)
        for n, (across, to_core) in enumerate(BRANCH + ((0, 1 - core),)):
            taker = device(0, across, to_core)
            at = k * (len(BRANCH) + 1) + n
            stage[at] = buf[jnp.maximum(pick_of_dev(pick_ref, taker, source), 0)]
            if across == 2:
                relay, over = ((relay_up, 1), (relay_down, 3))[to_core]
                which = relay_recv.at[to_core * RING + k]
                copy = send(
                    stage.at[at], relay.at[k], stage_send.at[at], which, device(0, over, core)
                )
            else:
                copy = send(
                    stage.at[at],
                    tab_ref.at[BLK_DEV + source],
                    stage_send.at[at],
                    tab_recv.at[source],
                    taker,
                )
            copy.start()
            sent.append(copy)
        if k > 0:
            at = RING * (len(BRANCH) + 1) + group_count - 1 + k - 1
            stage[at] = buf[jnp.maximum(pick_of_dev(pick_ref, me_dev, source), 0)]
            pltpu.make_async_copy(
                stage.at[at], tab_ref.at[BLK_DEV + source], tab_recv.at[source]
            ).start()

    def pass_on(k):
        for way, (relay, back, over) in enumerate(((relay_up, 3, 1), (relay_down, 1, 3))):
            source = device(TRUNK[k], back, core)
            at = way * RING + k
            copy = send(
                relay.at[k],
                tab_ref.at[BLK_DEV + source],
                fwd_send.at[at],
                tab_recv.at[source],
                device(0, over, way),
            )
            send(
                relay.at[k], relay.at[k], fwd_send.at[at], relay_recv.at[at], ahead
            ).wait_recv()
            copy.start()
            sent.append(copy)

    known.wait()
    needs[0].wait()
    branch(0, tgt_ref)
    from_groups = []
    for step in range(1, group_count):
        peer = lax.rem(me_group + step, group_count)
        at = RING * (len(BRANCH) + 1) + step - 1
        pick = pick_of_group(pick_ref, dev_count, peer, me_dev)
        stage[at] = tgt_ref[jnp.maximum(pick, 0)]
        copy = send(
            stage.at[at],
            tab_ref.at[BLK_DEV + dev_count + me_group],
            stage_send.at[at],
            grp_recv.at[step],
            me_dev,
            peer,
        )
        copy.start()
        sent.append(copy)
        from_groups.append(copy)
    trunks[0].wait_recv()
    trunks[4].start()
    trunks[1].wait_recv()
    trunks[5].start()
    trunks[2].wait_recv()
    branch(1, prev_buf)
    trunks[3].wait_recv()
    branch(2, next_buf)
    pass_on(0)
    trunks[4].wait_recv()
    trunks[5].wait_recv()
    branch(3, far_buf)
    pass_on(1)
    pass_on(2)
    pass_on(3)
    for copy in sent + trunks:
        copy.wait_send()
    for step in range(1, dev_count):
        source = lax.rem(me_dev + step, dev_count)
        send(
            stage.at[0], tab_ref.at[BLK_DEV + source], stage_send.at[0], tab_recv.at[source], ahead
        ).wait_recv()
    for copy in from_groups:
        copy.wait_recv()
    for copy in needs[1:]:
        copy.wait()


def greet(dev_count, group_count, me_dev, me_group):
    barrier = pltpu.get_barrier_semaphore()

    def to_dev(step, carry):
        peer = lax.rem(me_dev + step, dev_count)
        pl.semaphore_signal(barrier, inc=1, device_id=(me_group, peer), device_id_type=MESH)
        return carry

    def to_group(step, carry):
        peer = lax.rem(me_group + step, group_count)
        pl.semaphore_signal(barrier, inc=1, device_id=(peer, me_dev), device_id_type=MESH)
        return carry

    lax.fori_loop(1, dev_count, to_dev, 0)
    lax.fori_loop(1, group_count, to_group, 0)
    pl.semaphore_wait(barrier, dev_count + group_count - 2)


def exchange(
    out_ref, out_base, in_ref, in_base, send_sem, recv_sem, dev_count, group_count, me_dev, me_group
):
    def to_dev(step):
        peer = lax.rem(me_dev + step, dev_count)
        return pltpu.make_async_remote_copy(
            src_ref=out_ref.at[out_base + peer],
            dst_ref=in_ref.at[in_base + me_dev],
            send_sem=send_sem.at[step],
            recv_sem=recv_sem.at[step],
            device_id=(me_group, peer),
            device_id_type=MESH,
        )

    def to_group(step):
        peer = lax.rem(me_group + step, group_count)
        return pltpu.make_async_remote_copy(
            src_ref=out_ref.at[out_base + dev_count + peer],
            dst_ref=in_ref.at[in_base + dev_count + me_group],
            send_sem=send_sem.at[dev_count + step],
            recv_sem=recv_sem.at[dev_count + step],
            device_id=(peer, me_dev),
            device_id_type=MESH,
        )

    def start(copy_of):
        def body(step, carry):
            copy_of(step).start()
            return carry

        return body

    def wait(copy_of):
        def body(step, carry):
            copy_of(step).wait()
            return carry

        return body

    lax.fori_loop(1, dev_count, start(to_dev), 0)
    lax.fori_loop(1, group_count, start(to_group), 0)

    def finish():
        lax.fori_loop(1, dev_count, wait(to_dev), 0)
        lax.fori_loop(1, group_count, wait(to_group), 0)

    return finish


def picks_of_peers(pick_ref, dev_count, group_count, me_group, me_dev):
    return [
        jnp.where(me_dev == e, -1, pick_of_dev(pick_ref, e, me_dev)) for e in range(dev_count)
    ] + [
        jnp.where(me_group == e, -1, pick_of_group(pick_ref, dev_count, e, me_dev))
        for e in range(group_count)
    ]


def finish_kernel(
    dev_count, group_count, pick_ref, place_ref, part_ref, tgt_logw_ref, src_hbm,
    src_logw_ref, fs_ref, tab_hbm,
    pot_ref, map_ref, tgt_pot_ref,
    src_ref, tab_ref, own_sem, inbox, outbox, dual_ref, inbox2, outbox2, kept, ready, fs_col, acc, wts, col_sum,
    send_a, recv_a, send_b, recv_b, send_c, recv_c,
):
    me_group, me_dev = lax.axis_index("group"), lax.axis_index("dev")
    blocks, rows = BLK_DEV, src_ref.shape[1]
    needs = [
        pltpu.make_async_copy(src_hbm, src_ref, own_sem.at[0]),
        pltpu.make_async_copy(tab_hbm, tab_ref, own_sem.at[1]),
    ]
    for copy in needs:
        copy.start()
    scale = LOG2E / math.sqrt(EMB)
    position_of, count_of = slot_reader(place_ref, me_dev)
    place = (dev_count, group_count, me_dev, me_group)
    greet(*place)
    arrived = exchange(part_ref, blocks, inbox, 0, send_a, recv_a, *place)
    empty = jnp.full(inbox.shape[1:], NEG_FILL, jnp.float32)
    for at in (me_dev, dev_count + me_group):
        inbox[at] = empty
        inbox2[at] = jnp.zeros_like(empty)
        dual_ref[blocks + at] = jnp.zeros_like(empty)
    picks = picks_of_peers(pick_ref, dev_count, group_count, me_group, me_dev)
    fs_col[...] = as_columns(fs_ref[...] * LOG2E)

    def exponent(blk, part, points):
        span = pl.ds(part * LANES, LANES)
        shift = fs_col[pl.ds(blk * rows + part * LANES, LANES), :]
        shift = jnp.concatenate([shift] * (rows // LANES), axis=1)
        return raw_scores(src_ref[blk, span, :], points) * scale + shift

    def prepare(first, last):
        @pl.loop(first, last)
        def _(blk):
            for slot in range(SLOTS):
                points = tab_ref[position_of(blk, slot)]
                for part in range(rows // LANES):
                    span = pl.ds(part * LANES, LANES)
                    ready[blk * SLOTS + slot, span, :] = exponent(blk, part, points)

    for copy in needs:
        copy.wait()
    prepare(0, (PREPARED + 1) // 2)
    arrived()
    for q in range(blocks):
        terms = [part_ref[q]] + [
            jnp.where(pick == q, inbox[e], NEG_FILL) for e, pick in enumerate(picks)
        ]
        high = functools.reduce(jnp.maximum, terms)
        total = sum(jnp.exp(term - high) for term in terms)
        dual_ref[q] = tgt_logw_ref[q] - (high + jnp.log(total))
    duals = [dual_ref[q] for q in range(blocks)]
    for e, pick in enumerate(picks):
        chosen = duals[0]
        for q in range(1, blocks):
            chosen = jnp.where(pick == q, duals[q], chosen)
        outbox[e] = chosen
    arrived = exchange(outbox, 0, dual_ref, blocks, send_b, recv_b, *place)
    prepare((PREPARED + 1) // 2, PREPARED)
    arrived()
    ones = jnp.ones((rows, LANES), jnp.bfloat16)

    def plans(blk, exponent_of):
        count = count_of(blk)
        for slot in range(SLOTS):
            position = position_of(blk, slot)
            dual = jnp.where(slot < count, dual_ref[position] * LOG2E, NEG_FILL)
            points = tab_ref[position]
            beside = jnp.concatenate([points, ones], axis=1)
            for part in range(rows // LANES):
                span = pl.ds(part * LANES, LANES)
                here = pl.ds(blk * rows + part * LANES, LANES)
                plan = jnp.exp2(exponent_of(slot, part, points) + dual).astype(jnp.bfloat16)
                kept[blk * SLOTS + slot, span, :] = plan
                product = jnp.dot(plan, beside, preferred_element_type=jnp.float32)
                acc[here, :] = product if slot == 0 else acc[here, :] + product

    @pl.loop(0, PREPARED)
    def _(blk):
        plans(
            blk,
            lambda slot, part, points: ready[
                blk * SLOTS + slot, pl.ds(part * LANES, LANES), :
            ],
        )

    for blk in range(PREPARED, blocks):
        plans(blk, lambda slot, part, points: exponent(blk, part, points))

    row_sum = lane_sums(acc[:, LANES:]) * (1.0 / LANES)
    logw = src_logw_ref[...]
    weights = weight_rows(jnp.exp(logw) / row_sum)
    for blk in range(blocks):
        wts[blk] = weights[:, blk * rows : (blk + 1) * rows]

    @pl.loop(0, blocks)
    def _(blk):
        for slot in range(SLOTS):
            col_sum[pl.ds(blk * SLOTS + slot, 1), :] = column_sums(
                wts[blk], kept[blk * SLOTS + slot]
            )

    table, pairs = part_ref.shape[0], blocks * SLOTS
    row_at = lax.broadcasted_iota(jnp.int32, (table, pairs), 0)
    col_at = lax.broadcasted_iota(jnp.int32, (table, pairs), 1)
    into = jnp.full((table, pairs), -1, jnp.int32)
    for blk in range(blocks):
        count = count_of(blk)
        for slot in range(SLOTS):
            position = jnp.where(slot < count, position_of(blk, slot), -1)
            into = jnp.where(col_at == blk * SLOTS + slot, position, into)
    gathered = lax.dot_general(
        jnp.where(into == row_at, 1.0, 0.0),
        col_sum[...],
        (((1,), (0,)), ((), ())),
        precision=lax.Precision.HIGHEST,
        preferred_element_type=jnp.float32,
    )
    for e in range(table):
        outbox2[e] = gathered[e : e + 1]
    arrived = exchange(outbox2, blocks, inbox2, 0, send_c, recv_c, *place)
    pot_ref[...] = logw + fs_ref[...] - jnp.log(row_sum)
    for blk in range(blocks):
        span = pl.ds(blk * rows, rows)
        map_ref[blk] = acc[span, :LANES] / acc[span, LANES:]
    arrived()
    for q in range(blocks):
        total = outbox2[q]
        for e, pick in enumerate(picks):
            total = total + jnp.where(pick == q, inbox2[e], 0.0)
        tgt_pot_ref[q] = tgt_logw_ref[q] - jnp.log(total) + dual_ref[q]


def shards(source_points, target_points, source_logw, target_logw, pair_targets, pair_count):
    group_count = lax.axis_size("group")
    dev_count = lax.axis_size("dev")
    blocks, rows, slots = BLK_DEV, BLOCK, SLOTS
    table = blocks + dev_count + group_count
    peers = dev_count + group_count
    sources = source_points.reshape(blocks, rows, EMB)
    targets = target_points.reshape(blocks, rows, EMB)
    log_src = source_logw.reshape(1, blocks * rows)
    log_tgt = target_logw.reshape(blocks, 1, rows)

    named = jnp.concatenate([pair_targets.T, pair_count[None, :]], axis=0)

    smem = pl.BlockSpec(memory_space=pltpu.SMEM)
    vmem = pl.BlockSpec(memory_space=pltpu.VMEM)
    anywhere = pl.BlockSpec(memory_space=pl.ANY)
    f32 = jnp.float32
    kept = pltpu.VMEM((blocks * slots, rows, rows), jnp.bfloat16)
    pairs = blocks * slots
    dma = pltpu.SemaphoreType.DMA
    block = (rows, EMB)
    lots = RING * (len(BRANCH) + 1) + group_count - 1 + RING - 1
    picks = (peers, dev_count * blocks)
    hbm = pl.BlockSpec(memory_space=pltpu.HBM)
    delivered, pick, places, near_src, near_log_src = pl.pallas_call(
        functools.partial(deliver_kernel, dev_count, group_count),
        out_shape=(
            jax.ShapeDtypeStruct((table, *block), jnp.bfloat16),
            jax.ShapeDtypeStruct(picks, jnp.int32),
            jax.ShapeDtypeStruct((2 * slots, dev_count * blocks), jnp.int32),
            jax.ShapeDtypeStruct((blocks, *block), jnp.bfloat16),
            jax.ShapeDtypeStruct((1, blocks * rows), f32),
        ),
        in_specs=[vmem, hbm, hbm],
        out_specs=(anywhere, vmem, vmem, anywhere, anywhere),
        scratch_shapes=[
            pltpu.SMEM(picks, jnp.int32),
        ]
        + [pltpu.VMEM((blocks, *block), jnp.bfloat16)] * 4
        + [pltpu.VMEM((RING, *block), jnp.bfloat16)] * 2
        + [
            pltpu.VMEM((lots, *block), jnp.bfloat16),
            dma((6,)),
            dma((6,)),
            dma((lots,)),
            dma((dev_count,)),
            dma((2 * RING,)),
            dma((2 * RING,)),
            dma((group_count,)),
            dma((5,)),
        ],
        compiler_params=pltpu.CompilerParams(
            collective_id=2, has_side_effects=True, vmem_limit_bytes=VMEM_LIMIT
        ),
        name="deliver_blocks",
    )(named, jnp.stack([targets, sources]), log_src)

    first_source, part = pl.pallas_call(
        first_kernel,
        out_shape=(
            jax.ShapeDtypeStruct((1, blocks * rows), f32),
            jax.ShapeDtypeStruct((table, 1, rows), f32),
        ),
        in_specs=[smem, vmem, vmem, vmem],
        out_specs=(vmem, vmem),
        scratch_shapes=[
            kept,
            pltpu.VMEM((blocks * rows, LANES), f32),
            pltpu.VMEM((blocks, 16, rows), jnp.bfloat16),
            pltpu.VMEM((1, rows), f32),
            pltpu.VMEM((rows, LANES), f32),
            pltpu.VMEM((rows, LANES), f32),
        ],
        compiler_params=pltpu.CompilerParams(vmem_limit_bytes=PAIR_LIMIT),
        cost_estimate=pl.CostEstimate(
            flops=4 * pairs * rows * rows * EMB, bytes_accessed=6 * 2**20, transcendentals=pairs * rows * rows
        ),
        name="first_pass",
    )(places, near_src, near_log_src, delivered)

    row = pltpu.VMEM((peers, 1, rows), f32)
    full = pltpu.VMEM((table, 1, rows), f32)
    potential, mapped, target_potential = pl.pallas_call(
        functools.partial(finish_kernel, dev_count, group_count),
        out_shape=(
            jax.ShapeDtypeStruct((1, blocks * rows), f32),
            jax.ShapeDtypeStruct((blocks, rows, EMB), f32),
            jax.ShapeDtypeStruct((blocks, 1, rows), f32),
        ),
        in_specs=[smem, smem, vmem, vmem, hbm, vmem, vmem, hbm],
        out_specs=(vmem, vmem, vmem),
        scratch_shapes=[
            pltpu.VMEM((blocks, *block), jnp.bfloat16),
            pltpu.VMEM((table, *block), jnp.bfloat16),
            dma((2,)),
            row,
            row,
            full,
            row,
            full,
            kept,
            pltpu.VMEM((PREPARED * slots, rows, rows), f32),
            pltpu.VMEM((blocks * rows, LANES), f32),
            pltpu.VMEM((blocks * rows, 2 * LANES), f32),
            pltpu.VMEM((blocks, 16, rows), jnp.bfloat16),
            pltpu.VMEM((pairs, rows), f32),
        ]
        + [dma((peers,))] * 6,
        compiler_params=pltpu.CompilerParams(
            collective_id=0, has_side_effects=True, vmem_limit_bytes=FINISH_LIMIT
        ),
        cost_estimate=pl.CostEstimate(
            flops=8 * pairs * rows * rows * EMB, bytes_accessed=7 * 2**20, transcendentals=pairs * rows * rows
        ),
        name="finish",
    )(
        pick, places, part, log_tgt, sources, near_log_src, first_source, delivered
    )
    return (
        potential.reshape(blocks * rows),
        target_potential.reshape(blocks * rows),
        mapped.reshape(blocks * rows, EMB),
    )


def solution(mesh):
    return jax.shard_map(
        shards,
        mesh=mesh,
        in_specs=(
            P(("group", "dev"), None),
            P(("group", "dev"), None),
            P(("group", "dev")),
            P(("group", "dev")),
            P(),
            P(),
        ),
        out_specs=(P(("group", "dev")), P(("group", "dev")), P(("group", "dev"), None)),
        check_vma=False,
    )
```
